32 devices in a mesh: pipe: 2 (over x), expert: 16 (over z, y, core).
Axes of the slice: x: 2, y: 2, z: 4, core: 2. Of those that a mesh axis runs over, the one named last changes fastest.
Arguments:
- acts: bfloat16 [2, 2048, 3584], P('pipe', 'expert'), may hold values from -6 to 6
- grad_out: bfloat16 [2, 2048, 3584], P('pipe', 'expert'), may hold values from -6 to 6
- expert_ids: int32 [2, 2048, 2], P('pipe', 'expert'), may hold values from 0 to 7, all different within a row; in each aligned block of 64 rows (0 to 63, 64 to 127, ..., all dimensions but the last counted through in order) at most 24 rows name the same one
- route_weights: float32 [2, 2048, 2], P('pipe', 'expert'), may hold values from 0.1 to 1
- w_gate: bfloat16 [2, 3584, 8192], P('pipe', None, 'expert'), may hold values from -0.09375 to 0.09375
- w_up: bfloat16 [2, 3584, 8192], P('pipe', None, 'expert'), may hold values from -0.09375 to 0.09375
- w_down: bfloat16 [2, 8192, 3584], P('pipe', 'expert'), may hold values from -0.1875 to 0.1875
Outputs:
- out_acts: bfloat16 [2, 2048, 3584], P('pipe', 'expert')
- grad_acts: bfloat16 [2, 2048, 3584], P('pipe', 'expert')
- grad_gate: bfloat16 [2, 3584, 4096], P('pipe', None, 'expert')
- grad_up: bfloat16 [2, 3584, 4096], P('pipe', None, 'expert')
- grad_down: bfloat16 [2, 4096, 3584], P('pipe', 'expert')
The draws below stay inside these ranges and needn't reach their ends.
Inputs may be any that keep to these rules, and one draw needn't show every extreme that they name: `expert_ids`: in each aligned block of 64 rows of one rank (one micro-batch of one device), no expert is named by more than 24 rows; the 2 experts of a row differ.
All inputs are finite; a program needn't handle non-finite values.
Results may differ from the reference program's by a relative error of at most 0.0072.
Values may be sent and summed in bfloat16 or wider, within the bound.
No kernel may reach another device: no remote copies, remote signals or barrier semaphores. Data moves between devices by JAX's collectives and lax.ppermute only.
A program may use at most 192 MiB of HBM per device.

```python
import math
import jax
import jax.numpy as jnp
import numpy as np
from jax import lax

D = 3584
FF = 1024
TOPK = 2
MB = 2
TOK_MB = 64
NEXP = 8
FF_DEV = 512
CAP = 24
TOKENS = 2048
N_PIPE = 2
N_EXPERT = 16


def shard_levels(stream_key, dims, cuts, least, largest):
    factor_of, own = 1.0, jax.random.fold_in(stream_key, 6)
    for axis_at, blocks in cuts:
        draws = jnp.exp(jax.random.uniform(jax.random.fold_in(own, axis_at), (blocks,), jnp.float32, least / len(cuts), largest / len(cuts)))
        factor_of = factor_of * jnp.repeat(draws, dims[axis_at] // blocks).reshape([-1 if axis == axis_at else 1 for axis in range(len(dims))])
    return factor_of


def shared_out(stream_key, own, number, rows, count, top, limit, lean):
    ranking = jax.random.permutation(stream_key, count)
    packed, ordinary = portions_of(count, rows * top, limit, lean, True), portions_of(count, rows * top, limit, lean, False)
    places = jnp.arange(count)

    def named(sizes, turn):
        used = int((sizes > 0).sum())
        fixed = max(1, used // 4)
        moved = fixed + (places - fixed + turn * (used - fixed)) % max(1, count - fixed)
        return jnp.zeros((count,), jnp.int32).at[ranking[jnp.where(places < fixed, places, moved)]].set(jnp.asarray(sizes, jnp.int32))

    sizes = jnp.where(number % 4 == 0, named(packed, number // 4), named(ordinary, number - number // 4 - 1))
    mixed = jax.random.permutation(jax.random.fold_in(own, 3), count)
    donor, sink = mixed[0:count // 2 * 2:2], mixed[1:count // 2 * 2:2]
    slack = jnp.minimum(sizes[donor] - 1, limit - sizes[sink]) // 2
    slack = jnp.where((donor == ranking[0]) | (sink == ranking[0]) | (sizes[sink] == 0), 0, jnp.maximum(slack, 0))
    moved = jax.random.randint(jax.random.fold_in(own, 4), (count // 2,), 0, 1 << 20) % (slack + 1)
    sizes = sizes.at[donor].add(-moved).at[sink].add(moved)
    items = jnp.searchsorted(jnp.cumsum(sizes), jnp.arange(rows * top), side="right").astype(jnp.int32)
    listing = items.reshape(top, rows).T
    listing = listing[jax.random.permutation(jax.random.fold_in(own, 1), rows)]
    turn = jax.random.randint(jax.random.fold_in(own, 2), (rows, 1), 0, top)
    return jnp.take_along_axis(listing, (jnp.arange(top)[None, :] + turn) % top, axis=1)


def portions_of(number_of, total, limit, lean, full):
    portions = [(1 << 20) // math.isqrt(standing ** lean) + 1 for standing in range(1, number_of + 1)]
    largest = limit if full else min(limit, max(-(-total // number_of), total * portions[0] // sum(portions)))
    least = 1 if total - largest >= number_of - 1 else 0
    counts, surplus = [largest] + [least] * (number_of - 1), total - largest - least * (number_of - 1)
    while surplus > 0:
        movable = [i for i in range(1, number_of) if counts[i] < largest] or [i for i in range(1, number_of) if counts[i] < limit]
        mass, remaining = sum([portions[i] for i in movable]), surplus
        for i in movable:
            more = min(limit - counts[i], max(1, remaining * portions[i] // mass), surplus)
            counts[i] = counts[i] + more
            surplus = surplus - more
    return np.array(counts)


def gaussian(key, extent, scale, bound, shards=(), kind=jnp.bfloat16):
    gain = shard_levels(key, extent, shards, -0.22, 0.18) if shards else 1.0
    array = jax.random.normal(key, extent, jnp.float32) * scale * gain
    return jnp.minimum(jnp.maximum(array, -bound), bound).astype(kind)


def setup_inputs(seed: int = 0) -> dict:
    keys = jax.random.split(jax.random.key(seed), 8)
    acts = gaussian(keys[0], (N_PIPE, TOKENS, D), 1.0, 6.0, ((0, 2), (1, 16)))
    grad_out = gaussian(keys[1], (N_PIPE, TOKENS, D), 1.0, 6.0, ((0, 2), (1, 16)))
    expert_ids_keys = jax.random.split(jax.random.fold_in(keys[2], 1), N_PIPE * TOKENS // TOK_MB)
    expert_ids_turns = jax.random.permutation(jax.random.fold_in(keys[2], 3), N_PIPE * TOKENS // TOK_MB)
    expert_ids = jax.vmap(lambda own, number: shared_out(jax.random.fold_in(keys[2], 2), own, number, TOK_MB, NEXP, TOPK, CAP, 2))(expert_ids_keys, expert_ids_turns).reshape((N_PIPE, TOKENS, TOPK))
    route_weights = jnp.clip(0.1 + 0.9 * jax.random.uniform(keys[3], (N_PIPE, TOKENS, TOPK), jnp.float32) ** shard_levels(keys[3], (N_PIPE, TOKENS, TOPK), ((0, 2), (1, 16)), -0.2, 0.2), 0.1, 1.0)
    w_gate = gaussian(keys[4], (N_PIPE, D, N_EXPERT * FF_DEV), D ** -0.5, 0.09375, ((0, 2), (2, 16)))
    w_up = gaussian(keys[5], (N_PIPE, D, N_EXPERT * FF_DEV), D ** -0.5, 0.09375, ((0, 2), (2, 16)))
    w_down = gaussian(keys[6], (N_PIPE, N_EXPERT * FF_DEV, D), FF ** -0.5, 0.1875, ((0, 2), (1, 16)))
    return {"acts": acts, "grad_out": grad_out, "expert_ids": expert_ids, "route_weights": route_weights, "w_gate": w_gate, "w_up": w_up, "w_down": w_down}


def expert_half(rows_in, rows_grad, gate_weight, up_weight, down_weight):
    pre_gate = jnp.dot(rows_in, gate_weight, preferred_element_type=jnp.float32)
    pre_up = jnp.dot(rows_in, up_weight, preferred_element_type=jnp.float32)
    sigma = jax.nn.sigmoid(pre_gate)
    active = pre_gate * sigma
    hidden = (active * pre_up).astype(jnp.bfloat16)
    part_out = jnp.dot(hidden, down_weight, preferred_element_type=jnp.float32).astype(jnp.bfloat16)
    hidden_grad = lax.dot_general(rows_grad, down_weight, (((1,), (1,)), ((), ())), preferred_element_type=jnp.float32)
    gate_grad = (hidden_grad * pre_up * sigma * (1.0 + pre_gate * (1.0 - sigma))).astype(jnp.bfloat16)
    up_grad = (hidden_grad * active).astype(jnp.bfloat16)
    part_input = lax.dot_general(gate_grad, gate_weight, (((1,), (1,)), ((), ())), preferred_element_type=jnp.float32)
    part_input = part_input + lax.dot_general(up_grad, up_weight, (((1,), (1,)), ((), ())), preferred_element_type=jnp.float32)
    grad_gate = lax.dot_general(rows_in, gate_grad, (((0,), (0,)), ((), ())), preferred_element_type=jnp.float32)
    grad_up = lax.dot_general(rows_in, up_grad, (((0,), (0,)), ((), ())), preferred_element_type=jnp.float32)
    grad_down = lax.dot_general(hidden, rows_grad, (((0,), (0,)), ((), ())), preferred_element_type=jnp.float32)
    return part_out, part_input.astype(jnp.bfloat16), grad_gate, grad_up, grad_down


def keep_halves(summed, axis_pos):
    if axis_pos == 2:
        shaped = summed.reshape(N_PIPE, D, N_EXPERT, 2, FF_DEV // 2)
        lower = shaped[: N_PIPE // 2, :, :, 0]
        upper = shaped[N_PIPE // 2:, :, :, 1]
        return jnp.concatenate([lower, upper], axis=0).reshape(N_PIPE, D, N_EXPERT * FF_DEV // 2)
    shaped = summed.reshape(N_PIPE, N_EXPERT, 2, FF_DEV // 2, D)
    lower = shaped[: N_PIPE // 2, :, 0]
    upper = shaped[N_PIPE // 2:, :, 1]
    return jnp.concatenate([lower, upper], axis=0).reshape(N_PIPE, N_EXPERT * FF_DEV // 2, D)


def mirror_sum(local):
    return (local.astype(jnp.float32) + local[::-1].astype(jnp.float32)).astype(jnp.bfloat16)


def reference(acts, grad_out, expert_ids, route_weights, w_gate, w_up, w_down):
    total_slots = N_EXPERT * MB * CAP
    positions = jnp.arange(total_slots, dtype=jnp.int32)
    zero_value = jnp.zeros((), jnp.bfloat16)
    out_list = []
    input_list = []
    gate_list = []
    up_list = []
    down_list = []
    for rank in range(N_PIPE):
        token_rows = acts[rank]
        choice_ids = expert_ids[rank].reshape(-1)
        choice_gain = route_weights[rank].reshape(-1)
        scaled_grad = (route_weights[rank][:, :, None] * grad_out[rank][:, None, :].astype(jnp.float32)).astype(jnp.bfloat16).reshape(-1, D)
        out_acc = jnp.zeros((TOKENS, D), jnp.float32)
        input_acc = jnp.zeros((TOKENS, D), jnp.float32)
        gate_cols = []
        up_cols = []
        down_rows = []
        for expert in range(NEXP):
            chosen = choice_ids == expert
            found = jnp.nonzero(chosen, size=total_slots, fill_value=0)[0].astype(jnp.int32)
            number = jnp.sum(chosen.astype(jnp.int32))
            live = positions < number
            row_index = (found // TOPK).astype(jnp.int32)
            rows_in = jnp.where(live[:, None], token_rows[row_index], zero_value)
            rows_grad = jnp.where(live[:, None], scaled_grad[found], zero_value)
            out_sum = jnp.zeros((total_slots, D), jnp.float32)
            input_sum = jnp.zeros((total_slots, D), jnp.float32)
            for half_index in range(2):
                start = (2 * expert + half_index) * FF_DEV
                part_out, part_input, grad_g, grad_u, grad_d = expert_half(
                    rows_in, rows_grad, w_gate[rank][:, start:start + FF_DEV],
                    w_up[rank][:, start:start + FF_DEV], w_down[rank][start:start + FF_DEV, :])
                out_sum = out_sum + part_out.astype(jnp.float32)
                input_sum = input_sum + part_input.astype(jnp.float32)
                gate_cols.append(grad_g)
                up_cols.append(grad_u)
                down_rows.append(grad_d)
            expert_out = out_sum.astype(jnp.bfloat16).astype(jnp.float32)
            expert_input = input_sum.astype(jnp.bfloat16).astype(jnp.float32)
            gains = jnp.where(live, choice_gain[found], jnp.zeros((), jnp.float32))
            out_acc = out_acc.at[row_index].add(gains[:, None] * expert_out)
            input_acc = input_acc.at[row_index].add(jnp.where(live[:, None], expert_input, jnp.zeros((), jnp.float32)))
        out_list.append(out_acc.astype(jnp.bfloat16))
        input_list.append(input_acc.astype(jnp.bfloat16))
        gate_list.append(jnp.concatenate(gate_cols, axis=1).astype(jnp.bfloat16))
        up_list.append(jnp.concatenate(up_cols, axis=1).astype(jnp.bfloat16))
        down_list.append(jnp.concatenate(down_rows, axis=0).astype(jnp.bfloat16))
    grad_gate = keep_halves(mirror_sum(jnp.stack(gate_list)), 2)
    grad_up = keep_halves(mirror_sum(jnp.stack(up_list)), 2)
    grad_down = keep_halves(mirror_sum(jnp.stack(down_list)), 1)
    return jnp.stack(out_list), jnp.stack(input_list), grad_gate, grad_up, grad_down
```

```python
import jax
import jax.numpy as jnp
from jax import lax
from jax.sharding import PartitionSpec as P

TOPK = 2
MB = 2
TOK_MB = 64
F32 = jnp.float32
BF16 = jnp.bfloat16


def dot(a, b, dims):
    return lax.dot_general(a, b, (dims, ((), ())), preferred_element_type=F32)


def route(ids, gain, expert_count, capacity):
    flat_ids = ids.reshape(-1)
    member = (flat_ids[:, None] == jnp.arange(expert_count, dtype=jnp.int32)[None, :]).astype(jnp.int32)
    running = jnp.cumsum(member, axis=0) - 1
    slot_rank = jnp.sum(member * running, axis=1)
    target = (flat_ids * capacity + slot_rank).reshape(ids.shape)
    slots = jnp.arange(expert_count * capacity, dtype=jnp.int32)
    matches = (target[:, :, None] == slots[None, None, :]).astype(F32)
    placing = jnp.sum(matches, axis=1).astype(BF16)
    weighting = jnp.sum(matches * gain[:, :, None], axis=1)
    return placing, weighting, jnp.sum(weighting, axis=0)


def on_device(acts, grad_out, expert_ids, route_weights, w_gate, w_up, w_down):
    gate_weight, up_weight, down_weight = w_gate[0], w_up[0], w_down[0]
    devices = lax.axis_size("expert")
    chips = devices // 2
    capacity = 3 * TOPK * TOK_MB // (2 * chips)
    slot_count = chips * capacity
    width = gate_weight.shape[0]
    half_units = gate_weight.shape[1] // 2
    same_core = [[2 * chip + core for chip in range(chips)] for core in range(2)]
    other_core = [(i, i ^ 1) for i in range(devices)]

    def across(blocks):
        moved = lax.all_to_all(
            blocks.reshape(chips, capacity, width),
            "expert",
            split_axis=0,
            concat_axis=0,
            axis_index_groups=same_core,
            tiled=True,
        )
        return moved.reshape(slot_count, width)

    def swap(rows):
        return lax.ppermute(rows, "expert", other_core)

    rows_in, rows_grad, hiddens, gate_grads, up_grads = [], [], [], [], []
    routes, outs, inputs = [], [], []
    for b in range(MB):
        rows = slice(b * TOK_MB, (b + 1) * TOK_MB)
        placing, weighting, slot_gain = route(
            expert_ids[0, rows], route_weights[0, rows], chips, capacity
        )
        routes.append((placing, weighting))
        tokens = dot(placing, acts[0, rows], ((0,), (0,))).astype(BF16)
        grads = dot(placing, grad_out[0, rows], ((0,), (0,)))
        grads = (grads * slot_gain[:, None]).astype(BF16)
        tokens = across(tokens)
        rows_in.append([tokens, swap(tokens)])
        grads = across(grads)
        rows_grad.append([grads, swap(grads)])

    for b in range(MB):
        part_out, part_input = [], []
        hiddens.append([])
        gate_grads.append([])
        up_grads.append([])
        for tokens, grads in zip(rows_in[b], rows_grad[b]):
            pre_gate = dot(tokens, gate_weight, ((1,), (0,)))
            pre_up = dot(tokens, up_weight, ((1,), (0,)))
            sigma = jax.nn.sigmoid(pre_gate)
            active = pre_gate * sigma
            hidden = (active * pre_up).astype(BF16)
            part_out.append(dot(hidden, down_weight, ((1,), (0,))).astype(BF16))
            hidden_grad = dot(grads, down_weight, ((1,), (1,)))
            gate_grad = (
                hidden_grad * pre_up * sigma * (1.0 + pre_gate * (1.0 - sigma))
            ).astype(BF16)
            up_grad = (hidden_grad * active).astype(BF16)
            part_input.append(
                (
                    dot(gate_grad, gate_weight, ((1,), (1,)))
                    + dot(up_grad, up_weight, ((1,), (1,)))
                ).astype(BF16)
            )
            hiddens[b].append(hidden)
            gate_grads[b].append(gate_grad)
            up_grads[b].append(up_grad)
        back = []
        for own, other in (part_out, part_input):
            both = (own.astype(F32) + swap(other).astype(F32)).astype(BF16)
            back.append(across(both))
        placing, weighting = routes[b]
        outs.append(
            lax.dot_general(
                weighting,
                back[0].astype(F32),
                (((1,), (0,)), ((), ())),
                precision=lax.Precision.HIGHEST,
                preferred_element_type=F32,
            ).astype(BF16)
        )
        inputs.append(dot(placing, back[1], ((1,), (0,))).astype(BF16))

    rank_index = lax.axis_index("pipe")
    rank_count = lax.axis_size("pipe")
    mirror = [(p, rank_count - 1 - p) for p in range(rank_count)]
    kept_half = (rank_index >= rank_count // 2).astype(jnp.int32)

    def joined(parts):
        return jnp.concatenate([part for batch in parts for part in batch], axis=0)

    def halves(units):
        return (
            lax.dynamic_slice_in_dim(units, kept_half * half_units, half_units, 1),
            lax.dynamic_slice_in_dim(units, (1 - kept_half) * half_units, half_units, 1),
        )

    all_in = joined(rows_in)
    all_grad = joined(rows_grad)
    keep_hidden, send_hidden = halves(joined(hiddens))
    keep_gate, send_gate = halves(joined(gate_grads))
    keep_up, send_up = halves(joined(up_grads))
    rows_dims = ((0,), (0,))
    sent = [
        lax.ppermute(dot(a, b, rows_dims).astype(BF16), "pipe", mirror)
        for a, b in ((send_hidden, all_grad), (all_in, send_gate), (all_in, send_up))
    ]
    kept = [
        dot(a, b, rows_dims).astype(BF16)
        for a, b in ((keep_hidden, all_grad), (all_in, keep_gate), (all_in, keep_up))
    ]
    grad_down, grad_gate, grad_up = [
        (own.astype(F32) + other.astype(F32)).astype(BF16)[None] for own, other in zip(kept, sent)
    ]
    out_acts = jnp.concatenate(outs, axis=0)[None]
    grad_acts = jnp.concatenate(inputs, axis=0)[None]
    return out_acts, grad_acts, grad_gate, grad_up, grad_down


def solution(mesh):
    tokens = P("pipe", "expert", None)
    columns = P("pipe", None, "expert")
    return jax.shard_map(
        on_device,
        mesh=mesh,
        in_specs=(tokens, tokens, tokens, tokens, columns, columns, tokens),
        out_specs=(tokens, tokens, columns, columns, tokens),
        check_vma=False,
    )
```

```python
import jax
import jax.numpy as jnp
from jax import lax
from jax.sharding import PartitionSpec as P

TOPK = 2
MB = 2
TOK_MB = 64
F32 = jnp.float32
BF16 = jnp.bfloat16


def dot(a, b, dims):
    return lax.dot_general(a, b, (dims, ((), ())), preferred_element_type=F32)


def route(ids, gain, expert_count, capacity, chip):
    flat_ids = ids.reshape(-1)
    member = (flat_ids[:, None] == jnp.arange(expert_count, dtype=jnp.int32)[None, :]).astype(jnp.int32)
    running = jnp.cumsum(member, axis=0) - 1
    slot_rank = jnp.sum(member * running, axis=1)
    target = ((flat_ids ^ chip) * capacity + slot_rank).reshape(ids.shape)
    slots = jnp.arange(expert_count * capacity, dtype=jnp.int32)
    matches = (target[:, :, None] == slots[None, None, :]).astype(F32)
    placing = jnp.sum(matches, axis=1).astype(BF16)
    weighting = jnp.sum(matches * gain[:, :, None], axis=1)
    return placing, weighting, jnp.sum(weighting, axis=0)


def on_device(acts, grad_out, expert_ids, route_weights, w_gate, w_up, w_down):
    gate_weight, up_weight, down_weight = w_gate[0], w_up[0], w_down[0]
    devices = lax.axis_size("expert")
    chips = devices // 2
    capacity = 3 * TOPK * TOK_MB // (2 * chips)
    slot_count = chips * capacity
    width = gate_weight.shape[0]
    half_units = gate_weight.shape[1] // 2
    chip = lax.axis_index("expert") // 2
    other_core = [(i, i ^ 1) for i in range(devices)]

    def across(blocks):
        pieces = [blocks[d * capacity : (d + 1) * capacity] for d in range(chips)]
        moved = [
            piece if d == 0 else lax.ppermute(piece, "expert", [(i, i ^ (2 * d)) for i in range(devices)])
            for d, piece in enumerate(pieces)
        ]
        return jnp.concatenate(moved, axis=0)

    def swap(rows):
        return lax.ppermute(rows, "expert", other_core)

    rows_in, rows_grad, hiddens, gate_grads, up_grads = [], [], [], [], []
    routes, outs, inputs = [], [], []
    for b in range(MB):
        rows = slice(b * TOK_MB, (b + 1) * TOK_MB)
        placing, weighting, slot_gain = route(
            expert_ids[0, rows], route_weights[0, rows], chips, capacity, chip
        )
        routes.append((placing, weighting))
        tokens = dot(placing, acts[0, rows], ((0,), (0,))).astype(BF16)
        grads = dot(placing, grad_out[0, rows], ((0,), (0,)))
        grads = (grads * slot_gain[:, None]).astype(BF16)
        tokens = across(tokens)
        rows_in.append([tokens, swap(tokens)])
        grads = across(grads)
        rows_grad.append([grads, swap(grads)])

    for b in range(MB):
        part_out, part_input = [], []
        hiddens.append([])
        gate_grads.append([])
        up_grads.append([])
        for tokens, grads in zip(rows_in[b], rows_grad[b]):
            pre_gate = dot(tokens, gate_weight, ((1,), (0,)))
            pre_up = dot(tokens, up_weight, ((1,), (0,)))
            sigma = jax.nn.sigmoid(pre_gate)
            active = pre_gate * sigma
            hidden = (active * pre_up).astype(BF16)
            part_out.append(dot(hidden, down_weight, ((1,), (0,))).astype(BF16))
            hidden_grad = dot(grads, down_weight, ((1,), (1,)))
            gate_grad = (
                hidden_grad * pre_up * sigma * (1.0 + pre_gate * (1.0 - sigma))
            ).astype(BF16)
            up_grad = (hidden_grad * active).astype(BF16)
            part_input.append(
                (
                    dot(gate_grad, gate_weight, ((1,), (1,)))
                    + dot(up_grad, up_weight, ((1,), (1,)))
                ).astype(BF16)
            )
            hiddens[b].append(hidden)
            gate_grads[b].append(gate_grad)
            up_grads[b].append(up_grad)
        back = []
        for own, other in (part_out, part_input):
            both = (own.astype(F32) + swap(other).astype(F32)).astype(BF16)
            back.append(across(both))
        placing, weighting = routes[b]
        outs.append(
            lax.dot_general(
                weighting,
                back[0].astype(F32),
                (((1,), (0,)), ((), ())),
                precision=lax.Precision.HIGHEST,
                preferred_element_type=F32,
            ).astype(BF16)
        )
        inputs.append(dot(placing, back[1], ((1,), (0,))).astype(BF16))

    rank_index = lax.axis_index("pipe")
    rank_count = lax.axis_size("pipe")
    mirror = [(p, rank_count - 1 - p) for p in range(rank_count)]
    kept_half = (rank_index >= rank_count // 2).astype(jnp.int32)

    def joined(parts):
        return jnp.concatenate([part for batch in parts for part in batch], axis=0)

    def halves(units):
        return (
            lax.dynamic_slice_in_dim(units, kept_half * half_units, half_units, 1),
            lax.dynamic_slice_in_dim(units, (1 - kept_half) * half_units, half_units, 1),
        )

    all_in = joined(rows_in)
    all_grad = joined(rows_grad)
    keep_hidden, send_hidden = halves(joined(hiddens))
    keep_gate, send_gate = halves(joined(gate_grads))
    keep_up, send_up = halves(joined(up_grads))
    rows_dims = ((0,), (0,))
    sent = [
        lax.ppermute(dot(a, b, rows_dims).astype(BF16), "pipe", mirror)
        for a, b in ((send_hidden, all_grad), (all_in, send_gate), (all_in, send_up))
    ]
    kept = [
        dot(a, b, rows_dims).astype(BF16)
        for a, b in ((keep_hidden, all_grad), (all_in, keep_gate), (all_in, keep_up))
    ]
    grad_down, grad_gate, grad_up = [
        (own.astype(F32) + other.astype(F32)).astype(BF16)[None] for own, other in zip(kept, sent)
    ]
    out_acts = jnp.concatenate(outs, axis=0)[None]
    grad_acts = jnp.concatenate(inputs, axis=0)[None]
    return out_acts, grad_acts, grad_gate, grad_up, grad_down


def solution(mesh):
    tokens = P("pipe", "expert", None)
    columns = P("pipe", None, "expert")
    return jax.shard_map(
        on_device,
        mesh=mesh,
        in_specs=(tokens, tokens, tokens, tokens, columns, columns, tokens),
        out_specs=(tokens, tokens, columns, columns, tokens),
        check_vma=False,
    )
```

```python
import jax
import jax.numpy as jnp
from jax import lax
from jax.sharding import PartitionSpec as P

TOPK = 2
MB = 2
TOK_MB = 64
F32 = jnp.float32
BF16 = jnp.bfloat16


def dot(a, b, dims):
    return lax.dot_general(a, b, (dims, ((), ())), preferred_element_type=F32)


def route(meta, chip, expert_count, capacity):
    ids, gain = meta[:, :TOPK].astype(jnp.int32), meta[:, TOPK:]
    flat_ids = ids.reshape(MB, TOK_MB * TOPK)
    member = (flat_ids[:, :, None] == jnp.arange(expert_count, dtype=jnp.int32)).astype(jnp.int32)
    running = jnp.cumsum(member, axis=1) - 1
    rank = jnp.sum(member * running, axis=2)
    batch = jnp.arange(MB, dtype=jnp.int32)[:, None]
    target = (((flat_ids ^ chip) * MB + batch) * capacity + rank).reshape(ids.shape)
    slots = jnp.arange(expert_count // 2 * MB * capacity, dtype=jnp.int32)
    matches = (target[:, :, None] == slots).astype(F32)
    placing = jnp.sum(matches, axis=1).astype(BF16)
    weighting = jnp.sum(matches * gain[:, :, None], axis=1)
    return placing, weighting, jnp.sum(weighting, axis=0)


def on_device(acts, grad_out, expert_ids, route_weights, w_gate, w_up, w_down):
    gate_weight, up_weight, down_weight = w_gate[0], w_up[0], w_down[0]
    devices = lax.axis_size("expert")
    chips = devices // 2
    near = chips // 2
    capacity = 3 * TOPK * TOK_MB // (2 * chips)
    piece = MB * capacity
    width = gate_weight.shape[0]
    half_units = gate_weight.shape[1] // 2
    chip = lax.axis_index("expert") // 2

    def hop(rows, distance):
        return lax.ppermute(rows, "expert", [(i, i ^ distance) for i in range(devices)])

    def far(rows):
        return hop(rows, devices // 2)

    def swap(rows):
        return hop(rows, 1)

    def near_exchange(arrays):
        moved = [[array[:piece] for array in arrays]]
        for d in range(1, near):
            sent = [array[d * piece : (d + 1) * piece] for array in arrays]
            got = hop(jnp.concatenate(sent, axis=0), 2 * d)
            moved.append([got[n * piece : (n + 1) * piece] for n in range(len(arrays))])
        return [jnp.concatenate(parts, axis=0) for parts in zip(*moved)]

    def place(placing, rows):
        return dot(placing, rows, ((0,), (0,)))

    meta = jnp.concatenate([expert_ids[0].astype(F32), route_weights[0]], axis=1)
    far_meta = far(meta)
    far_acts = far(acts[0])
    far_grads = far(grad_out[0])
    own_placing, own_weighting, own_gain = route(meta, chip, chips, capacity)
    far_placing, far_weighting, far_gain = route(far_meta, chip, chips, capacity)

    own_in = place(own_placing, acts[0]).astype(BF16)
    own_grad = (place(own_placing, grad_out[0]) * own_gain[:, None]).astype(BF16)
    own_in, own_grad = near_exchange([own_in, own_grad])
    far_in = near_exchange([place(far_placing, far_acts).astype(BF16)])[0]
    far_grad = near_exchange([(place(far_placing, far_grads) * far_gain[:, None]).astype(BF16)])[0]
    rows_in = [far_in, swap(far_in), own_in, swap(own_in)]
    rows_grad = [far_grad, swap(far_grad), own_grad, swap(own_grad)]

    hiddens, gate_grads, up_grads, part_out, part_input = [], [], [], [], []
    for tokens, grads in zip(rows_in, rows_grad):
        pre_gate = dot(tokens, gate_weight, ((1,), (0,)))
        pre_up = dot(tokens, up_weight, ((1,), (0,)))
        sigma = jax.nn.sigmoid(pre_gate)
        active = pre_gate * sigma
        hidden = (active * pre_up).astype(BF16)
        part_out.append(dot(hidden, down_weight, ((1,), (0,))).astype(BF16))
        hidden_grad = dot(grads, down_weight, ((1,), (1,)))
        gate_grad = (hidden_grad * pre_up * sigma * (1.0 + pre_gate * (1.0 - sigma))).astype(BF16)
        up_grad = (hidden_grad * active).astype(BF16)
        part_input.append(
            (
                dot(gate_grad, gate_weight, ((1,), (1,))) + dot(up_grad, up_weight, ((1,), (1,)))
            ).astype(BF16)
        )
        hiddens.append(hidden)
        gate_grads.append(gate_grad)
        up_grads.append(up_grad)

    def expert_sum(parts):
        return (parts[0].astype(F32) + swap(parts[1]).astype(F32)).astype(BF16)

    def weighted(matrix, rows):
        return lax.dot_general(
            matrix,
            rows.astype(F32),
            (((1,), (0,)), ((), ())),
            precision=lax.Precision.HIGHEST,
            preferred_element_type=F32,
        )

    far_out = near_exchange([expert_sum(part_out[:2])])[0]
    far_input = near_exchange([expert_sum(part_input[:2])])[0]
    got_out = far(weighted(far_weighting, far_out).astype(BF16))
    got_input = far(dot(far_placing, far_input, ((1,), (0,))).astype(BF16))
    own_out, own_input = near_exchange([expert_sum(part_out[2:]), expert_sum(part_input[2:])])
    out_acts = (weighted(own_weighting, own_out) + got_out.astype(F32)).astype(BF16)
    grad_acts = (dot(own_placing, own_input, ((1,), (0,))) + got_input.astype(F32)).astype(BF16)

    rank_index = lax.axis_index("pipe")
    rank_count = lax.axis_size("pipe")
    mirror = [(p, rank_count - 1 - p) for p in range(rank_count)]
    kept_half = (rank_index >= rank_count // 2).astype(jnp.int32)

    def halves(units):
        units = jnp.concatenate(units, axis=0)
        return (
            lax.dynamic_slice_in_dim(units, kept_half * half_units, half_units, 1),
            lax.dynamic_slice_in_dim(units, (1 - kept_half) * half_units, half_units, 1),
        )

    all_in = jnp.concatenate(rows_in, axis=0)
    all_grad = jnp.concatenate(rows_grad, axis=0)
    keep_hidden, send_hidden = halves(hiddens)
    keep_gate, send_gate = halves(gate_grads)
    keep_up, send_up = halves(up_grads)
    rows_dims = ((0,), (0,))
    sent = [
        lax.ppermute(dot(a, b, rows_dims).astype(BF16), "pipe", mirror)
        for a, b in ((send_hidden, all_grad), (all_in, send_gate), (all_in, send_up))
    ]
    kept = [
        dot(a, b, rows_dims).astype(BF16)
        for a, b in ((keep_hidden, all_grad), (all_in, keep_gate), (all_in, keep_up))
    ]
    grad_down, grad_gate, grad_up = [
        (own.astype(F32) + other.astype(F32)).astype(BF16)[None] for own, other in zip(kept, sent)
    ]
    return out_acts[None], grad_acts[None], grad_gate, grad_up, grad_down


def solution(mesh):
    tokens = P("pipe", "expert", None)
    columns = P("pipe", None, "expert")
    return jax.shard_map(
        on_device,
        mesh=mesh,
        in_specs=(tokens, tokens, tokens, tokens, columns, columns, tokens),
        out_specs=(tokens, tokens, columns, columns, tokens),
        check_vma=False,
    )
```

```python
import jax
import jax.numpy as jnp
from jax import lax
from jax.sharding import PartitionSpec as P

TOPK = 2
MB = 2
TOK_MB = 64
F32 = jnp.float32
BF16 = jnp.bfloat16


def dot(a, b, dims):
    return lax.dot_general(a, b, (dims, ((), ())), preferred_element_type=F32)


def route(meta, half, expert_count, capacity):
    ids, gain = meta[:, :TOPK].astype(jnp.int32), meta[:, TOPK:]
    flat_ids = ids.reshape(MB, TOK_MB * TOPK)
    member = (flat_ids[:, :, None] == jnp.arange(expert_count, dtype=jnp.int32)).astype(jnp.int32)
    running = jnp.cumsum(member, axis=1) - 1
    rank = jnp.sum(member * running, axis=2)
    batch = jnp.arange(MB, dtype=jnp.int32)[:, None]
    target = (((flat_ids - half * (expert_count // 2)) * MB + batch) * capacity + rank).reshape(ids.shape)
    slots = jnp.arange(expert_count // 2 * MB * capacity, dtype=jnp.int32)
    matches = (target[:, :, None] == slots).astype(F32)
    placing = jnp.sum(matches, axis=1).astype(BF16)
    weighting = jnp.sum(matches * gain[:, :, None], axis=1)
    return placing, weighting, jnp.sum(weighting, axis=0)


def on_device(acts, grad_out, expert_ids, route_weights, w_gate, w_up, w_down):
    gate_weight, up_weight, down_weight = w_gate[0], w_up[0], w_down[0]
    devices = lax.axis_size("expert")
    chips = devices // 2
    near = chips // 2
    capacity = 3 * TOPK * TOK_MB // (2 * chips)
    piece = MB * capacity
    width = gate_weight.shape[0]
    half_units = gate_weight.shape[1] // 2
    half = (lax.axis_index("expert") >= devices // 2).astype(jnp.int32)

    def hop(rows, distance):
        return lax.ppermute(rows, "expert", [(i, i ^ distance) for i in range(devices)])

    def far(rows):
        return hop(rows, devices // 2)

    def swap(rows):
        return hop(rows, 1)

    groups = [
        [(half * near + member) * 2 + core for member in range(near)]
        for half in range(2)
        for core in range(2)
    ]

    def near_exchange(rows):
        return lax.all_to_all(
            rows.reshape(near, piece, width),
            "expert",
            split_axis=0,
            concat_axis=0,
            axis_index_groups=groups,
            tiled=True,
        ).reshape(near * piece, width)

    def after(rows, *others):
        return lax.optimization_barrier((rows, *others))[0]

    def place(placing, rows):
        return dot(placing, rows, ((0,), (0,)))

    meta = jnp.concatenate([expert_ids[0].astype(F32), route_weights[0]], axis=1)
    far_meta = far(meta)
    far_acts = far(acts[0])
    own_placing, own_weighting, own_gain = route(meta, half, chips, capacity)
    far_placing, far_weighting, far_gain = route(far_meta, half, chips, capacity)

    own_in = near_exchange(place(own_placing, acts[0]).astype(BF16))
    own_grad = (place(own_placing, grad_out[0]) * own_gain[:, None]).astype(BF16)
    own_grad = near_exchange(after(own_grad, own_in))
    far_grads = far(after(grad_out[0], far_meta))
    far_acts = after(far_acts, own_grad)
    far_in = near_exchange(place(far_placing, far_acts).astype(BF16))
    far_grads = after(far_grads, far_in)
    far_grad = near_exchange((place(far_placing, far_grads) * far_gain[:, None]).astype(BF16))
    rows_in = [far_in, swap(far_in), own_in, swap(own_in)]
    rows_grad = [far_grad, swap(far_grad), own_grad, swap(own_grad)]

    hiddens, gate_grads, up_grads, part_out, part_input = [], [], [], [], []
    for tokens, grads in zip(rows_in, rows_grad):
        pre_gate = dot(tokens, gate_weight, ((1,), (0,)))
        pre_up = dot(tokens, up_weight, ((1,), (0,)))
        sigma = jax.nn.sigmoid(pre_gate)
        active = pre_gate * sigma
        hidden = (active * pre_up).astype(BF16)
        part_out.append(dot(hidden, down_weight, ((1,), (0,))).astype(BF16))
        hidden_grad = dot(grads, down_weight, ((1,), (1,)))
        gate_grad = (hidden_grad * pre_up * sigma * (1.0 + pre_gate * (1.0 - sigma))).astype(BF16)
        up_grad = (hidden_grad * active).astype(BF16)
        part_input.append(
            (
                dot(gate_grad, gate_weight, ((1,), (1,))) + dot(up_grad, up_weight, ((1,), (1,)))
            ).astype(BF16)
        )
        hiddens.append(hidden)
        gate_grads.append(gate_grad)
        up_grads.append(up_grad)

    def expert_sum(parts):
        return (parts[0].astype(F32) + swap(parts[1]).astype(F32)).astype(BF16)

    def weighted(matrix, rows):
        return lax.dot_general(
            matrix,
            rows.astype(F32),
            (((1,), (0,)), ((), ())),
            precision=lax.Precision.HIGHEST,
            preferred_element_type=F32,
        )

    far_out = near_exchange(expert_sum(part_out[:2]))
    got_out = far(weighted(far_weighting, far_out).astype(BF16))
    far_input = near_exchange(after(expert_sum(part_input[:2]), far_out))
    got_input = far(dot(far_placing, far_input, ((1,), (0,))).astype(BF16))
    own_out = near_exchange(after(expert_sum(part_out[2:]), far_input))
    own_input = near_exchange(after(expert_sum(part_input[2:]), own_out))
    out_acts = (weighted(own_weighting, own_out) + got_out.astype(F32)).astype(BF16)
    grad_acts = (dot(own_placing, own_input, ((1,), (0,))) + got_input.astype(F32)).astype(BF16)

    rank_index = lax.axis_index("pipe")
    rank_count = lax.axis_size("pipe")
    mirror = [(p, rank_count - 1 - p) for p in range(rank_count)]
    kept_half = (rank_index >= rank_count // 2).astype(jnp.int32)

    def halves(units):
        units = jnp.concatenate(units, axis=0)
        return (
            lax.dynamic_slice_in_dim(units, kept_half * half_units, half_units, 1),
            lax.dynamic_slice_in_dim(units, (1 - kept_half) * half_units, half_units, 1),
        )

    all_in = jnp.concatenate(rows_in, axis=0)
    all_grad = jnp.concatenate(rows_grad, axis=0)
    keep_hidden, send_hidden = halves(hiddens)
    keep_gate, send_gate = halves(gate_grads)
    keep_up, send_up = halves(up_grads)
    rows_dims = ((0,), (0,))
    sent = []
    for a, b in ((send_hidden, all_grad), (all_in, send_gate), (all_in, send_up)):
        local = dot(a, b, rows_dims).astype(BF16)
        sent.append(lax.ppermute(after(local, *sent[-1:]), "pipe", mirror))
    kept = [
        dot(a, b, rows_dims).astype(BF16)
        for a, b in ((keep_hidden, all_grad), (all_in, keep_gate), (all_in, keep_up))
    ]
    grad_down, grad_gate, grad_up = [
        (own.astype(F32) + other.astype(F32)).astype(BF16)[None] for own, other in zip(kept, sent)
    ]
    return out_acts[None], grad_acts[None], grad_gate, grad_up, grad_down


def solution(mesh):
    tokens = P("pipe", "expert", None)
    columns = P("pipe", None, "expert")
    return jax.shard_map(
        on_device,
        mesh=mesh,
        in_specs=(tokens, tokens, tokens, tokens, columns, columns, tokens),
        out_specs=(tokens, tokens, columns, columns, tokens),
        check_vma=False,
    )
```

```python
import jax
import jax.numpy as jnp
from jax import lax
from jax.experimental import pallas as pl
from jax.experimental.pallas import tpu as pltpu
from jax.sharding import PartitionSpec as P

TOPK = 2
MB = 2
TOK_MB = 64
F32 = jnp.float32
BF16 = jnp.bfloat16
NN = ((1,), (0,))
NT = ((1,), (1,))
TN = ((0,), (0,))
VMEM_BYTES = 56 * 1024 * 1024


def dot(a, b, dims):
    return lax.dot_general(a, b, (dims, ((), ())), preferred_element_type=F32)


def tile_of(width):
    return 512 if width % 512 == 0 else width


def kernel_call(body, grid, in_specs, out_specs, out_shape, scratch=(), scalars=0):
    return pl.pallas_call(
        body,
        grid_spec=pltpu.PrefetchScalarGridSpec(
            num_scalar_prefetch=scalars,
            grid=grid,
            in_specs=in_specs,
            out_specs=out_specs,
            scratch_shapes=scratch,
        ),
        out_shape=out_shape,
        compiler_params=pltpu.CompilerParams(
            vmem_limit_bytes=VMEM_BYTES, dimension_semantics=("arbitrary",)
        ),
        cost_estimate=pl.CostEstimate(flops=1, bytes_accessed=1, transcendentals=0),
    )


def split3(w):
    high = w.astype(BF16)
    rest = w - high.astype(F32)
    middle = rest.astype(BF16)
    return high, middle, (rest - middle.astype(F32)).astype(BF16)


def place(placing, gain, parts):
    slots, tokens = placing.shape
    width = parts[0].shape[1]
    tile = tile_of(width)
    weighted = gain is not None

    def body(placing_ref, *refs):
        gain_ref = refs[0] if weighted else None
        part_refs, out_ref = refs[weighted:-1], refs[-1]
        rows = [ref[...] for ref in part_refs]
        rows = rows[0] if len(rows) == 1 else jnp.concatenate(rows, axis=0)
        total = dot(placing_ref[...], rows, NN)
        if weighted:
            total = total * gain_ref[...]
        out_ref[...] = total.astype(BF16)

    fixed = [placing] + ([gain] if weighted else [])
    return kernel_call(
        body,
        (width // tile,),
        [pl.BlockSpec(a.shape, lambda n: (0, 0)) for a in fixed]
        + [pl.BlockSpec((a.shape[0], tile), lambda n: (0, n)) for a in parts],
        pl.BlockSpec((slots, tile), lambda n: (0, n)),
        jax.ShapeDtypeStruct((slots, width), BF16),
    )(*fixed, *parts)


def combine(matrix, rows, parts=None):
    tokens, slots = matrix.shape
    width = rows.shape[1]
    tile = tile_of(width)

    def body(matrix_ref, rows_ref, *refs):
        rows = rows_ref[...]
        if matrix_ref.dtype == BF16:
            total = dot(matrix_ref[...], rows, NN)
        else:
            total = sum(dot(term, rows, NN) for term in split3(matrix_ref[...]))
        if parts is None:
            for b, ref in enumerate(refs):
                ref[...] = total[b * TOK_MB : (b + 1) * TOK_MB].astype(BF16)
        else:
            got = jnp.concatenate([ref[...] for ref in refs[:-1]], axis=0)
            refs[-1][...] = (total + got.astype(F32)).astype(BF16)

    part_spec = pl.BlockSpec((TOK_MB, tile), lambda n: (0, n))
    if parts is None:
        out_specs, out_shape = [part_spec] * MB, [jax.ShapeDtypeStruct((TOK_MB, width), BF16)] * MB
    else:
        out_specs = pl.BlockSpec((tokens, tile), lambda n: (0, n))
        out_shape = jax.ShapeDtypeStruct((tokens, width), BF16)
    return kernel_call(
        body,
        (width // tile,),
        [
            pl.BlockSpec((tokens, slots), lambda n: (0, 0)),
            pl.BlockSpec((slots, tile), lambda n: (0, n)),
        ]
        + [part_spec] * (0 if parts is None else MB),
        out_specs,
        out_shape,
    )(matrix, rows, *(parts or []))


def chunks(width):
    tile = tile_of(width)
    return [slice(n * tile, (n + 1) * tile) for n in range(width // tile)]


def forward(rows, gate_weight, up_weight, down_weight):
    count, width = rows[0].shape
    half_units = gate_weight.shape[1] // 2

    def body(a_ref, b_ref, gate_ref, up_ref, down_ref, pre_gate_ref, pre_up_ref, hidden_ref, out_a, out_b, acc_ref):
        step = pl.program_id(0)
        for r, (x_ref, out_ref) in enumerate(((a_ref, out_a), (b_ref, out_b))):
            here = slice(r * count, (r + 1) * count)
            pre_gate = dot(x_ref[...], gate_ref[...], NN)
            pre_up = dot(x_ref[...], up_ref[...], NN)
            pre_gate_ref[0, here] = pre_gate
            pre_up_ref[0, here] = pre_up
            hidden = (pre_gate * jax.nn.sigmoid(pre_gate) * pre_up).astype(BF16)
            hidden_ref[0, here] = hidden

            @pl.when(step == 0)
            def _():
                for cut in chunks(width):
                    acc_ref[here, cut] = dot(hidden, down_ref[:, cut], NN)

            @pl.when(step == 1)
            def _():
                for cut in chunks(width):
                    total = acc_ref[here, cut] + dot(hidden, down_ref[:, cut], NN)
                    out_ref[:, cut] = total.astype(BF16)

    whole = pl.BlockSpec((count, width), lambda n: (0, 0))
    columns = pl.BlockSpec((width, half_units), lambda n: (0, n))
    units = pl.BlockSpec((1, 2 * count, half_units), lambda n: (n, 0, 0))
    return kernel_call(
        body,
        (2,),
        [whole, whole, columns, columns, pl.BlockSpec((half_units, width), lambda n: (n, 0))],
        [units, units, units, whole, whole],
        [
            jax.ShapeDtypeStruct((2, 2 * count, half_units), F32),
            jax.ShapeDtypeStruct((2, 2 * count, half_units), F32),
            jax.ShapeDtypeStruct((2, 2 * count, half_units), BF16),
            jax.ShapeDtypeStruct((count, width), BF16),
            jax.ShapeDtypeStruct((count, width), BF16),
        ],
        [pltpu.VMEM((2 * count, width), F32)],
    )(*rows, gate_weight, up_weight, down_weight)


def backward(rows_grad, pre_gate, pre_up, gate_weight, up_weight, down_weight):
    count, width = rows_grad[0].shape
    half_units = gate_weight.shape[1] // 2

    def body(a_ref, b_ref, pre_gate_ref, pre_up_ref, gate_ref, up_ref, down_ref, units_ref, out_a, out_b, acc_ref):
        step = pl.program_id(0)
        for r, (g_ref, out_ref) in enumerate(((a_ref, out_a), (b_ref, out_b))):
            here = slice(r * count, (r + 1) * count)
            hidden_grad = dot(g_ref[...], down_ref[...], NT)
            pre_gate = pre_gate_ref[0, here]
            sigma = jax.nn.sigmoid(pre_gate)
            gate_grad = (
                hidden_grad * pre_up_ref[0, here] * sigma * (1.0 + pre_gate * (1.0 - sigma))
            ).astype(BF16)
            up_grad = (hidden_grad * (pre_gate * sigma)).astype(BF16)
            units_ref[0, here, :half_units] = gate_grad
            units_ref[0, here, half_units:] = up_grad

            @pl.when(step == 0)
            def _():
                for cut in chunks(width):
                    acc_ref[here, cut] = dot(gate_grad, gate_ref[cut], NT) + dot(
                        up_grad, up_ref[cut], NT
                    )

            @pl.when(step == 1)
            def _():
                for cut in chunks(width):
                    total = acc_ref[here, cut] + dot(gate_grad, gate_ref[cut], NT)
                    out_ref[:, cut] = (total + dot(up_grad, up_ref[cut], NT)).astype(BF16)

    whole = pl.BlockSpec((count, width), lambda n: (0, 0))
    columns = pl.BlockSpec((width, half_units), lambda n: (0, n))
    units = pl.BlockSpec((1, 2 * count, half_units), lambda n: (n, 0, 0))
    return kernel_call(
        body,
        (2,),
        [whole, whole, units, units, columns, columns, pl.BlockSpec((half_units, width), lambda n: (n, 0))],
        [pl.BlockSpec((1, 2 * count, 2 * half_units), lambda n: (n, 0, 0)), whole, whole],
        [
            jax.ShapeDtypeStruct((2, 2 * count, 2 * half_units), BF16),
            jax.ShapeDtypeStruct((count, width), BF16),
            jax.ShapeDtypeStruct((count, width), BF16),
        ],
        [pltpu.VMEM((2 * count, width), F32)],
    )(*rows_grad, pre_gate, pre_up, gate_weight, up_weight, down_weight)


def down_grad(which, hiddens, rows_grad, got=None):
    count, width = rows_grad[0].shape
    half_units = hiddens[0].shape[2]
    tile = tile_of(width)

    def body(which_ref, *refs):
        unit_refs, row_refs, rest = refs[:2], refs[2:6], refs[6:]
        total = None
        for n, row_ref in enumerate(row_refs):
            start = (n % 2) * count
            term = dot(unit_refs[n // 2][0, start : start + count], row_ref[...], TN)
            total = term if total is None else total + term
        if got is not None:
            total = total.astype(BF16).astype(F32) + rest[0][...].astype(F32)
        rest[-1][...] = total.astype(BF16)

    out_spec = pl.BlockSpec((half_units, tile), lambda n, w: (0, n))
    return kernel_call(
        body,
        (width // tile,),
        [pl.BlockSpec((1, 2 * count, half_units), lambda n, w: (w[0], 0, 0))] * 2
        + [pl.BlockSpec((count, tile), lambda n, w: (0, n))] * 4
        + [out_spec] * (got is not None),
        out_spec,
        jax.ShapeDtypeStruct((half_units, width), BF16),
        scalars=1,
    )(which, *hiddens, *rows_grad, *([] if got is None else [got]))


def gate_up_grad(which, units, rows, mirror_units, mirror_rows):
    count, width = rows[0].shape
    both = units[0].shape[2]
    half_units = both // 2
    tile = tile_of(width)

    def body(which_ref, *refs):
        unit_refs, mirror_refs, row_refs = refs[:2], refs[2:4], refs[4:12]
        gate_ref, up_ref = refs[12:]
        total = None
        for n, row_ref in enumerate(row_refs):
            start = (n % 2) * count
            here = slice(start, start + count)
            factor = unit_refs[n // 2][0, here] if n < 4 else mirror_refs[n // 2 - 2][here]
            term = dot(row_ref[...], factor, TN)
            total = term if total is None else total + term
        gate_ref[...] = total[:, :half_units].astype(BF16)
        up_ref[...] = total[:, half_units:].astype(BF16)

    out_spec = pl.BlockSpec((tile, half_units), lambda n, w: (n, 0))
    return kernel_call(
        body,
        (width // tile,),
        [pl.BlockSpec((1, 2 * count, both), lambda n, w: (w[0], 0, 0))] * 2
        + [pl.BlockSpec((2 * count, both), lambda n, w: (0, 0))] * 2
        + [pl.BlockSpec((count, tile), lambda n, w: (0, n))] * 8,
        [out_spec] * 2,
        [jax.ShapeDtypeStruct((width, half_units), BF16)] * 2,
        scalars=1,
    )(which, *units, *mirror_units, *rows, *mirror_rows)


def route(meta, half, expert_count, capacity):
    ids, gain = meta[:, :TOPK].astype(jnp.int32), meta[:, TOPK:]
    flat_ids = ids.reshape(MB, TOK_MB * TOPK)
    member = (flat_ids[:, :, None] == jnp.arange(expert_count, dtype=jnp.int32)).astype(jnp.int32)
    running = jnp.cumsum(member, axis=1) - 1
    rank = jnp.sum(member * running, axis=2)
    batch = jnp.arange(MB, dtype=jnp.int32)[:, None]
    near = expert_count // 2
    target = (((flat_ids - half * near) * MB + batch) * capacity + rank).reshape(ids.shape)
    slots = jnp.arange(near * MB * capacity, dtype=jnp.int32)
    matches = (target[:, :, None] == slots).astype(F32)
    turned = (target.T[:, None, :] == slots[:, None]).astype(F32)
    weighting = jnp.sum(matches * gain[:, :, None], axis=1)
    slot_gain = jnp.sum(turned * gain.T[:, None, :], axis=(0, 2))[:, None]
    return jnp.sum(turned, axis=0).astype(BF16), jnp.sum(matches, axis=1).astype(BF16), weighting, slot_gain


def on_device(acts, grad_out, expert_ids, route_weights, w_gate, w_up, w_down):
    weights = (w_gate[0], w_up[0], w_down[0])
    devices = lax.axis_size("expert")
    chips = devices // 2
    near = chips // 2
    capacity = 3 * TOPK * TOK_MB // (2 * chips)
    piece = MB * capacity
    width = acts.shape[2]
    half = (lax.axis_index("expert") >= devices // 2).astype(jnp.int32)
    rank_count = lax.axis_size("pipe")
    kept_half = (lax.axis_index("pipe") >= rank_count // 2).astype(jnp.int32)
    kept = kept_half.reshape(1)

    def hop(rows, distance):
        return lax.ppermute(rows, "expert", [(i, i ^ distance) for i in range(devices)])

    def far(rows):
        return hop(rows, devices // 2)

    def swap(rows):
        return hop(rows, 1)

    def mirror(rows):
        return lax.ppermute(rows, "pipe", [(p, rank_count - 1 - p) for p in range(rank_count)])

    groups = [
        [(part * near + member) * 2 + core for member in range(near)]
        for part in range(2)
        for core in range(2)
    ]

    def near_exchange(rows):
        return lax.all_to_all(
            rows.reshape(near, piece, width),
            "expert",
            split_axis=0,
            concat_axis=0,
            axis_index_groups=groups,
            tiled=True,
        ).reshape(near * piece, width)

    def tie(*arrays):
        return lax.optimization_barrier(arrays)

    def expert_sum(mine, other):
        return (mine.astype(F32) + swap(other).astype(F32)).astype(BF16)

    acts_parts = [acts[0, b * TOK_MB : (b + 1) * TOK_MB] for b in range(MB)]
    grad_parts = [grad_out[0, b * TOK_MB : (b + 1) * TOK_MB] for b in range(MB)]
    meta = jnp.concatenate([expert_ids[0].astype(F32), route_weights[0]], axis=1)
    far_meta = far(meta)
    own_placing, own_back, own_weighting, own_gain = route(meta, half, chips, capacity)
    far_placing, far_back, far_weighting, far_gain = route(far_meta, half, chips, capacity)

    own_in = place(own_placing, None, [acts[0]])
    far_acts_0 = far(acts_parts[0])
    own_in = near_exchange(own_in)
    own_grad = place(own_placing, own_gain, [grad_out[0]])
    own_in, far_acts_0, acts_1, own_grad = tie(own_in, far_acts_0, acts_parts[1], own_grad)
    far_acts_1 = far(acts_1)
    own_grad = near_exchange(own_grad)
    own_in_b = swap(own_in)
    mirror_own = mirror(own_in)
    far_in = place(far_placing, None, [far_acts_0, far_acts_1])
    far_in, own_grad, own_in_b, grads_0 = tie(far_in, own_grad, own_in_b, grad_parts[0])
    far_grads_0 = far(grads_0)
    far_in = near_exchange(far_in)
    own_pre_gate, own_pre_up, own_hidden, own_out, own_out_b = forward(
        (own_in, own_in_b), *weights
    )
    own_out = expert_sum(own_out, own_out_b)
    own_grad_b = swap(own_grad)
    far_in, far_grads_0, own_out, mirror_own, grads_1 = tie(
        far_in, far_grads_0, own_out, mirror_own, grad_parts[1]
    )
    far_grads_1 = far(grads_1)
    own_out = near_exchange(own_out)
    far_in_b = swap(far_in)
    mirror_far = mirror(far_in)
    mirror_own_b = swap(mirror_own)
    own_units, own_input, own_input_b = backward(
        (own_grad, own_grad_b), own_pre_gate, own_pre_up, *weights
    )
    far_grad = place(far_placing, far_gain, [far_grads_0, far_grads_1])
    far_grad, own_out = tie(far_grad, own_out)
    far_grad = near_exchange(far_grad)
    far_pre_gate, far_pre_up, far_hidden, far_out, far_out_b = forward(
        (far_in, far_in_b), *weights
    )
    far_out = expert_sum(far_out, far_out_b)
    own_input = expert_sum(own_input, own_input_b)
    far_grad, far_out, mirror_far, own_input = tie(far_grad, far_out, mirror_far, own_input)
    far_out = near_exchange(far_out)
    far_grad_b = swap(far_grad)
    mirror_far_b = swap(mirror_far)
    far_units, far_input, far_input_b = backward(
        (far_grad, far_grad_b), far_pre_gate, far_pre_up, *weights
    )
    far_input = expert_sum(far_input, far_input_b)
    rows_grad = (own_grad, own_grad_b, far_grad, far_grad_b)
    got_down = mirror(down_grad(1 - kept, (own_hidden, far_hidden), rows_grad))
    back_out = combine(far_weighting, far_out)
    far_input, back_out = tie(far_input, back_out)
    got_out_0 = far(back_out[0])
    far_input = near_exchange(far_input)
    far_input, got_out_0, back_out_1, own_input = tie(far_input, got_out_0, back_out[1], own_input)
    got_out_1 = far(back_out_1)
    own_input = near_exchange(own_input)
    back_input = combine(far_back, far_input)
    got_out_1, own_input, got_down, back_input, own_units, far_units = tie(
        got_out_1, own_input, got_down, back_input, own_units, far_units
    )
    got_input = [far(part) for part in back_input]
    mirror_units = [
        mirror(lax.dynamic_index_in_dim(units, 1 - kept_half, 0, keepdims=False))
        for units in (own_units, far_units)
    ]
    grad_down = down_grad(kept, (own_hidden, far_hidden), rows_grad, got_down)
    out_acts = combine(own_weighting, own_out, [got_out_0, got_out_1])
    grad_gate, grad_up = gate_up_grad(
        kept,
        (own_units, far_units),
        (own_in, own_in_b, far_in, far_in_b),
        mirror_units,
        (mirror_own, mirror_own_b, mirror_far, mirror_far_b),
    )
    grad_acts = combine(own_back, own_input, got_input)
    return out_acts[None], grad_acts[None], grad_gate[None], grad_up[None], grad_down[None]


def solution(mesh):
    tokens = P("pipe", "expert", None)
    columns = P("pipe", None, "expert")
    return jax.shard_map(
        on_device,
        mesh=mesh,
        in_specs=(tokens, tokens, tokens, tokens, columns, columns, tokens),
        out_specs=(tokens, tokens, columns, columns, tokens),
        check_vma=False,
    )
```

```python
import jax
import jax.numpy as jnp
from jax import lax
from jax.experimental import pallas as pl
from jax.experimental.pallas import tpu as pltpu
from jax.sharding import PartitionSpec as P

TOPK = 2
MB = 2
TOK_MB = 64
F32 = jnp.float32
BF16 = jnp.bfloat16
NN = ((1,), (0,))
NT = ((1,), (1,))
TN = ((0,), (0,))
VMEM_BYTES = 56 * 1024 * 1024


def dot(a, b, dims):
    return lax.dot_general(a, b, (dims, ((), ())), preferred_element_type=F32)


def tile_of(width):
    return 512 if width % 512 == 0 else width


def kernel_call(body, grid, in_specs, out_specs, out_shape, scratch=(), scalars=0):
    return pl.pallas_call(
        body,
        grid_spec=pltpu.PrefetchScalarGridSpec(
            num_scalar_prefetch=scalars,
            grid=grid,
            in_specs=in_specs,
            out_specs=out_specs,
            scratch_shapes=scratch,
        ),
        out_shape=out_shape,
        compiler_params=pltpu.CompilerParams(
            vmem_limit_bytes=VMEM_BYTES, dimension_semantics=("arbitrary",)
        ),
        cost_estimate=pl.CostEstimate(flops=1, bytes_accessed=1, transcendentals=0),
    )


def place(placing, rows, gain=None):
    slots = dot(placing, rows, NN)
    return (slots if gain is None else slots * gain).astype(BF16)


def combine(matrix, rows):
    if matrix.dtype == BF16:
        return dot(matrix, rows, NN)
    return lax.dot_general(
        matrix,
        rows.astype(F32),
        (NN, ((), ())),
        precision=lax.Precision.HIGHEST,
        preferred_element_type=F32,
    )


def chunks(width):
    tile = tile_of(width)
    return [slice(n * tile, (n + 1) * tile) for n in range(width // tile)]


def forward(rows, gate_weight, up_weight, down_weight):
    count, width = rows[0].shape
    half_units = gate_weight.shape[1] // 2

    def body(a_ref, b_ref, gate_ref, up_ref, down_ref, pre_gate_ref, pre_up_ref, hidden_ref, out_a, out_b, x_ref, acc_ref):
        step = pl.program_id(0)

        @pl.when(step == 0)
        def _():
            x_ref[:count] = a_ref[...]
            x_ref[count:] = b_ref[...]

        pre_gate = dot(x_ref[...], gate_ref[...], NN)
        pre_up = dot(x_ref[...], up_ref[...], NN)
        pre_gate_ref[0] = pre_gate
        pre_up_ref[0] = pre_up
        hidden = (pre_gate * jax.nn.sigmoid(pre_gate) * pre_up).astype(BF16)
        hidden_ref[0] = hidden

        @pl.when(step == 0)
        def _():
            for cut in chunks(width):
                acc_ref[:, cut] = dot(hidden, down_ref[:, cut], NN)

        @pl.when(step == 1)
        def _():
            for cut in chunks(width):
                total = (acc_ref[:, cut] + dot(hidden, down_ref[:, cut], NN)).astype(BF16)
                out_a[:, cut] = total[:count]
                out_b[:, cut] = total[count:]

    whole = pl.BlockSpec((count, width), lambda n: (0, 0))
    columns = pl.BlockSpec((width, half_units), lambda n: (0, n))
    units = pl.BlockSpec((1, 2 * count, half_units), lambda n: (n, 0, 0))
    return kernel_call(
        body,
        (2,),
        [whole, whole, columns, columns, pl.BlockSpec((half_units, width), lambda n: (n, 0))],
        [units, units, units, whole, whole],
        [
            jax.ShapeDtypeStruct((2, 2 * count, half_units), F32),
            jax.ShapeDtypeStruct((2, 2 * count, half_units), F32),
            jax.ShapeDtypeStruct((2, 2 * count, half_units), BF16),
            jax.ShapeDtypeStruct((count, width), BF16),
            jax.ShapeDtypeStruct((count, width), BF16),
        ],
        [pltpu.VMEM((2 * count, width), BF16), pltpu.VMEM((2 * count, width), F32)],
    )(*rows, gate_weight, up_weight, down_weight)


def backward(rows_grad, pre_gate, pre_up, gate_weight, up_weight, down_weight):
    count, width = rows_grad[0].shape
    half_units = gate_weight.shape[1] // 2

    def body(a_ref, b_ref, pre_gate_ref, pre_up_ref, gate_ref, up_ref, down_ref, units_ref, out_a, out_b, x_ref, acc_ref):
        step = pl.program_id(0)

        @pl.when(step == 0)
        def _():
            x_ref[:count] = a_ref[...]
            x_ref[count:] = b_ref[...]

        hidden_grad = dot(x_ref[...], down_ref[...], NT)
        pre_gate = pre_gate_ref[0]
        sigma = jax.nn.sigmoid(pre_gate)
        gate_grad = (
            hidden_grad * pre_up_ref[0] * sigma * (1.0 + pre_gate * (1.0 - sigma))
        ).astype(BF16)
        up_grad = (hidden_grad * (pre_gate * sigma)).astype(BF16)
        units_ref[0, :, :half_units] = gate_grad
        units_ref[0, :, half_units:] = up_grad

        @pl.when(step == 0)
        def _():
            for cut in chunks(width):
                acc_ref[:, cut] = dot(gate_grad, gate_ref[cut], NT) + dot(up_grad, up_ref[cut], NT)

        @pl.when(step == 1)
        def _():
            for cut in chunks(width):
                total = acc_ref[:, cut] + dot(gate_grad, gate_ref[cut], NT)
                total = (total + dot(up_grad, up_ref[cut], NT)).astype(BF16)
                out_a[:, cut] = total[:count]
                out_b[:, cut] = total[count:]

    whole = pl.BlockSpec((count, width), lambda n: (0, 0))
    columns = pl.BlockSpec((width, half_units), lambda n: (0, n))
    units = pl.BlockSpec((1, 2 * count, half_units), lambda n: (n, 0, 0))
    return kernel_call(
        body,
        (2,),
        [whole, whole, units, units, columns, columns, pl.BlockSpec((half_units, width), lambda n: (n, 0))],
        [pl.BlockSpec((1, 2 * count, 2 * half_units), lambda n: (n, 0, 0)), whole, whole],
        [
            jax.ShapeDtypeStruct((2, 2 * count, 2 * half_units), BF16),
            jax.ShapeDtypeStruct((count, width), BF16),
            jax.ShapeDtypeStruct((count, width), BF16),
        ],
        [pltpu.VMEM((2 * count, width), BF16), pltpu.VMEM((2 * count, width), F32)],
    )(*rows_grad, pre_gate, pre_up, gate_weight, up_weight, down_weight)


def down_grad(which, hiddens, rows_grad, got=None):
    count, width = rows_grad[0].shape
    half_units = hiddens[0].shape[2]
    tile = tile_of(width)

    def body(which_ref, *refs):
        unit_refs, row_refs, rest = refs[:2], refs[2:6], refs[6:]
        turned_ref = rest[-1]

        @pl.when(pl.program_id(0) == 0)
        def _():
            for n, unit_ref in enumerate(unit_refs):
                turned_ref[:, 2 * n * count : 2 * (n + 1) * count] = unit_ref[0].T

        rows = jnp.concatenate([ref[...] for ref in row_refs], axis=0)
        total = dot(turned_ref[...], rows, NN)
        if got is not None:
            total = total.astype(BF16).astype(F32) + rest[0][...].astype(F32)
        rest[-2][...] = total.astype(BF16)

    out_spec = pl.BlockSpec((half_units, tile), lambda n, w: (0, n))
    return kernel_call(
        body,
        (width // tile,),
        [pl.BlockSpec((1, 2 * count, half_units), lambda n, w: (w[0], 0, 0))] * 2
        + [pl.BlockSpec((count, tile), lambda n, w: (0, n))] * 4
        + [out_spec] * (got is not None),
        out_spec,
        jax.ShapeDtypeStruct((half_units, width), BF16),
        [pltpu.VMEM((half_units, 4 * count), BF16)],
        scalars=1,
    )(which, *hiddens, *rows_grad, *([] if got is None else [got]))


def gate_up_grad(which, units, rows, mirror_units, mirror_rows):
    count, width = rows[0].shape
    both = units[0].shape[2]
    half_units = both // 2
    tile = tile_of(width)

    def body(which_ref, *refs):
        unit_refs, mirror_refs, row_refs = refs[:2], refs[2:4], refs[4:12]
        gate_ref, up_ref, turned_ref = refs[12:]

        @pl.when(pl.program_id(0) == 0)
        def _():
            for n, factor in enumerate([ref[0] for ref in unit_refs] + [ref[...] for ref in mirror_refs]):
                turned_ref[:, 2 * n * count : 2 * (n + 1) * count] = factor.T

        rows = jnp.concatenate([ref[...] for ref in row_refs], axis=0)
        total = dot(turned_ref[...], rows, NN).astype(BF16).T
        gate_ref[...] = total[:, :half_units]
        up_ref[...] = total[:, half_units:]

    out_spec = pl.BlockSpec((tile, half_units), lambda n, w: (n, 0))
    return kernel_call(
        body,
        (width // tile,),
        [pl.BlockSpec((1, 2 * count, both), lambda n, w: (w[0], 0, 0))] * 2
        + [pl.BlockSpec((2 * count, both), lambda n, w: (0, 0))] * 2
        + [pl.BlockSpec((count, tile), lambda n, w: (0, n))] * 8,
        [out_spec] * 2,
        [jax.ShapeDtypeStruct((width, half_units), BF16)] * 2,
        [pltpu.VMEM((both, 8 * count), BF16)],
        scalars=1,
    )(which, *units, *mirror_units, *rows, *mirror_rows)


def route(meta, half, expert_count, capacity):
    ids, gain = meta[:, :TOPK].astype(jnp.int32), meta[:, TOPK:]
    flat_ids = ids.reshape(MB, TOK_MB * TOPK)
    member = (flat_ids[:, :, None] == jnp.arange(expert_count, dtype=jnp.int32)).astype(jnp.int32)
    running = jnp.cumsum(member, axis=1) - 1
    rank = jnp.sum(member * running, axis=2)
    batch = jnp.arange(MB, dtype=jnp.int32)[:, None]
    near = expert_count // 2
    target = (((flat_ids - half * near) * MB + batch) * capacity + rank).reshape(ids.shape)
    slots = jnp.arange(near * MB * capacity, dtype=jnp.int32)
    matches = (target[:, :, None] == slots).astype(F32)
    turned = (target.T[:, None, :] == slots[:, None]).astype(F32)
    weighting = jnp.sum(matches * gain[:, :, None], axis=1)
    slot_gain = jnp.sum(turned * gain.T[:, None, :], axis=(0, 2))[:, None]
    return jnp.sum(turned, axis=0).astype(BF16), jnp.sum(matches, axis=1).astype(BF16), weighting, slot_gain


def on_device(acts, grad_out, expert_ids, route_weights, w_gate, w_up, w_down):
    weights = (w_gate[0], w_up[0], w_down[0])
    devices = lax.axis_size("expert")
    chips = devices // 2
    near = chips // 2
    capacity = 3 * TOPK * TOK_MB // (2 * chips)
    piece = MB * capacity
    width = acts.shape[2]
    half = (lax.axis_index("expert") >= devices // 2).astype(jnp.int32)
    rank_count = lax.axis_size("pipe")
    kept_half = (lax.axis_index("pipe") >= rank_count // 2).astype(jnp.int32)
    kept = kept_half.reshape(1)

    def hop(rows, distance):
        return lax.ppermute(rows, "expert", [(i, i ^ distance) for i in range(devices)])

    def far(rows):
        return hop(rows, devices // 2)

    def swap(rows):
        return hop(rows, 1)

    def mirror(rows):
        return lax.ppermute(rows, "pipe", [(p, rank_count - 1 - p) for p in range(rank_count)])

    groups = [
        [(part * near + member) * 2 + core for member in range(near)]
        for part in range(2)
        for core in range(2)
    ]

    def near_exchange(rows):
        return lax.all_to_all(
            rows.reshape(near, piece, width),
            "expert",
            split_axis=0,
            concat_axis=0,
            axis_index_groups=groups,
            tiled=True,
        ).reshape(near * piece, width)

    def tie(*arrays):
        return lax.optimization_barrier(arrays)

    def expert_sum(mine, other):
        return (mine.astype(F32) + swap(other).astype(F32)).astype(BF16)

    acts_parts = [acts[0, b * TOK_MB : (b + 1) * TOK_MB] for b in range(MB)]
    grad_parts = [grad_out[0, b * TOK_MB : (b + 1) * TOK_MB] for b in range(MB)]
    meta = jnp.concatenate([expert_ids[0].astype(F32), route_weights[0]], axis=1)
    far_meta = far(meta)
    own_placing, own_back, own_weighting, own_gain = route(meta, half, chips, capacity)

    own_in = near_exchange(place(own_placing, acts[0]))
    far_acts_0 = far(acts_parts[0])
    acts_1, far_meta = tie(acts_parts[1], far_meta)
    far_acts_1 = far(acts_1)
    far_placing, far_back, far_weighting, far_gain = route(far_meta, half, chips, capacity)

    own_grad, own_in = tie(place(own_placing, grad_out[0], own_gain), own_in)
    own_grad = near_exchange(own_grad)
    own_in_b = swap(own_in)
    mirror_own = mirror(own_in)
    grads_0, far_acts_0 = tie(grad_parts[0], far_acts_0)
    far_grads_0 = far(grads_0)

    far_acts_1, own_grad, own_in_b = tie(far_acts_1, own_grad, own_in_b)
    far_in = near_exchange(place(far_placing, jnp.concatenate([far_acts_0, far_acts_1], axis=0)))
    grads_1, far_acts_1 = tie(grad_parts[1], far_acts_1)
    far_grads_1 = far(grads_1)
    own_grad_b = swap(own_grad)
    own_pre_gate, own_pre_up, own_hidden, own_out, own_out_b = forward((own_in, own_in_b), *weights)
    own_units, own_input, own_input_b = backward(
        (own_grad, own_grad_b), own_pre_gate, own_pre_up, *weights
    )

    far_grad = place(far_placing, jnp.concatenate([far_grads_0, far_grads_1], axis=0), far_gain)
    far_grad, far_in, own_units, own_input, own_input_b, mirror_own = tie(
        far_grad, far_in, own_units, own_input, own_input_b, mirror_own
    )
    far_in_b = swap(far_in)
    far_grad = near_exchange(far_grad)
    mirror_far = mirror(far_in)
    own_out = expert_sum(own_out, own_out_b)
    far_pre_gate, far_pre_up, far_hidden, far_out, far_out_b = forward((far_in, far_in_b), *weights)
    far_out = expert_sum(far_out, far_out_b)

    far_out, far_grad, own_out = tie(far_out, far_grad, own_out)
    far_out = near_exchange(far_out)
    far_grad_b = swap(far_grad)
    own_input = expert_sum(own_input, own_input_b)
    mirror_own_b = swap(mirror_own)
    mirror_units_own = mirror(lax.dynamic_index_in_dim(own_units, 1 - kept_half, 0, keepdims=False))
    far_units, far_input, far_input_b = backward(
        (far_grad, far_grad_b), far_pre_gate, far_pre_up, *weights
    )
    far_input = expert_sum(far_input, far_input_b)

    far_input, far_out, own_input, mirror_own_b, mirror_far, mirror_units_own = tie(
        far_input, far_out, own_input, mirror_own_b, mirror_far, mirror_units_own
    )
    back_out = combine(far_weighting, far_out).astype(BF16)
    got_out_0 = far(back_out[:TOK_MB])
    got_out_1 = far(back_out[TOK_MB:])
    far_input = near_exchange(far_input)
    mirror_units_far = mirror(lax.dynamic_index_in_dim(far_units, 1 - kept_half, 0, keepdims=False))
    rows_grad = (own_grad, own_grad_b, far_grad, far_grad_b)
    send_down = down_grad(1 - kept, (own_hidden, far_hidden), rows_grad)
    mirror_far_b = swap(mirror_far)

    send_down, mirror_units_far = tie(send_down, mirror_units_far)
    got_down = mirror(send_down)
    back_input = combine(far_back, far_input).astype(BF16)
    own_out, far_input, back_input, got_out_0, mirror_far_b, send_down = tie(
        own_out, far_input, back_input, got_out_0, mirror_far_b, send_down
    )
    own_out = near_exchange(own_out)
    got_input_0 = far(back_input[:TOK_MB])
    back_input_1, got_out_1 = tie(back_input[TOK_MB:], got_out_1)
    got_input_1 = far(back_input_1)
    own_input, own_out, got_out_1 = tie(own_input, own_out, got_out_1)
    own_input = near_exchange(own_input)
    grad_gate, grad_up = gate_up_grad(
        kept,
        (own_units, far_units),
        (own_in, own_in_b, far_in, far_in_b),
        (mirror_units_own, mirror_units_far),
        (mirror_own, mirror_own_b, mirror_far, mirror_far_b),
    )
    got_out = jnp.concatenate([got_out_0, got_out_1], axis=0).astype(F32)
    out_acts = (combine(own_weighting, own_out) + got_out).astype(BF16)
    grad_down = down_grad(kept, (own_hidden, far_hidden), rows_grad, got_down)
    got_input = jnp.concatenate([got_input_0, got_input_1], axis=0).astype(F32)
    grad_acts = (combine(own_back, own_input) + got_input).astype(BF16)
    return out_acts[None], grad_acts[None], grad_gate[None], grad_up[None], grad_down[None]


def solution(mesh):
    tokens = P("pipe", "expert", None)
    columns = P("pipe", None, "expert")
    return jax.shard_map(
        on_device,
        mesh=mesh,
        in_specs=(tokens, tokens, tokens, tokens, columns, columns, tokens),
        out_specs=(tokens, tokens, columns, columns, tokens),
        check_vma=False,
    )
```

```python
import jax
import jax.numpy as jnp
from jax import lax
from jax.sharding import PartitionSpec as P

TOPK = 2
MB = 2
TOK_MB = 64
F32 = jnp.float32
BF16 = jnp.bfloat16


def dot(a, b, dims):
    return lax.dot_general(a, b, (dims, ((), ())), preferred_element_type=F32)


def route(ids, gain, expert_count, capacity, chip):
    flat_ids = ids.reshape(-1)
    member = (flat_ids[:, None] == jnp.arange(expert_count, dtype=jnp.int32)[None, :]).astype(jnp.int32)
    running = jnp.cumsum(member, axis=0) - 1
    slot_rank = jnp.sum(member * running, axis=1)
    target = ((flat_ids ^ chip) * capacity + slot_rank).reshape(ids.shape)
    slots = jnp.arange(expert_count * capacity, dtype=jnp.int32)
    matches = (target[:, :, None] == slots[None, None, :]).astype(F32)
    placing = jnp.sum(matches, axis=1).astype(BF16)
    weighting = jnp.sum(matches * gain[:, :, None], axis=1)
    return placing, weighting, jnp.sum(weighting, axis=0)


def on_device(acts, grad_out, expert_ids, route_weights, w_gate, w_up, w_down):
    gate_weight, up_weight, down_weight = w_gate[0], w_up[0], w_down[0]
    devices = lax.axis_size("expert")
    chips = devices // 2
    capacity = 3 * TOPK * TOK_MB // (2 * chips)
    slot_count = chips * capacity
    width = gate_weight.shape[0]
    half_units = gate_weight.shape[1] // 2
    chip = lax.axis_index("expert") // 2
    other_core = [(i, i ^ 1) for i in range(devices)]

    def across(blocks):
        pieces = [blocks[d * capacity : (d + 1) * capacity] for d in range(chips)]
        moved = [
            piece if d == 0 else lax.ppermute(piece, "expert", [(i, i ^ (2 * d)) for i in range(devices)])
            for d, piece in enumerate(pieces)
        ]
        return jnp.concatenate(moved, axis=0)

    def swap(rows):
        return lax.ppermute(rows, "expert", other_core)

    rows_in, rows_grad, hiddens, gate_grads, up_grads = [], [], [], [], []
    routes, outs, inputs = [], [], []
    for b in range(MB):
        rows = slice(b * TOK_MB, (b + 1) * TOK_MB)
        placing, weighting, slot_gain = route(
            expert_ids[0, rows], route_weights[0, rows], chips, capacity, chip
        )
        routes.append((placing, weighting))
        tokens = dot(placing, acts[0, rows], ((0,), (0,))).astype(BF16)
        grads = dot(placing, grad_out[0, rows], ((0,), (0,)))
        grads = (grads * slot_gain[:, None]).astype(BF16)
        tokens = across(tokens)
        rows_in.append([tokens, swap(tokens)])
        grads = across(grads)
        rows_grad.append([grads, swap(grads)])

    for b in range(MB):
        part_out, part_input = [], []
        hiddens.append([])
        gate_grads.append([])
        up_grads.append([])
        for tokens, grads in zip(rows_in[b], rows_grad[b]):
            pre_gate = dot(tokens, gate_weight, ((1,), (0,)))
            pre_up = dot(tokens, up_weight, ((1,), (0,)))
            sigma = jax.nn.sigmoid(pre_gate)
            active = pre_gate * sigma
            hidden = (active * pre_up).astype(BF16)
            part_out.append(dot(hidden, down_weight, ((1,), (0,))).astype(BF16))
            hidden_grad = dot(grads, down_weight, ((1,), (1,)))
            gate_grad = (
                hidden_grad * pre_up * sigma * (1.0 + pre_gate * (1.0 - sigma))
            ).astype(BF16)
            up_grad = (hidden_grad * active).astype(BF16)
            part_input.append(
                (
                    dot(gate_grad, gate_weight, ((1,), (1,)))
                    + dot(up_grad, up_weight, ((1,), (1,)))
                ).astype(BF16)
            )
            hiddens[b].append(hidden)
            gate_grads[b].append(gate_grad)
            up_grads[b].append(up_grad)
        back = []
        for own, other in (part_out, part_input):
            both = (own.astype(F32) + swap(other).astype(F32)).astype(BF16)
            back.append(across(both))
        placing, weighting = routes[b]
        outs.append(
            lax.dot_general(
                weighting,
                back[0].astype(F32),
                (((1,), (0,)), ((), ())),
                precision=lax.Precision.HIGHEST,
                preferred_element_type=F32,
            ).astype(BF16)
        )
        inputs.append(dot(placing, back[1], ((1,), (0,))).astype(BF16))

    rank_index = lax.axis_index("pipe")
    rank_count = lax.axis_size("pipe")
    mirror = [(p, rank_count - 1 - p) for p in range(rank_count)]
    kept_half = (rank_index >= rank_count // 2).astype(jnp.int32)

    def joined(parts):
        return jnp.concatenate([part for batch in parts for part in batch], axis=0)

    def halves(units):
        return (
            lax.dynamic_slice_in_dim(units, kept_half * half_units, half_units, 1),
            lax.dynamic_slice_in_dim(units, (1 - kept_half) * half_units, half_units, 1),
        )

    all_in = joined(rows_in)
    all_grad = joined(rows_grad)
    keep_hidden, send_hidden = halves(joined(hiddens))
    keep_gate, send_gate = halves(joined(gate_grads))
    keep_up, send_up = halves(joined(up_grads))
    rows_dims = ((0,), (0,))
    sent = []
    for a, b in ((send_hidden, all_grad), (all_in, send_gate), (all_in, send_up)):
        local = dot(a, b, rows_dims).astype(BF16)
        if sent:
            local, sent[-1] = lax.optimization_barrier((local, sent[-1]))
        sent.append(lax.ppermute(local, "pipe", mirror))
    kept = [
        dot(a, b, rows_dims).astype(BF16)
        for a, b in ((keep_hidden, all_grad), (all_in, keep_gate), (all_in, keep_up))
    ]
    grad_down, grad_gate, grad_up = [
        (own.astype(F32) + other.astype(F32)).astype(BF16)[None] for own, other in zip(kept, sent)
    ]
    out_acts = jnp.concatenate(outs, axis=0)[None]
    grad_acts = jnp.concatenate(inputs, axis=0)[None]
    return out_acts, grad_acts, grad_gate, grad_up, grad_down


def solution(mesh):
    tokens = P("pipe", "expert", None)
    columns = P("pipe", None, "expert")
    return jax.shard_map(
        on_device,
        mesh=mesh,
        in_specs=(tokens, tokens, tokens, tokens, columns, columns, tokens),
        out_specs=(tokens, tokens, columns, columns, tokens),
        check_vma=False,
    )
```

```python
import jax
import jax.numpy as jnp
from jax import lax
from jax.experimental import pallas as pl
from jax.experimental.pallas import tpu as pltpu
from jax.sharding import PartitionSpec as P

TOPK = 2
MB = 2
TOK_MB = 64
F32 = jnp.float32
BF16 = jnp.bfloat16
NN = ((1,), (0,))
NT = ((1,), (1,))
TN = ((0,), (0,))
VMEM_BYTES = 56 * 1024 * 1024


def dot(a, b, dims):
    return lax.dot_general(a, b, (dims, ((), ())), preferred_element_type=F32)


def tile_of(width):
    return 512 if width % 512 == 0 else width


def kernel_call(body, grid, in_specs, out_specs, out_shape, scratch=(), scalars=0):
    return pl.pallas_call(
        body,
        grid_spec=pltpu.PrefetchScalarGridSpec(
            num_scalar_prefetch=scalars,
            grid=grid,
            in_specs=in_specs,
            out_specs=out_specs,
            scratch_shapes=scratch,
        ),
        out_shape=out_shape,
        compiler_params=pltpu.CompilerParams(
            vmem_limit_bytes=VMEM_BYTES, dimension_semantics=("arbitrary",)
        ),
        cost_estimate=pl.CostEstimate(flops=1, bytes_accessed=1, transcendentals=0),
    )


def place(placing, rows, gain=None):
    slots = dot(placing, rows, NN)
    return (slots if gain is None else slots * gain).astype(BF16)


def combine(matrix, rows):
    if matrix.dtype == BF16:
        return dot(matrix, rows, NN)
    return lax.dot_general(
        matrix,
        rows.astype(F32),
        (NN, ((), ())),
        precision=lax.Precision.HIGHEST,
        preferred_element_type=F32,
    )


def chunks(width):
    tile = tile_of(width)
    return [slice(n * tile, (n + 1) * tile) for n in range(width // tile)]


def forward(rows, gate_weight, up_weight, down_weight):
    count, width = rows[0].shape
    half_units = gate_weight.shape[1] // 2

    def body(a_ref, b_ref, gate_ref, up_ref, down_ref, pre_gate_ref, pre_up_ref, hidden_ref, out_a, out_b, x_ref, acc_ref):
        step = pl.program_id(0)

        @pl.when(step == 0)
        def _():
            x_ref[:count] = a_ref[...]
            x_ref[count:] = b_ref[...]

        pre_gate = dot(x_ref[...], gate_ref[...], NN)
        pre_up = dot(x_ref[...], up_ref[...], NN)
        pre_gate_ref[0] = pre_gate
        pre_up_ref[0] = pre_up
        hidden = (pre_gate * jax.nn.sigmoid(pre_gate) * pre_up).astype(BF16)
        hidden_ref[0] = hidden

        @pl.when(step == 0)
        def _():
            for cut in chunks(width):
                acc_ref[:, cut] = dot(hidden, down_ref[:, cut], NN)

        @pl.when(step == 1)
        def _():
            for cut in chunks(width):
                total = (acc_ref[:, cut] + dot(hidden, down_ref[:, cut], NN)).astype(BF16)
                out_a[:, cut] = total[:count]
                out_b[:, cut] = total[count:]

    whole = pl.BlockSpec((count, width), lambda n: (0, 0))
    columns = pl.BlockSpec((width, half_units), lambda n: (0, n))
    units = pl.BlockSpec((1, 2 * count, half_units), lambda n: (n, 0, 0))
    return kernel_call(
        body,
        (2,),
        [whole, whole, columns, columns, pl.BlockSpec((half_units, width), lambda n: (n, 0))],
        [units, units, units, whole, whole],
        [
            jax.ShapeDtypeStruct((2, 2 * count, half_units), F32),
            jax.ShapeDtypeStruct((2, 2 * count, half_units), F32),
            jax.ShapeDtypeStruct((2, 2 * count, half_units), BF16),
            jax.ShapeDtypeStruct((count, width), BF16),
            jax.ShapeDtypeStruct((count, width), BF16),
        ],
        [pltpu.VMEM((2 * count, width), BF16), pltpu.VMEM((2 * count, width), F32)],
    )(*rows, gate_weight, up_weight, down_weight)


def backward(rows_grad, pre_gate, pre_up, gate_weight, up_weight, down_weight):
    count, width = rows_grad[0].shape
    half_units = gate_weight.shape[1] // 2

    def body(a_ref, b_ref, pre_gate_ref, pre_up_ref, gate_ref, up_ref, down_ref, units_ref, out_a, out_b, x_ref, acc_ref):
        step = pl.program_id(0)

        @pl.when(step == 0)
        def _():
            x_ref[:count] = a_ref[...]
            x_ref[count:] = b_ref[...]

        hidden_grad = dot(x_ref[...], down_ref[...], NT)
        pre_gate = pre_gate_ref[0]
        sigma = jax.nn.sigmoid(pre_gate)
        gate_grad = (
            hidden_grad * pre_up_ref[0] * sigma * (1.0 + pre_gate * (1.0 - sigma))
        ).astype(BF16)
        up_grad = (hidden_grad * (pre_gate * sigma)).astype(BF16)
        units_ref[0, :, :half_units] = gate_grad
        units_ref[0, :, half_units:] = up_grad

        @pl.when(step == 0)
        def _():
            for cut in chunks(width):
                acc_ref[:, cut] = dot(gate_grad, gate_ref[cut], NT) + dot(up_grad, up_ref[cut], NT)

        @pl.when(step == 1)
        def _():
            for cut in chunks(width):
                total = acc_ref[:, cut] + dot(gate_grad, gate_ref[cut], NT)
                total = (total + dot(up_grad, up_ref[cut], NT)).astype(BF16)
                out_a[:, cut] = total[:count]
                out_b[:, cut] = total[count:]

    whole = pl.BlockSpec((count, width), lambda n: (0, 0))
    columns = pl.BlockSpec((width, half_units), lambda n: (0, n))
    units = pl.BlockSpec((1, 2 * count, half_units), lambda n: (n, 0, 0))
    return kernel_call(
        body,
        (2,),
        [whole, whole, units, units, columns, columns, pl.BlockSpec((half_units, width), lambda n: (n, 0))],
        [pl.BlockSpec((1, 2 * count, 2 * half_units), lambda n: (n, 0, 0)), whole, whole],
        [
            jax.ShapeDtypeStruct((2, 2 * count, 2 * half_units), BF16),
            jax.ShapeDtypeStruct((count, width), BF16),
            jax.ShapeDtypeStruct((count, width), BF16),
        ],
        [pltpu.VMEM((2 * count, width), BF16), pltpu.VMEM((2 * count, width), F32)],
    )(*rows_grad, pre_gate, pre_up, gate_weight, up_weight, down_weight)


def down_grad(which, hiddens, rows_grad):
    count, width = rows_grad[0].shape
    half_units = hiddens[0].shape[2]
    tile = tile_of(width)

    def body(which_ref, *refs):
        unit_refs, row_refs, rest = refs[:2], refs[2:6], refs[6:]
        turned_ref = rest[-1]

        @pl.when(pl.program_id(0) == 0)
        def _():
            for n, unit_ref in enumerate(unit_refs):
                turned_ref[:, 2 * n * count : 2 * (n + 1) * count] = unit_ref[0].T

        rows = jnp.concatenate([ref[...] for ref in row_refs], axis=0)
        total = dot(turned_ref[...], rows, NN)
        rest[-2][...] = total.astype(BF16)

    out_spec = pl.BlockSpec((half_units, tile), lambda n, w: (0, n))
    return kernel_call(
        body,
        (width // tile,),
        [pl.BlockSpec((1, 2 * count, half_units), lambda n, w: (w[0], 0, 0))] * 2
        + [pl.BlockSpec((count, tile), lambda n, w: (0, n))] * 4,
        out_spec,
        jax.ShapeDtypeStruct((half_units, width), BF16),
        [pltpu.VMEM((half_units, 4 * count), BF16)],
        scalars=1,
    )(which, *hiddens, *rows_grad)


def gate_up_grad(which, units, rows, mirror_units, mirror_rows):
    count, width = rows[0].shape
    both = units[0].shape[2]
    half_units = both // 2
    tile = tile_of(width)

    def body(which_ref, *refs):
        unit_refs, mirror_refs, row_refs = refs[:2], refs[2:4], refs[4:12]
        gate_ref, up_ref, turned_ref = refs[12:]

        @pl.when(pl.program_id(0) == 0)
        def _():
            for n, factor in enumerate([ref[0] for ref in unit_refs] + [ref[...] for ref in mirror_refs]):
                turned_ref[:, 2 * n * count : 2 * (n + 1) * count] = factor.T

        rows = jnp.concatenate([ref[...] for ref in row_refs], axis=0)
        total = dot(turned_ref[...], rows, NN).astype(BF16).T
        gate_ref[...] = total[:, :half_units]
        up_ref[...] = total[:, half_units:]

    out_spec = pl.BlockSpec((tile, half_units), lambda n, w: (n, 0))
    return kernel_call(
        body,
        (width // tile,),
        [pl.BlockSpec((1, 2 * count, both), lambda n, w: (w[0], 0, 0))] * 2
        + [pl.BlockSpec((2 * count, both), lambda n, w: (0, 0))] * 2
        + [pl.BlockSpec((count, tile), lambda n, w: (0, n))] * 8,
        [out_spec] * 2,
        [jax.ShapeDtypeStruct((width, half_units), BF16)] * 2,
        [pltpu.VMEM((both, 8 * count), BF16)],
        scalars=1,
    )(which, *units, *mirror_units, *rows, *mirror_rows)


def route(meta, half, expert_count, capacity):
    ids, gain = meta[:, :TOPK].astype(jnp.int32), meta[:, TOPK:]
    flat_ids = ids.reshape(MB, TOK_MB * TOPK)
    member = (flat_ids[:, :, None] == jnp.arange(expert_count, dtype=jnp.int32)).astype(jnp.int32)
    running = jnp.cumsum(member, axis=1) - 1
    rank = jnp.sum(member * running, axis=2)
    batch = jnp.arange(MB, dtype=jnp.int32)[:, None]
    near = expert_count // 2
    target = (((flat_ids - half * near) * MB + batch) * capacity + rank).reshape(ids.shape)
    slots = jnp.arange(near * MB * capacity, dtype=jnp.int32)
    matches = (target[:, :, None] == slots).astype(F32)
    turned = (target.T[:, None, :] == slots[:, None]).astype(F32)
    weighting = jnp.sum(matches * gain[:, :, None], axis=1)
    slot_gain = jnp.sum(turned * gain.T[:, None, :], axis=(0, 2))[:, None]
    return jnp.sum(turned, axis=0).astype(BF16), jnp.sum(matches, axis=1).astype(BF16), weighting, slot_gain


def on_device(acts, grad_out, expert_ids, route_weights, w_gate, w_up, w_down):
    weights = (w_gate[0], w_up[0], w_down[0])
    devices = lax.axis_size("expert")
    chips = devices // 2
    near = chips // 2
    capacity = 3 * TOPK * TOK_MB // (2 * chips)
    piece = MB * capacity
    width = acts.shape[2]
    half = (lax.axis_index("expert") >= devices // 2).astype(jnp.int32)
    rank_count = lax.axis_size("pipe")
    kept_half = (lax.axis_index("pipe") >= rank_count // 2).astype(jnp.int32)
    kept = kept_half.reshape(1)

    def hop(rows, distance):
        return lax.ppermute(rows, "expert", [(i, i ^ distance) for i in range(devices)])

    def far(rows):
        return hop(rows, devices // 2)

    def swap(rows):
        return hop(rows, 1)

    def mirror(rows):
        return lax.ppermute(rows, "pipe", [(p, rank_count - 1 - p) for p in range(rank_count)])

    groups = [
        [(part * near + member) * 2 + core for member in range(near)]
        for part in range(2)
        for core in range(2)
    ]

    def near_exchange(rows):
        return lax.all_to_all(
            rows.reshape(near, -1, width),
            "expert",
            split_axis=0,
            concat_axis=0,
            axis_index_groups=groups,
            tiled=True,
        ).reshape(rows.shape)

    def tie(*arrays):
        return lax.optimization_barrier(arrays)

    def expert_sum(mine, other):
        return (mine.astype(F32) + swap(other).astype(F32)).astype(BF16)

    def both(own, other):
        pair = [a.reshape(near, piece, width) for a in (own, other)]
        return jnp.stack(pair, axis=1).reshape(2 * near * piece, width)

    def of_set(matrix, which):
        shaped = matrix.reshape(matrix.shape[0], near, 1, piece)
        pair = [jnp.zeros_like(shaped), shaped] if which else [shaped, jnp.zeros_like(shaped)]
        return jnp.concatenate(pair, axis=2).reshape(matrix.shape[0], 2 * near * piece)

    first = acts.shape[1] // 4
    meta = jnp.concatenate([expert_ids[0].astype(F32), route_weights[0]], axis=1)
    far_meta = far(meta)
    far_acts_0 = far(acts[0, :first])
    own_placing, own_back, own_weighting, own_gain = route(meta, half, chips, capacity)
    own_in = place(own_placing, acts[0])
    own_in, far_acts_0, far_meta, acts_1 = tie(own_in, far_acts_0, far_meta, acts[0, first:])

    far_acts_1 = far(acts_1)
    own_in = near_exchange(own_in)
    far_placing, far_back, far_weighting, far_gain = route(far_meta, half, chips, capacity)
    far_acts_1, own_in, grads = tie(far_acts_1, own_in, grad_out[0])

    far_grads = far(grads)
    far_in = place(far_placing, jnp.concatenate([far_acts_0, far_acts_1], axis=0))
    far_in = near_exchange(far_in)
    own_in_b = swap(own_in)
    mirror_own = mirror(own_in)
    far_grads, far_in, own_in_b, mirror_own = tie(far_grads, far_in, own_in_b, mirror_own)

    all_grads = near_exchange(
        both(place(own_placing, grads, own_gain), place(far_placing, far_grads, far_gain))
    )
    far_in_b = swap(far_in)
    mirror_own_b = swap(mirror_own)
    own_pre_gate, own_pre_up, own_hidden, own_out, own_out_b = forward((own_in, own_in_b), *weights)
    far_pre_gate, far_pre_up, far_hidden, far_out, far_out_b = forward((far_in, far_in_b), *weights)
    all_grads, mirror_own_b, own_out, own_out_b, far_out, far_out_b = tie(
        all_grads, mirror_own_b, own_out, own_out_b, far_out, far_out_b
    )

    own_out = expert_sum(own_out, own_out_b)
    far_out = expert_sum(far_out, far_out_b)
    all_grads = all_grads.reshape(near, 2, piece, width)
    own_grad = all_grads[:, 0].reshape(near * piece, width)
    far_grad = all_grads[:, 1].reshape(near * piece, width)
    own_out, far_out, own_grad, far_grad = tie(own_out, far_out, own_grad, far_grad)

    all_out = near_exchange(both(own_out, far_out))
    far_grad_b = swap(far_grad)
    own_grad_b = swap(own_grad)
    far_units, far_input, far_input_b = backward(
        (far_grad, far_grad_b), far_pre_gate, far_pre_up, *weights
    )
    own_units, own_input, own_input_b = backward(
        (own_grad, own_grad_b), own_pre_gate, own_pre_up, *weights
    )
    all_out, far_units, far_input, far_input_b, own_units, own_input, own_input_b = tie(
        all_out, far_units, far_input, far_input_b, own_units, own_input, own_input_b
    )

    far_input = expert_sum(far_input, far_input_b)
    own_input = expert_sum(own_input, own_input_b)
    far_input, own_input, all_out, far_units, own_units, mirror_far, own_grad_b = tie(
        far_input, own_input, all_out, far_units, own_units, far_in, own_grad_b
    )

    got_out = far(combine(of_set(far_weighting, 1), all_out).astype(BF16))
    far_input = near_exchange(far_input)
    mirror_far = mirror(mirror_far)
    mirror_units = [
        mirror(lax.dynamic_index_in_dim(units, 1 - kept_half, 0, keepdims=False))
        for units in (own_units, far_units)
    ]
    rows_grad = (own_grad, own_grad_b, far_grad, far_grad_b)
    send_down = down_grad(1 - kept, (own_hidden, far_hidden), rows_grad)
    keep_down = down_grad(kept, (own_hidden, far_hidden), rows_grad)
    got_out, far_input, mirror_far, mirror_own_units, mirror_far_units, send_down, keep_down, own_input = tie(
        got_out, far_input, mirror_far, *mirror_units, send_down, keep_down, own_input
    )

    got_input = far(combine(far_back, far_input).astype(BF16))
    own_input = near_exchange(own_input)
    got_down = mirror(send_down)
    mirror_far_b = swap(mirror_far)
    grad_gate, grad_up = gate_up_grad(
        kept,
        (own_units, far_units),
        (own_in, own_in_b, far_in, far_in_b),
        (mirror_own_units, mirror_far_units),
        (mirror_own, mirror_own_b, mirror_far, mirror_far_b),
    )
    out_acts = (combine(of_set(own_weighting, 0), all_out) + got_out.astype(F32)).astype(BF16)
    got_input, own_input, got_down, grad_gate, grad_up, out_acts = tie(
        got_input, own_input, got_down, grad_gate, grad_up, out_acts
    )

    grad_acts = (combine(own_back, own_input) + got_input.astype(F32)).astype(BF16)
    grad_down = (keep_down.astype(F32) + got_down.astype(F32)).astype(BF16)
    return out_acts[None], grad_acts[None], grad_gate[None], grad_up[None], grad_down[None]


def solution(mesh):
    tokens = P("pipe", "expert", None)
    columns = P("pipe", None, "expert")
    return jax.shard_map(
        on_device,
        mesh=mesh,
        in_specs=(tokens, tokens, tokens, tokens, columns, columns, tokens),
        out_specs=(tokens, tokens, columns, columns, tokens),
        check_vma=False,
    )
```

```python
import jax
import jax.numpy as jnp
from jax import lax
from jax.experimental import pallas as pl
from jax.experimental.pallas import tpu as pltpu
from jax.sharding import PartitionSpec as P

TOPK = 2
MB = 2
TOK_MB = 64
F32 = jnp.float32
BF16 = jnp.bfloat16
NN = ((1,), (0,))
NT = ((1,), (1,))
TN = ((0,), (0,))
VMEM_BYTES = 56 * 1024 * 1024


def dot(a, b, dims):
    return lax.dot_general(a, b, (dims, ((), ())), preferred_element_type=F32)


def tile_of(width):
    return 512 if width % 512 == 0 else width


def kernel_call(body, grid, in_specs, out_specs, out_shape, scratch=(), scalars=0):
    return pl.pallas_call(
        body,
        grid_spec=pltpu.PrefetchScalarGridSpec(
            num_scalar_prefetch=scalars,
            grid=grid,
            in_specs=in_specs,
            out_specs=out_specs,
            scratch_shapes=scratch,
        ),
        out_shape=out_shape,
        compiler_params=pltpu.CompilerParams(
            vmem_limit_bytes=VMEM_BYTES, dimension_semantics=("arbitrary",)
        ),
        cost_estimate=pl.CostEstimate(flops=1, bytes_accessed=1, transcendentals=0),
    )


def place(placing, rows, gain=None):
    slots = dot(placing, rows, NN)
    return (slots if gain is None else slots * gain).astype(BF16)


def combine(matrix, rows):
    if matrix.dtype == BF16:
        return dot(matrix, rows, NN)
    return lax.dot_general(
        matrix,
        rows.astype(F32),
        (NN, ((), ())),
        precision=lax.Precision.HIGHEST,
        preferred_element_type=F32,
    )


def chunks(width):
    tile = tile_of(width)
    return [slice(n * tile, (n + 1) * tile) for n in range(width // tile)]


def row_spec(rows, tile):
    if isinstance(rows, tuple):
        array, which = rows
        return pl.BlockSpec(
            (array.shape[0], 1, array.shape[2], tile), lambda n, *w: (0, which, 0, n * (tile < array.shape[3]))
        )
    return pl.BlockSpec((rows.shape[0], tile), lambda n, *w: (0, n * (tile < rows.shape[1])))


def row_array(rows):
    return rows[0] if isinstance(rows, tuple) else rows


def flat(ref):
    value = ref[...]
    return value.reshape(-1, value.shape[-1])


def forward(count, rows, gate_weight, up_weight, down_weight):
    width = gate_weight.shape[0]
    half_units = gate_weight.shape[1] // 2

    def body(a_ref, b_ref, gate_ref, up_ref, down_ref, pre_gate_ref, pre_up_ref, hidden_ref, out_a, out_b, x_ref, acc_ref):
        step = pl.program_id(0)

        @pl.when(step == 0)
        def _():
            x_ref[:count] = flat(a_ref)
            x_ref[count:] = flat(b_ref)

        pre_gate = dot(x_ref[...], gate_ref[...], NN)
        pre_up = dot(x_ref[...], up_ref[...], NN)
        pre_gate_ref[0] = pre_gate
        pre_up_ref[0] = pre_up
        hidden = (pre_gate * jax.nn.sigmoid(pre_gate) * pre_up).astype(BF16)
        hidden_ref[0] = hidden

        @pl.when(step == 0)
        def _():
            for cut in chunks(width):
                acc_ref[:, cut] = dot(hidden, down_ref[:, cut], NN)

        @pl.when(step == 1)
        def _():
            for cut in chunks(width):
                total = (acc_ref[:, cut] + dot(hidden, down_ref[:, cut], NN)).astype(BF16)
                out_a[:, cut] = total[:count]
                out_b[:, cut] = total[count:]

    whole = pl.BlockSpec((count, width), lambda n: (0, 0))
    columns = pl.BlockSpec((width, half_units), lambda n: (0, n))
    units = pl.BlockSpec((1, 2 * count, half_units), lambda n: (n, 0, 0))
    return kernel_call(
        body,
        (2,),
        [row_spec(a, width) for a in rows]
        + [columns, columns, pl.BlockSpec((half_units, width), lambda n: (n, 0))],
        [units, units, units, whole, whole],
        [
            jax.ShapeDtypeStruct((2, 2 * count, half_units), F32),
            jax.ShapeDtypeStruct((2, 2 * count, half_units), F32),
            jax.ShapeDtypeStruct((2, 2 * count, half_units), BF16),
            jax.ShapeDtypeStruct((count, width), BF16),
            jax.ShapeDtypeStruct((count, width), BF16),
        ],
        [pltpu.VMEM((2 * count, width), BF16), pltpu.VMEM((2 * count, width), F32)],
    )(*map(row_array, rows), gate_weight, up_weight, down_weight)


def backward(count, rows_grad, pre_gate, pre_up, gate_weight, up_weight, down_weight):
    width = gate_weight.shape[0]
    half_units = gate_weight.shape[1] // 2

    def body(a_ref, b_ref, pre_gate_ref, pre_up_ref, gate_ref, up_ref, down_ref, units_ref, out_a, out_b, x_ref, acc_ref):
        step = pl.program_id(0)

        @pl.when(step == 0)
        def _():
            x_ref[:count] = flat(a_ref)
            x_ref[count:] = flat(b_ref)

        hidden_grad = dot(x_ref[...], down_ref[...], NT)
        pre_gate = pre_gate_ref[0]
        sigma = jax.nn.sigmoid(pre_gate)
        gate_grad = (
            hidden_grad * pre_up_ref[0] * sigma * (1.0 + pre_gate * (1.0 - sigma))
        ).astype(BF16)
        up_grad = (hidden_grad * (pre_gate * sigma)).astype(BF16)
        units_ref[0, :, :half_units] = gate_grad
        units_ref[0, :, half_units:] = up_grad

        @pl.when(step == 0)
        def _():
            for cut in chunks(width):
                acc_ref[:, cut] = dot(gate_grad, gate_ref[cut], NT) + dot(up_grad, up_ref[cut], NT)

        @pl.when(step == 1)
        def _():
            for cut in chunks(width):
                total = acc_ref[:, cut] + dot(gate_grad, gate_ref[cut], NT)
                total = (total + dot(up_grad, up_ref[cut], NT)).astype(BF16)
                out_a[:, cut] = total[:count]
                out_b[:, cut] = total[count:]

    whole = pl.BlockSpec((count, width), lambda n: (0, 0))
    columns = pl.BlockSpec((width, half_units), lambda n: (0, n))
    units = pl.BlockSpec((1, 2 * count, half_units), lambda n: (n, 0, 0))
    return kernel_call(
        body,
        (2,),
        [row_spec(a, width) for a in rows_grad]
        + [units, units, columns, columns, pl.BlockSpec((half_units, width), lambda n: (n, 0))],
        [pl.BlockSpec((1, 2 * count, 2 * half_units), lambda n: (n, 0, 0)), whole, whole],
        [
            jax.ShapeDtypeStruct((2, 2 * count, 2 * half_units), BF16),
            jax.ShapeDtypeStruct((count, width), BF16),
            jax.ShapeDtypeStruct((count, width), BF16),
        ],
        [pltpu.VMEM((2 * count, width), BF16), pltpu.VMEM((2 * count, width), F32)],
    )(*map(row_array, rows_grad), pre_gate, pre_up, gate_weight, up_weight, down_weight)


def down_grad(count, which, hiddens, rows_grad):
    width = row_array(rows_grad[0]).shape[-1]
    half_units = hiddens[0].shape[2]
    tile = tile_of(width)

    def body(which_ref, *refs):
        unit_refs, row_refs, rest = refs[:2], refs[2:6], refs[6:]
        turned_ref = rest[-1]

        @pl.when(pl.program_id(0) == 0)
        def _():
            for n, unit_ref in enumerate(unit_refs):
                turned_ref[:, 2 * n * count : 2 * (n + 1) * count] = unit_ref[0].T

        rows = jnp.concatenate([flat(ref) for ref in row_refs], axis=0)
        total = dot(turned_ref[...], rows, NN)
        rest[-2][...] = total.astype(BF16)

    out_spec = pl.BlockSpec((half_units, tile), lambda n, w: (0, n))
    return kernel_call(
        body,
        (width // tile,),
        [pl.BlockSpec((1, 2 * count, half_units), lambda n, w: (w[0], 0, 0))] * 2
        + [row_spec(a, tile) for a in rows_grad],
        out_spec,
        jax.ShapeDtypeStruct((half_units, width), BF16),
        [pltpu.VMEM((half_units, 4 * count), BF16)],
        scalars=1,
    )(which, *hiddens, *map(row_array, rows_grad))


def gate_up_grad(count, which, units, rows, mirror_units, mirror_rows):
    width = row_array(rows[0]).shape[-1]
    both = units[0].shape[2]
    half_units = both // 2
    tile = tile_of(width)

    def body(which_ref, *refs):
        unit_refs, mirror_refs, row_refs = refs[:2], refs[2:4], refs[4:12]
        gate_ref, up_ref, turned_ref = refs[12:]

        @pl.when(pl.program_id(0) == 0)
        def _():
            for n, factor in enumerate([ref[0] for ref in unit_refs] + [ref[...] for ref in mirror_refs]):
                turned_ref[:, 2 * n * count : 2 * (n + 1) * count] = factor.T

        rows = jnp.concatenate([flat(ref) for ref in row_refs], axis=0)
        total = dot(turned_ref[...], rows, NN).astype(BF16).T
        gate_ref[...] = total[:, :half_units]
        up_ref[...] = total[:, half_units:]

    out_spec = pl.BlockSpec((tile, half_units), lambda n, w: (n, 0))
    return kernel_call(
        body,
        (width // tile,),
        [pl.BlockSpec((1, 2 * count, both), lambda n, w: (w[0], 0, 0))] * 2
        + [pl.BlockSpec((2 * count, both), lambda n, w: (0, 0))] * 2
        + [row_spec(a, tile) for a in (*rows, *mirror_rows)],
        [out_spec] * 2,
        [jax.ShapeDtypeStruct((width, half_units), BF16)] * 2,
        [pltpu.VMEM((both, 8 * count), BF16)],
        scalars=1,
    )(which, *units, *mirror_units, *map(row_array, (*rows, *mirror_rows)))


def route(meta, half, expert_count, capacity):
    ids, gain = meta[:, :TOPK].astype(jnp.int32), meta[:, TOPK:]
    flat_ids = ids.reshape(MB, TOK_MB * TOPK)
    member = (flat_ids[:, :, None] == jnp.arange(expert_count, dtype=jnp.int32)).astype(jnp.int32)
    running = jnp.cumsum(member, axis=1) - 1
    rank = jnp.sum(member * running, axis=2)
    batch = jnp.arange(MB, dtype=jnp.int32)[:, None]
    near = expert_count // 2
    target = (((flat_ids - half * near) * MB + batch) * capacity + rank).reshape(ids.shape)
    slots = jnp.arange(near * MB * capacity, dtype=jnp.int32)
    matches = (target[:, :, None] == slots).astype(F32)
    turned = (target.T[:, None, :] == slots[:, None]).astype(F32)
    weighting = jnp.sum(matches * gain[:, :, None], axis=1)
    slot_gain = jnp.sum(turned * gain.T[:, None, :], axis=(0, 2))[:, None]
    return jnp.sum(turned, axis=0).astype(BF16), jnp.sum(matches, axis=1).astype(BF16), weighting, slot_gain


def on_device(acts, grad_out, expert_ids, route_weights, w_gate, w_up, w_down):
    weights = (w_gate[0], w_up[0], w_down[0])
    devices = lax.axis_size("expert")
    chips = devices // 2
    near = chips // 2
    capacity = 3 * TOPK * TOK_MB // (2 * chips)
    piece = MB * capacity
    width = acts.shape[2]
    half = (lax.axis_index("expert") >= devices // 2).astype(jnp.int32)
    rank_count = lax.axis_size("pipe")
    kept_half = (lax.axis_index("pipe") >= rank_count // 2).astype(jnp.int32)
    kept = kept_half.reshape(1)

    def hop(rows, distance):
        return lax.ppermute(rows, "expert", [(i, i ^ distance) for i in range(devices)])

    def far(rows):
        return hop(rows, devices // 2)

    def swap(rows):
        return hop(rows, 1)

    def mirror(rows):
        return lax.ppermute(rows, "pipe", [(p, rank_count - 1 - p) for p in range(rank_count)])

    groups = [
        [(part * near + member) * 2 + core for member in range(near)]
        for part in range(2)
        for core in range(2)
    ]

    def near_exchange(rows):
        return lax.all_to_all(
            rows.reshape(near, -1, width),
            "expert",
            split_axis=0,
            concat_axis=0,
            axis_index_groups=groups,
            tiled=True,
        ).reshape(rows.shape)

    def tie(*arrays):
        return lax.optimization_barrier(arrays)

    def expert_sum(mine, other):
        return (mine.astype(F32) + swap(other).astype(F32)).astype(BF16)

    def of_set(matrix, which):
        shaped = matrix.reshape(matrix.shape[0], near, 1, piece)
        pair = [jnp.zeros_like(shaped), shaped] if which else [shaped, jnp.zeros_like(shaped)]
        return jnp.concatenate(pair, axis=2).reshape(matrix.shape[0], 2 * near * piece)

    count = near * piece
    first = acts.shape[1] // 4
    far_acts_0 = far(acts[0, :first])
    meta = jnp.concatenate([expert_ids[0].astype(F32), route_weights[0]], axis=1)
    own_placing, own_back, own_weighting, own_gain = route(meta, half, chips, capacity)
    both_placing = jnp.concatenate([of_set(own_placing.T, 0), of_set(own_placing.T, 1)], axis=0).T
    both_gain = jnp.stack([jnp.ones_like(own_gain).reshape(near, piece), own_gain.reshape(near, piece)], axis=1)
    own = place(
        both_placing, jnp.concatenate([acts[0], grad_out[0]], axis=0), both_gain.reshape(2 * count, 1)
    )
    own, far_acts_0, acts_1, meta = tie(own, far_acts_0, acts[0, first:], meta)

    far_acts_1 = far(acts_1)
    own = near_exchange(own)
    far_meta = far(meta)
    far_placing, far_back, far_weighting, far_gain = route(far_meta, half, chips, capacity)
    far_acts_1, own, far_placing, far_gain, grads = tie(
        far_acts_1, own, far_placing, far_gain, grad_out[0]
    )

    far_grads = far(grads)
    far_in = place(far_placing, jnp.concatenate([far_acts_0, far_acts_1], axis=0))
    far_in = near_exchange(far_in)
    own_b = swap(own)
    own = own.reshape(near, 2, piece, width)
    own_b = own_b.reshape(near, 2, piece, width)
    mirror_own = mirror(own[:, 0].reshape(count, width))
    own_pre_gate, own_pre_up, own_hidden, own_out, own_out_b = forward(
        count, ((own, 0), (own_b, 0)), *weights
    )
    own_units, own_input, own_input_b = backward(
        count, ((own, 1), (own_b, 1)), own_pre_gate, own_pre_up, *weights
    )
    far_grads, far_in, mirror_own, own_out, own_out_b, own_input, own_input_b = tie(
        far_grads, far_in, mirror_own, own_out, own_out_b, own_input, own_input_b
    )

    far_grad = near_exchange(place(far_placing, far_grads, far_gain))
    far_in_b = swap(far_in)
    mirror_far = mirror(far_in)
    own_out = expert_sum(own_out, own_out_b)
    far_pre_gate, far_pre_up, far_hidden, far_out, far_out_b = forward(
        count, (far_in, far_in_b), *weights
    )
    far_grad, far_out, far_out_b, own_out, mirror_far, mirror_own = tie(
        far_grad, far_out, far_out_b, own_out, mirror_far, mirror_own
    )

    far_out = expert_sum(far_out, far_out_b)
    far_out, far_grad, own_input, own_input_b = tie(far_out, far_grad, own_input, own_input_b)

    far_out = near_exchange(far_out)
    far_grad_b = swap(far_grad)
    own_input = expert_sum(own_input, own_input_b)
    far_units, far_input, far_input_b = backward(
        count, (far_grad, far_grad_b), far_pre_gate, far_pre_up, *weights
    )
    far_out, far_units, far_input, far_input_b, own_input = tie(
        far_out, far_units, far_input, far_input_b, own_input
    )

    far_input = expert_sum(far_input, far_input_b)
    back_out = combine(far_weighting, far_out).astype(BF16)
    far_input, back_out, own_units, far_units, far_grad_b, mirror_own, mirror_far = tie(
        far_input, back_out, own_units, far_units, far_grad_b, mirror_own, mirror_far
    )

    got_out = far(back_out)
    back = near_exchange(
        jnp.stack([a.reshape(near, piece, width) for a in (far_input, own_out)], axis=1).reshape(2 * count, width)
    )
    mirror_units = [
        mirror(lax.dynamic_index_in_dim(units, 1 - kept_half, 0, keepdims=False))
        for units in (own_units, far_units)
    ]
    mirror_own_b = swap(mirror_own)
    mirror_far_b = swap(mirror_far)
    rows_grad = ((own, 1), (own_b, 1), far_grad, far_grad_b)
    send_down = down_grad(count, 1 - kept, (own_hidden, far_hidden), rows_grad)
    keep_down = down_grad(count, kept, (own_hidden, far_hidden), rows_grad)
    got_out, back, mirror_own_units, mirror_far_units, mirror_own_b, mirror_far_b, send_down, keep_down, own_input = tie(
        got_out, back, *mirror_units, mirror_own_b, mirror_far_b, send_down, keep_down, own_input
    )

    got_input = far(combine(of_set(far_back, 0), back).astype(BF16))
    own_input = near_exchange(own_input)
    got_down = mirror(send_down)
    grad_gate, grad_up = gate_up_grad(
        count,
        kept,
        (own_units, far_units),
        ((own, 0), (own_b, 0), far_in, far_in_b),
        (mirror_own_units, mirror_far_units),
        (mirror_own, mirror_own_b, mirror_far, mirror_far_b),
    )
    out_acts = (combine(of_set(own_weighting, 1), back) + got_out.astype(F32)).astype(BF16)
    got_input, own_input, got_down, grad_gate, grad_up, out_acts = tie(
        got_input, own_input, got_down, grad_gate, grad_up, out_acts
    )

    grad_acts = (combine(own_back, own_input) + got_input.astype(F32)).astype(BF16)
    grad_down = (keep_down.astype(F32) + got_down.astype(F32)).astype(BF16)
    return out_acts[None], grad_acts[None], grad_gate[None], grad_up[None], grad_down[None]


def solution(mesh):
    tokens = P("pipe", "expert", None)
    columns = P("pipe", None, "expert")
    return jax.shard_map(
        on_device,
        mesh=mesh,
        in_specs=(tokens, tokens, tokens, tokens, columns, columns, tokens),
        out_specs=(tokens, tokens, columns, columns, tokens),
        check_vma=False,
    )
```

```python
import jax
import jax.numpy as jnp
from jax import lax
from jax.experimental import pallas as pl
from jax.experimental.pallas import tpu as pltpu
from jax.sharding import PartitionSpec as P

TOPK = 2
MB = 2
TOK_MB = 64
F32 = jnp.float32
BF16 = jnp.bfloat16
NN = ((1,), (0,))
NT = ((1,), (1,))
TN = ((0,), (0,))
VMEM_BYTES = 56 * 1024 * 1024


def dot(a, b, dims):
    return lax.dot_general(a, b, (dims, ((), ())), preferred_element_type=F32)


def tile_of(width):
    return next((n for n in (512, 256) if width % n == 0), width)


def kernel_call(body, grid, in_specs, out_specs, out_shape, scratch=(), scalars=0, cost=1):
    return pl.pallas_call(
        body,
        grid_spec=pltpu.PrefetchScalarGridSpec(
            num_scalar_prefetch=scalars,
            grid=grid,
            in_specs=in_specs,
            out_specs=out_specs,
            scratch_shapes=scratch,
        ),
        out_shape=out_shape,
        compiler_params=pltpu.CompilerParams(
            vmem_limit_bytes=VMEM_BYTES, dimension_semantics=("arbitrary",)
        ),
        cost_estimate=pl.CostEstimate(flops=1, bytes_accessed=cost, transcendentals=0),
    )


def place(placing, rows, gain=None):
    slots = dot(placing, rows, NN)
    return (slots if gain is None else slots * gain).astype(BF16)


HOP_COST = 22_000_000


def wide_tile(width):
    return width // 2 if width % 256 == 0 else width


def place_far(placing, parts, gain=None):
    slots = placing.shape[0]
    width = parts[0].shape[1]
    tile = wide_tile(width)
    fixed = [placing] if gain is None else [placing, gain]

    def body(placing_ref, *refs):
        part_refs, out_ref = refs[len(fixed) - 1 : -1], refs[-1]
        for cut in chunks(tile):
            rows = [ref[:, cut] for ref in part_refs]
            rows = rows[0] if len(rows) == 1 else jnp.concatenate(rows, axis=0)
            total = dot(placing_ref[...], rows, NN)
            if gain is not None:
                total = total * refs[0][...]
            out_ref[:, cut] = total.astype(BF16)

    return kernel_call(
        body,
        (width // tile,),
        [pl.BlockSpec(a.shape, lambda n: (0, 0)) for a in fixed]
        + [pl.BlockSpec((a.shape[0], tile), lambda n: (0, n)) for a in parts],
        pl.BlockSpec((slots, tile), lambda n: (0, n)),
        jax.ShapeDtypeStruct((slots, width), BF16),
        cost=HOP_COST,
    )(*fixed, *parts)


def combine_got(matrix, rows, got):
    tokens, slots = matrix.shape
    width = rows.shape[1]
    tile = wide_tile(width)

    def body(matrix_ref, rows_ref, got_ref, out_ref):
        for cut in chunks(tile):
            total = dot(matrix_ref[...], rows_ref[:, cut], NN)
            out_ref[:, cut] = (total + got_ref[:, cut].astype(F32)).astype(BF16)

    return kernel_call(
        body,
        (width // tile,),
        [
            pl.BlockSpec((tokens, slots), lambda n: (0, 0)),
            pl.BlockSpec((slots, tile), lambda n: (0, n)),
            pl.BlockSpec((tokens, tile), lambda n: (0, n)),
        ],
        pl.BlockSpec((tokens, tile), lambda n: (0, n)),
        jax.ShapeDtypeStruct((tokens, width), BF16),
        cost=HOP_COST,
    )(matrix, rows, got)


def combine(matrix, rows):
    if matrix.dtype == BF16:
        return dot(matrix, rows, NN)
    return lax.dot_general(
        matrix,
        rows.astype(F32),
        (NN, ((), ())),
        precision=lax.Precision.HIGHEST,
        preferred_element_type=F32,
    )


def chunks(width):
    tile = tile_of(width)
    return [slice(n * tile, (n + 1) * tile) for n in range(width // tile)]


def row_spec(rows, tile):
    if isinstance(rows, tuple):
        array, which = rows
        return pl.BlockSpec(
            (array.shape[0], 1, array.shape[2], tile), lambda n, *w: (0, which, 0, n * (tile < array.shape[3]))
        )
    return pl.BlockSpec((rows.shape[0], tile), lambda n, *w: (0, n * (tile < rows.shape[1])))


def row_array(rows):
    return rows[0] if isinstance(rows, tuple) else rows


def flat(ref):
    value = ref[...]
    return value.reshape(-1, value.shape[-1])


def forward(count, rows, gate_weight, up_weight, down_weight):
    width = gate_weight.shape[0]
    half_units = gate_weight.shape[1] // 2

    def body(a_ref, b_ref, gate_ref, up_ref, down_ref, pre_gate_ref, pre_up_ref, hidden_ref, out_a, out_b, x_ref, acc_ref):
        step = pl.program_id(0)

        @pl.when(step == 0)
        def _():
            x_ref[:count] = flat(a_ref)
            x_ref[count:] = flat(b_ref)

        pre_gate = dot(x_ref[...], gate_ref[...], NN)
        pre_up = dot(x_ref[...], up_ref[...], NN)
        pre_gate_ref[0] = pre_gate
        pre_up_ref[0] = pre_up
        hidden = (pre_gate * jax.nn.sigmoid(pre_gate) * pre_up).astype(BF16)
        hidden_ref[0] = hidden

        @pl.when(step == 0)
        def _():
            for cut in chunks(width):
                acc_ref[:, cut] = dot(hidden, down_ref[:, cut], NN)

        @pl.when(step == 1)
        def _():
            for cut in chunks(width):
                total = (acc_ref[:, cut] + dot(hidden, down_ref[:, cut], NN)).astype(BF16)
                out_a[:, cut] = total[:count]
                out_b[:, cut] = total[count:]

    whole = pl.BlockSpec((count, width), lambda n: (0, 0))
    columns = pl.BlockSpec((width, half_units), lambda n: (0, n))
    units = pl.BlockSpec((1, 2 * count, half_units), lambda n: (n, 0, 0))
    return kernel_call(
        body,
        (2,),
        [row_spec(a, width) for a in rows]
        + [columns, columns, pl.BlockSpec((half_units, width), lambda n: (n, 0))],
        [units, units, units, whole, whole],
        [
            jax.ShapeDtypeStruct((2, 2 * count, half_units), F32),
            jax.ShapeDtypeStruct((2, 2 * count, half_units), F32),
            jax.ShapeDtypeStruct((2, 2 * count, half_units), BF16),
            jax.ShapeDtypeStruct((count, width), BF16),
            jax.ShapeDtypeStruct((count, width), BF16),
        ],
        [pltpu.VMEM((2 * count, width), BF16), pltpu.VMEM((2 * count, width), F32)],
    )(*map(row_array, rows), gate_weight, up_weight, down_weight)


def backward(count, rows_grad, pre_gate, pre_up, gate_weight, up_weight, down_weight):
    width = gate_weight.shape[0]
    half_units = gate_weight.shape[1] // 2

    def body(a_ref, b_ref, pre_gate_ref, pre_up_ref, gate_ref, up_ref, down_ref, units_ref, out_a, out_b, x_ref, acc_ref):
        step = pl.program_id(0)

        @pl.when(step == 0)
        def _():
            x_ref[:count] = flat(a_ref)
            x_ref[count:] = flat(b_ref)

        hidden_grad = dot(x_ref[...], down_ref[...], NT)
        pre_gate = pre_gate_ref[0]
        sigma = jax.nn.sigmoid(pre_gate)
        gate_grad = (
            hidden_grad * pre_up_ref[0] * sigma * (1.0 + pre_gate * (1.0 - sigma))
        ).astype(BF16)
        up_grad = (hidden_grad * (pre_gate * sigma)).astype(BF16)
        units_ref[0, :, :half_units] = gate_grad
        units_ref[0, :, half_units:] = up_grad

        @pl.when(step == 0)
        def _():
            for cut in chunks(width):
                acc_ref[:, cut] = dot(gate_grad, gate_ref[cut], NT) + dot(up_grad, up_ref[cut], NT)

        @pl.when(step == 1)
        def _():
            for cut in chunks(width):
                total = acc_ref[:, cut] + dot(gate_grad, gate_ref[cut], NT)
                total = (total + dot(up_grad, up_ref[cut], NT)).astype(BF16)
                out_a[:, cut] = total[:count]
                out_b[:, cut] = total[count:]

    whole = pl.BlockSpec((count, width), lambda n: (0, 0))
    columns = pl.BlockSpec((width, half_units), lambda n: (0, n))
    units = pl.BlockSpec((1, 2 * count, half_units), lambda n: (n, 0, 0))
    return kernel_call(
        body,
        (2,),
        [row_spec(a, width) for a in rows_grad]
        + [units, units, columns, columns, pl.BlockSpec((half_units, width), lambda n: (n, 0))],
        [pl.BlockSpec((1, 2 * count, 2 * half_units), lambda n: (n, 0, 0)), whole, whole],
        [
            jax.ShapeDtypeStruct((2, 2 * count, 2 * half_units), BF16),
            jax.ShapeDtypeStruct((count, width), BF16),
            jax.ShapeDtypeStruct((count, width), BF16),
        ],
        [pltpu.VMEM((2 * count, width), BF16), pltpu.VMEM((2 * count, width), F32)],
    )(*map(row_array, rows_grad), pre_gate, pre_up, gate_weight, up_weight, down_weight)


def down_grad(count, which, hiddens, rows_grad):
    width = row_array(rows_grad[0]).shape[-1]
    half_units = hiddens[0].shape[2]
    tile = tile_of(width)

    def body(which_ref, *refs):
        unit_refs, row_refs, rest = refs[:2], refs[2:6], refs[6:]
        turned_ref = rest[-1]

        @pl.when(pl.program_id(0) == 0)
        def _():
            for n, unit_ref in enumerate(unit_refs):
                turned_ref[:, 2 * n * count : 2 * (n + 1) * count] = unit_ref[0].T

        rows = jnp.concatenate([flat(ref) for ref in row_refs], axis=0)
        total = dot(turned_ref[...], rows, NN)
        rest[-2][...] = total.astype(BF16)

    out_spec = pl.BlockSpec((half_units, tile), lambda n, w: (0, n))
    return kernel_call(
        body,
        (width // tile,),
        [pl.BlockSpec((1, 2 * count, half_units), lambda n, w: (w[0], 0, 0))] * 2
        + [row_spec(a, tile) for a in rows_grad],
        out_spec,
        jax.ShapeDtypeStruct((half_units, width), BF16),
        [pltpu.VMEM((half_units, 4 * count), BF16)],
        scalars=1,
    )(which, *hiddens, *map(row_array, rows_grad))


def gate_up_grad(count, which, units, rows, mirror_units, mirror_rows):
    width = row_array(rows[0]).shape[-1]
    both = units[0].shape[2]
    half_units = both // 2
    tile = tile_of(width)

    def body(which_ref, *refs):
        unit_refs, mirror_refs, row_refs = refs[:2], refs[2:4], refs[4:12]
        gate_ref, up_ref, turned_ref = refs[12:]

        @pl.when(pl.program_id(0) == 0)
        def _():
            for n, factor in enumerate([ref[0] for ref in unit_refs] + [ref[...] for ref in mirror_refs]):
                turned_ref[:, 2 * n * count : 2 * (n + 1) * count] = factor.T

        rows = jnp.concatenate([flat(ref) for ref in row_refs], axis=0)
        total = dot(turned_ref[...], rows, NN).astype(BF16).T
        gate_ref[...] = total[:, :half_units]
        up_ref[...] = total[:, half_units:]

    out_spec = pl.BlockSpec((tile, half_units), lambda n, w: (n, 0))
    return kernel_call(
        body,
        (width // tile,),
        [pl.BlockSpec((1, 2 * count, both), lambda n, w: (w[0], 0, 0))] * 2
        + [pl.BlockSpec((2 * count, both), lambda n, w: (0, 0))] * 2
        + [row_spec(a, tile) for a in (*rows, *mirror_rows)],
        [out_spec] * 2,
        [jax.ShapeDtypeStruct((width, half_units), BF16)] * 2,
        [pltpu.VMEM((both, 8 * count), BF16)],
        scalars=1,
    )(which, *units, *mirror_units, *map(row_array, (*rows, *mirror_rows)))


def route(meta, half, expert_count, capacity):
    ids, gain = meta[:, :TOPK].astype(jnp.int32), meta[:, TOPK:]
    flat_ids = ids.reshape(MB, TOK_MB * TOPK)
    member = (flat_ids[:, :, None] == jnp.arange(expert_count, dtype=jnp.int32)).astype(jnp.int32)
    running = jnp.cumsum(member, axis=1) - 1
    rank = jnp.sum(member * running, axis=2)
    batch = jnp.arange(MB, dtype=jnp.int32)[:, None]
    near = expert_count // 2
    target = (((flat_ids - half * near) * MB + batch) * capacity + rank).reshape(ids.shape)
    slots = jnp.arange(near * MB * capacity, dtype=jnp.int32)
    matches = (target[:, :, None] == slots).astype(F32)
    turned = (target.T[:, None, :] == slots[:, None]).astype(F32)
    weighting = jnp.sum(matches * gain[:, :, None], axis=1)
    slot_gain = jnp.sum(turned * gain.T[:, None, :], axis=(0, 2))[:, None]
    return jnp.sum(turned, axis=0).astype(BF16), jnp.sum(matches, axis=1).astype(BF16), weighting, slot_gain


def on_device(acts, grad_out, expert_ids, route_weights, w_gate, w_up, w_down):
    weights = (w_gate[0], w_up[0], w_down[0])
    devices = lax.axis_size("expert")
    chips = devices // 2
    near = chips // 2
    capacity = 3 * TOPK * TOK_MB // (2 * chips)
    piece = MB * capacity
    width = acts.shape[2]
    half = (lax.axis_index("expert") >= devices // 2).astype(jnp.int32)
    rank_count = lax.axis_size("pipe")
    kept_half = (lax.axis_index("pipe") >= rank_count // 2).astype(jnp.int32)
    kept = kept_half.reshape(1)

    def hop(rows, distance):
        return lax.ppermute(rows, "expert", [(i, i ^ distance) for i in range(devices)])

    def far(rows):
        return hop(rows, devices // 2)

    def swap(rows):
        return hop(rows, 1)

    def mirror(rows):
        return lax.ppermute(rows, "pipe", [(p, rank_count - 1 - p) for p in range(rank_count)])

    groups = [
        [(part * near + member) * 2 + core for member in range(near)]
        for part in range(2)
        for core in range(2)
    ]

    def near_exchange(rows):
        return lax.all_to_all(
            rows.reshape(near, -1, width),
            "expert",
            split_axis=0,
            concat_axis=0,
            axis_index_groups=groups,
            tiled=True,
        ).reshape(rows.shape)

    def tie(*arrays):
        return lax.optimization_barrier(arrays)

    def expert_sum(mine, other):
        return (mine.astype(F32) + swap(other).astype(F32)).astype(BF16)

    def of_set(matrix, which):
        shaped = matrix.reshape(matrix.shape[0], near, 1, piece)
        pair = [jnp.zeros_like(shaped), shaped] if which else [shaped, jnp.zeros_like(shaped)]
        return jnp.concatenate(pair, axis=2).reshape(matrix.shape[0], 2 * near * piece)

    count = near * piece
    first = acts.shape[1] // 8
    far_acts_0 = far(acts[0, :first])
    meta = jnp.concatenate([expert_ids[0].astype(F32), route_weights[0]], axis=1)
    own_placing, own_back, own_weighting, own_gain = route(meta, half, chips, capacity)
    both_placing = jnp.concatenate([of_set(own_placing.T, 0), of_set(own_placing.T, 1)], axis=0).T
    both_gain = jnp.stack([jnp.ones_like(own_gain).reshape(near, piece), own_gain.reshape(near, piece)], axis=1)
    own = place(
        both_placing, jnp.concatenate([acts[0], grad_out[0]], axis=0), both_gain.reshape(2 * count, 1)
    )
    own, far_acts_0, acts_1, meta = tie(own, far_acts_0, acts[0, first:], meta)

    far_acts_1 = far(acts_1)
    own = near_exchange(own)
    far_meta = far(meta)
    far_placing, far_back, far_weighting, far_gain = route(far_meta, half, chips, capacity)
    far_in = place_far(far_placing, [far_acts_0, far_acts_1])
    far_in, own, far_placing, far_gain, grads = tie(far_in, own, far_placing, far_gain, grad_out[0])

    far_grads = far(grads)
    far_in = near_exchange(far_in)
    own_b = swap(own)
    own = own.reshape(near, 2, piece, width)
    own_b = own_b.reshape(near, 2, piece, width)
    mirror_own = mirror(own[:, 0].reshape(count, width))
    own_pre_gate, own_pre_up, own_hidden, own_out, own_out_b = forward(
        count, ((own, 0), (own_b, 0)), *weights
    )
    own_units, own_input, own_input_b = backward(
        count, ((own, 1), (own_b, 1)), own_pre_gate, own_pre_up, *weights
    )
    far_grads, own_out, own_out_b, own_input, own_input_b = tie(
        far_grads, own_out, own_out_b, own_input, own_input_b
    )
    far_grad = place_far(far_placing, [far_grads], far_gain)
    far_grad, far_in, mirror_own, own_out, own_out_b, own_input, own_input_b = tie(
        far_grad, far_in, mirror_own, own_out, own_out_b, own_input, own_input_b
    )

    far_grad = near_exchange(far_grad)
    far_in_b = swap(far_in)
    mirror_own_b = swap(mirror_own)
    own_out = expert_sum(own_out, own_out_b)
    far_pre_gate, far_pre_up, far_hidden, far_out, far_out_b = forward(
        count, (far_in, far_in_b), *weights
    )
    far_grad, far_out, far_out_b, own_out, mirror_own_b = tie(
        far_grad, far_out, far_out_b, own_out, mirror_own_b
    )

    far_out = expert_sum(far_out, far_out_b)
    far_out, far_grad, own_input, own_input_b = tie(far_out, far_grad, own_input, own_input_b)

    far_out = near_exchange(far_out)
    far_grad_b = swap(far_grad)
    own_input = expert_sum(own_input, own_input_b)
    far_units, far_input, far_input_b = backward(
        count, (far_grad, far_grad_b), far_pre_gate, far_pre_up, *weights
    )
    far_out, far_units, far_input, far_input_b, own_input = tie(
        far_out, far_units, far_input, far_input_b, own_input
    )

    far_input = expert_sum(far_input, far_input_b)
    back_out = combine(far_weighting, far_out).astype(BF16)
    far_input, back_out, own_units, far_units, far_grad_b, mirror_far = tie(
        far_input, back_out, own_units, far_units, far_grad_b, far_in
    )

    got_out = far(back_out)
    back = near_exchange(
        jnp.stack([a.reshape(near, piece, width) for a in (far_input, own_input)], axis=1).reshape(2 * count, width)
    )
    mirror_units = [
        mirror(lax.dynamic_index_in_dim(units, 1 - kept_half, 0, keepdims=False))
        for units in (own_units, far_units)
    ]
    mirror_far = mirror(mirror_far)
    rows_grad = ((own, 1), (own_b, 1), far_grad, far_grad_b)
    send_down = down_grad(count, 1 - kept, (own_hidden, far_hidden), rows_grad)
    keep_down = down_grad(count, kept, (own_hidden, far_hidden), rows_grad)
    got_out, back, mirror_own_units, mirror_far_units, mirror_far, send_down, keep_down, own_out = tie(
        got_out, back, *mirror_units, mirror_far, send_down, keep_down, own_out
    )

    got_input = far(combine(of_set(far_back, 0), back).astype(BF16))
    own_out = near_exchange(own_out)
    got_down = mirror(send_down)
    mirror_far_b = swap(mirror_far)
    grad_gate, grad_up = gate_up_grad(
        count,
        kept,
        (own_units, far_units),
        ((own, 0), (own_b, 0), far_in, far_in_b),
        (mirror_own_units, mirror_far_units),
        (mirror_own, mirror_own_b, mirror_far, mirror_far_b),
    )
    out_acts = (combine(own_weighting, own_out) + got_out.astype(F32)).astype(BF16)
    grad_down = (keep_down.astype(F32) + got_down.astype(F32)).astype(BF16)
    got_input, grad_down, grad_gate, grad_up, out_acts = tie(
        got_input, grad_down, grad_gate, grad_up, out_acts
    )
    grad_acts = combine_got(of_set(own_back, 1), back, got_input)
    return out_acts[None], grad_acts[None], grad_gate[None], grad_up[None], grad_down[None]


def solution(mesh):
    tokens = P("pipe", "expert", None)
    columns = P("pipe", None, "expert")
    return jax.shard_map(
        on_device,
        mesh=mesh,
        in_specs=(tokens, tokens, tokens, tokens, columns, columns, tokens),
        out_specs=(tokens, tokens, columns, columns, tokens),
        check_vma=False,
    )
```

```python
import jax
import jax.numpy as jnp
from jax import lax
from jax.experimental import pallas as pl
from jax.experimental.pallas import tpu as pltpu
from jax.sharding import PartitionSpec as P

TOPK = 2
MB = 2
TOK_MB = 64
F32 = jnp.float32
BF16 = jnp.bfloat16
NN = ((1,), (0,))
NT = ((1,), (1,))
TN = ((0,), (0,))
VMEM_BYTES = 56 * 1024 * 1024


def dot(a, b, dims):
    return lax.dot_general(a, b, (dims, ((), ())), preferred_element_type=F32)


def tile_of(width):
    return next((n for n in (512, 256) if width % n == 0), width)


def kernel_call(body, grid, in_specs, out_specs, out_shape, scratch=(), scalars=0, cost=1):
    return pl.pallas_call(
        body,
        grid_spec=pltpu.PrefetchScalarGridSpec(
            num_scalar_prefetch=scalars,
            grid=grid,
            in_specs=in_specs,
            out_specs=out_specs,
            scratch_shapes=scratch,
        ),
        out_shape=out_shape,
        compiler_params=pltpu.CompilerParams(
            vmem_limit_bytes=VMEM_BYTES, dimension_semantics=("arbitrary",)
        ),
        cost_estimate=pl.CostEstimate(flops=1, bytes_accessed=cost, transcendentals=0),
    )


def place(placing, rows, gain=None):
    slots = dot(placing, rows, NN)
    return (slots if gain is None else slots * gain).astype(BF16)


HOP_COST = 50_000_000


def wide_tile(width):
    return width // 2 if width % 256 == 0 else width


def place_far(placing, parts, gain=None):
    slots = placing.shape[0]
    width = parts[0].shape[1]
    tile = wide_tile(width)
    fixed = [placing] if gain is None else [placing, gain]

    def body(placing_ref, *refs):
        part_refs, out_ref = refs[len(fixed) - 1 : -1], refs[-1]
        for cut in chunks(tile):
            rows = [ref[:, cut] for ref in part_refs]
            rows = rows[0] if len(rows) == 1 else jnp.concatenate(rows, axis=0)
            total = dot(placing_ref[...], rows, NN)
            if gain is not None:
                total = total * refs[0][...]
            out_ref[:, cut] = total.astype(BF16)

    return kernel_call(
        body,
        (width // tile,),
        [pl.BlockSpec(a.shape, lambda n: (0, 0)) for a in fixed]
        + [pl.BlockSpec((a.shape[0], tile), lambda n: (0, n)) for a in parts],
        pl.BlockSpec((slots, tile), lambda n: (0, n)),
        jax.ShapeDtypeStruct((slots, width), BF16),
        cost=HOP_COST,
    )(*fixed, *parts)


def combine_got(matrix, rows, got):
    tokens, slots = matrix.shape
    width = rows.shape[1]
    tile = wide_tile(width)

    def body(matrix_ref, rows_ref, got_ref, out_ref):
        for cut in chunks(tile):
            total = dot(matrix_ref[...], rows_ref[:, cut], NN)
            out_ref[:, cut] = (total + got_ref[:, cut].astype(F32)).astype(BF16)

    return kernel_call(
        body,
        (width // tile,),
        [
            pl.BlockSpec((tokens, slots), lambda n: (0, 0)),
            pl.BlockSpec((slots, tile), lambda n: (0, n)),
            pl.BlockSpec((tokens, tile), lambda n: (0, n)),
        ],
        pl.BlockSpec((tokens, tile), lambda n: (0, n)),
        jax.ShapeDtypeStruct((tokens, width), BF16),
        cost=HOP_COST,
    )(matrix, rows, got)


def combine(matrix, rows):
    if matrix.dtype == BF16:
        return dot(matrix, rows, NN)
    return lax.dot_general(
        matrix,
        rows.astype(F32),
        (NN, ((), ())),
        precision=lax.Precision.HIGHEST,
        preferred_element_type=F32,
    )


def chunks(width):
    tile = tile_of(width)
    return [slice(n * tile, (n + 1) * tile) for n in range(width // tile)]


def row_spec(rows, tile):
    if isinstance(rows, tuple):
        array, which = rows
        return pl.BlockSpec(
            (array.shape[0], 1, array.shape[2], tile), lambda n, *w: (0, which, 0, n * (tile < array.shape[3]))
        )
    return pl.BlockSpec((rows.shape[0], tile), lambda n, *w: (0, n * (tile < rows.shape[1])))


def row_array(rows):
    return rows[0] if isinstance(rows, tuple) else rows


def flat(ref):
    value = ref[...]
    return value.reshape(-1, value.shape[-1])


def forward(count, rows, gate_weight, up_weight, down_weight):
    width = gate_weight.shape[0]
    half_units = gate_weight.shape[1] // 2

    def body(a_ref, b_ref, gate_ref, up_ref, down_ref, pre_gate_ref, pre_up_ref, hidden_ref, out_a, out_b, x_ref, acc_ref):
        step = pl.program_id(0)

        @pl.when(step == 0)
        def _():
            x_ref[:count] = flat(a_ref)
            x_ref[count:] = flat(b_ref)

        pre_gate = dot(x_ref[...], gate_ref[...], NN)
        pre_up = dot(x_ref[...], up_ref[...], NN)
        pre_gate_ref[0] = pre_gate
        pre_up_ref[0] = pre_up
        hidden = (pre_gate * jax.nn.sigmoid(pre_gate) * pre_up).astype(BF16)
        hidden_ref[0] = hidden

        @pl.when(step == 0)
        def _():
            for cut in chunks(width):
                acc_ref[:, cut] = dot(hidden, down_ref[:, cut], NN)

        @pl.when(step == 1)
        def _():
            for cut in chunks(width):
                total = (acc_ref[:, cut] + dot(hidden, down_ref[:, cut], NN)).astype(BF16)
                out_a[:, cut] = total[:count]
                out_b[:, cut] = total[count:]

    whole = pl.BlockSpec((count, width), lambda n: (0, 0))
    columns = pl.BlockSpec((width, half_units), lambda n: (0, n))
    units = pl.BlockSpec((1, 2 * count, half_units), lambda n: (n, 0, 0))
    return kernel_call(
        body,
        (2,),
        [row_spec(a, width) for a in rows]
        + [columns, columns, pl.BlockSpec((half_units, width), lambda n: (n, 0))],
        [units, units, units, whole, whole],
        [
            jax.ShapeDtypeStruct((2, 2 * count, half_units), F32),
            jax.ShapeDtypeStruct((2, 2 * count, half_units), F32),
            jax.ShapeDtypeStruct((2, 2 * count, half_units), BF16),
            jax.ShapeDtypeStruct((count, width), BF16),
            jax.ShapeDtypeStruct((count, width), BF16),
        ],
        [pltpu.VMEM((2 * count, width), BF16), pltpu.VMEM((2 * count, width), F32)],
    )(*map(row_array, rows), gate_weight, up_weight, down_weight)


def backward(count, rows_grad, pre_gate, pre_up, gate_weight, up_weight, down_weight):
    width = gate_weight.shape[0]
    half_units = gate_weight.shape[1] // 2

    def body(a_ref, b_ref, pre_gate_ref, pre_up_ref, gate_ref, up_ref, down_ref, units_ref, out_a, out_b, x_ref, acc_ref):
        step = pl.program_id(0)

        @pl.when(step == 0)
        def _():
            x_ref[:count] = flat(a_ref)
            x_ref[count:] = flat(b_ref)

        hidden_grad = dot(x_ref[...], down_ref[...], NT)
        pre_gate = pre_gate_ref[0]
        sigma = jax.nn.sigmoid(pre_gate)
        gate_grad = (
            hidden_grad * pre_up_ref[0] * sigma * (1.0 + pre_gate * (1.0 - sigma))
        ).astype(BF16)
        up_grad = (hidden_grad * (pre_gate * sigma)).astype(BF16)
        units_ref[0, :, :half_units] = gate_grad
        units_ref[0, :, half_units:] = up_grad

        @pl.when(step == 0)
        def _():
            for cut in chunks(width):
                acc_ref[:, cut] = dot(gate_grad, gate_ref[cut], NT) + dot(up_grad, up_ref[cut], NT)

        @pl.when(step == 1)
        def _():
            for cut in chunks(width):
                total = acc_ref[:, cut] + dot(gate_grad, gate_ref[cut], NT)
                total = (total + dot(up_grad, up_ref[cut], NT)).astype(BF16)
                out_a[:, cut] = total[:count]
                out_b[:, cut] = total[count:]

    whole = pl.BlockSpec((count, width), lambda n: (0, 0))
    columns = pl.BlockSpec((width, half_units), lambda n: (0, n))
    units = pl.BlockSpec((1, 2 * count, half_units), lambda n: (n, 0, 0))
    return kernel_call(
        body,
        (2,),
        [row_spec(a, width) for a in rows_grad]
        + [units, units, columns, columns, pl.BlockSpec((half_units, width), lambda n: (n, 0))],
        [pl.BlockSpec((1, 2 * count, 2 * half_units), lambda n: (n, 0, 0)), whole, whole],
        [
            jax.ShapeDtypeStruct((2, 2 * count, 2 * half_units), BF16),
            jax.ShapeDtypeStruct((count, width), BF16),
            jax.ShapeDtypeStruct((count, width), BF16),
        ],
        [pltpu.VMEM((2 * count, width), BF16), pltpu.VMEM((2 * count, width), F32)],
    )(*map(row_array, rows_grad), pre_gate, pre_up, gate_weight, up_weight, down_weight)


def down_grad(count, which, hiddens, rows_grad):
    width = row_array(rows_grad[0]).shape[-1]
    half_units = hiddens[0].shape[2]
    tile = tile_of(width)

    def body(which_ref, *refs):
        unit_refs, row_refs, rest = refs[:2], refs[2:6], refs[6:]
        turned_ref = rest[-1]

        @pl.when(pl.program_id(0) == 0)
        def _():
            for n, unit_ref in enumerate(unit_refs):
                turned_ref[:, 2 * n * count : 2 * (n + 1) * count] = unit_ref[0].T

        rows = jnp.concatenate([flat(ref) for ref in row_refs], axis=0)
        total = dot(turned_ref[...], rows, NN)
        rest[-2][...] = total.astype(BF16)

    out_spec = pl.BlockSpec((half_units, tile), lambda n, w: (0, n))
    return kernel_call(
        body,
        (width // tile,),
        [pl.BlockSpec((1, 2 * count, half_units), lambda n, w: (w[0], 0, 0))] * 2
        + [row_spec(a, tile) for a in rows_grad],
        out_spec,
        jax.ShapeDtypeStruct((half_units, width), BF16),
        [pltpu.VMEM((half_units, 4 * count), BF16)],
        scalars=1,
    )(which, *hiddens, *map(row_array, rows_grad))


def gate_up_grad(count, which, units, rows, mirror_units, mirror_rows):
    width = row_array(rows[0]).shape[-1]
    both = units[0].shape[2]
    half_units = both // 2
    tile = tile_of(width)

    def body(which_ref, *refs):
        unit_refs, mirror_refs, row_refs = refs[:2], refs[2:4], refs[4:12]
        gate_ref, up_ref, turned_ref = refs[12:]

        @pl.when(pl.program_id(0) == 0)
        def _():
            for n, factor in enumerate([ref[0] for ref in unit_refs] + [ref[...] for ref in mirror_refs]):
                turned_ref[:, 2 * n * count : 2 * (n + 1) * count] = factor.T

        rows = jnp.concatenate([flat(ref) for ref in row_refs], axis=0)
        total = dot(turned_ref[...], rows, NN).astype(BF16).T
        gate_ref[...] = total[:, :half_units]
        up_ref[...] = total[:, half_units:]

    out_spec = pl.BlockSpec((tile, half_units), lambda n, w: (n, 0))
    return kernel_call(
        body,
        (width // tile,),
        [pl.BlockSpec((1, 2 * count, both), lambda n, w: (w[0], 0, 0))] * 2
        + [pl.BlockSpec((2 * count, both), lambda n, w: (0, 0))] * 2
        + [row_spec(a, tile) for a in (*rows, *mirror_rows)],
        [out_spec] * 2,
        [jax.ShapeDtypeStruct((width, half_units), BF16)] * 2,
        [pltpu.VMEM((both, 8 * count), BF16)],
        scalars=1,
    )(which, *units, *mirror_units, *map(row_array, (*rows, *mirror_rows)))


def route(meta, half, expert_count, capacity):
    ids, gain = meta[:, :TOPK].astype(jnp.int32), meta[:, TOPK:]
    flat_ids = ids.reshape(MB, TOK_MB * TOPK)
    member = (flat_ids[:, :, None] == jnp.arange(expert_count, dtype=jnp.int32)).astype(jnp.int32)
    running = jnp.cumsum(member, axis=1) - 1
    rank = jnp.sum(member * running, axis=2)
    batch = jnp.arange(MB, dtype=jnp.int32)[:, None]
    near = expert_count // 2
    target = (((flat_ids - half * near) * MB + batch) * capacity + rank).reshape(ids.shape)
    slots = jnp.arange(near * MB * capacity, dtype=jnp.int32)
    matches = (target[:, :, None] == slots).astype(F32)
    turned = (target.T[:, None, :] == slots[:, None]).astype(F32)
    weighting = jnp.sum(matches * gain[:, :, None], axis=1)
    slot_gain = jnp.sum(turned * gain.T[:, None, :], axis=(0, 2))[:, None]
    return jnp.sum(turned, axis=0).astype(BF16), jnp.sum(matches, axis=1).astype(BF16), weighting, slot_gain


def on_device(acts, grad_out, expert_ids, route_weights, w_gate, w_up, w_down):
    weights = (w_gate[0], w_up[0], w_down[0])
    devices = lax.axis_size("expert")
    chips = devices // 2
    near = chips // 2
    capacity = 3 * TOPK * TOK_MB // (2 * chips)
    piece = MB * capacity
    width = acts.shape[2]
    half = (lax.axis_index("expert") >= devices // 2).astype(jnp.int32)
    rank_count = lax.axis_size("pipe")
    kept_half = (lax.axis_index("pipe") >= rank_count // 2).astype(jnp.int32)
    kept = kept_half.reshape(1)

    def hop(rows, distance):
        return lax.ppermute(rows, "expert", [(i, i ^ distance) for i in range(devices)])

    def far(rows):
        return hop(rows, devices // 2)

    def swap(rows):
        return hop(rows, 1)

    def mirror(rows):
        return lax.ppermute(rows, "pipe", [(p, rank_count - 1 - p) for p in range(rank_count)])

    groups = [
        [(part * near + member) * 2 + core for member in range(near)]
        for part in range(2)
        for core in range(2)
    ]

    def near_exchange(rows):
        return lax.all_to_all(
            rows.reshape(near, -1, width),
            "expert",
            split_axis=0,
            concat_axis=0,
            axis_index_groups=groups,
            tiled=True,
        ).reshape(rows.shape)

    def tie(*arrays):
        return lax.optimization_barrier(arrays)

    def expert_sum(mine, other):
        return (mine.astype(F32) + swap(other).astype(F32)).astype(BF16)

    def of_set(matrix, which):
        shaped = matrix.reshape(matrix.shape[0], near, 1, piece)
        pair = [jnp.zeros_like(shaped), shaped] if which else [shaped, jnp.zeros_like(shaped)]
        return jnp.concatenate(pair, axis=2).reshape(matrix.shape[0], 2 * near * piece)

    count = near * piece
    first = acts.shape[1] // 8
    far_acts_0 = far(acts[0, :first])
    meta = jnp.concatenate([expert_ids[0].astype(F32), route_weights[0]], axis=1)
    own_placing, own_back, own_weighting, own_gain = route(meta, half, chips, capacity)
    both_placing = jnp.concatenate([of_set(own_placing.T, 0), of_set(own_placing.T, 1)], axis=0).T
    both_gain = jnp.stack([jnp.ones_like(own_gain).reshape(near, piece), own_gain.reshape(near, piece)], axis=1)
    own = place(
        both_placing, jnp.concatenate([acts[0], grad_out[0]], axis=0), both_gain.reshape(2 * count, 1)
    )
    own, far_acts_0, acts_1, meta = tie(own, far_acts_0, acts[0, first:], meta)

    far_acts_1 = far(acts_1)
    own = near_exchange(own)
    far_meta = far(meta)
    far_placing, far_back, far_weighting, far_gain = route(far_meta, half, chips, capacity)
    far_in = place_far(far_placing, [far_acts_0, far_acts_1])
    far_in, own, far_placing, far_gain, grads = tie(far_in, own, far_placing, far_gain, grad_out[0])

    far_grads = far(grads)
    far_in = near_exchange(far_in)
    own_b = swap(own)
    own = own.reshape(near, 2, piece, width)
    own_b = own_b.reshape(near, 2, piece, width)
    mirror_own = mirror(own[:, 0].reshape(count, width))
    own_pre_gate, own_pre_up, own_hidden, own_out, own_out_b = forward(
        count, ((own, 0), (own_b, 0)), *weights
    )
    own_units, own_input, own_input_b = backward(
        count, ((own, 1), (own_b, 1)), own_pre_gate, own_pre_up, *weights
    )
    far_grads, own_out, own_out_b, own_input, own_input_b = tie(
        far_grads, own_out, own_out_b, own_input, own_input_b
    )
    far_grad = place_far(far_placing, [far_grads], far_gain)
    far_grad, far_in, mirror_own, own_out, own_out_b, own_input, own_input_b = tie(
        far_grad, far_in, mirror_own, own_out, own_out_b, own_input, own_input_b
    )

    far_grad = near_exchange(far_grad)
    far_in_b = swap(far_in)
    mirror_own_b = swap(mirror_own)
    own_out = expert_sum(own_out, own_out_b)
    far_pre_gate, far_pre_up, far_hidden, far_out, far_out_b = forward(
        count, (far_in, far_in_b), *weights
    )
    far_grad, far_out, far_out_b, own_out, mirror_own_b = tie(
        far_grad, far_out, far_out_b, own_out, mirror_own_b
    )

    far_out = expert_sum(far_out, far_out_b)
    far_out, far_grad, own_input, own_input_b = tie(far_out, far_grad, own_input, own_input_b)

    far_out = near_exchange(far_out)
    far_grad_b = swap(far_grad)
    own_input = expert_sum(own_input, own_input_b)
    far_units, far_input, far_input_b = backward(
        count, (far_grad, far_grad_b), far_pre_gate, far_pre_up, *weights
    )
    far_out, far_units, far_input, far_input_b, own_input = tie(
        far_out, far_units, far_input, far_input_b, own_input
    )

    far_input = expert_sum(far_input, far_input_b)
    back_out = combine(far_weighting, far_out).astype(BF16)
    far_input, back_out, own_units, far_units, far_grad_b, mirror_far = tie(
        far_input, back_out, own_units, far_units, far_grad_b, far_in
    )

    got_out = far(back_out)
    back = near_exchange(
        jnp.stack([a.reshape(near, piece, width) for a in (far_input, own_input)], axis=1).reshape(2 * count, width)
    )
    mirror_units = [
        mirror(lax.dynamic_index_in_dim(units, 1 - kept_half, 0, keepdims=False))
        for units in (own_units, far_units)
    ]
    mirror_far = mirror(mirror_far)
    rows_grad = ((own, 1), (own_b, 1), far_grad, far_grad_b)
    send_down = down_grad(count, 1 - kept, (own_hidden, far_hidden), rows_grad)
    keep_down = down_grad(count, kept, (own_hidden, far_hidden), rows_grad)
    got_out, back, mirror_own_units, mirror_far_units, mirror_far, send_down, keep_down, own_out = tie(
        got_out, back, *mirror_units, mirror_far, send_down, keep_down, own_out
    )

    got_input = far(combine(of_set(far_back, 0), back).astype(BF16))
    own_out = near_exchange(own_out)
    got_down = mirror(send_down)
    mirror_far_b = swap(mirror_far)
    grad_gate, grad_up = gate_up_grad(
        count,
        kept,
        (own_units, far_units),
        ((own, 0), (own_b, 0), far_in, far_in_b),
        (mirror_own_units, mirror_far_units),
        (mirror_own, mirror_own_b, mirror_far, mirror_far_b),
    )
    out_acts = (combine(own_weighting, own_out) + got_out.astype(F32)).astype(BF16)
    grad_down = (keep_down.astype(F32) + got_down.astype(F32)).astype(BF16)
    got_input, grad_down, grad_gate, grad_up, out_acts = tie(
        got_input, grad_down, grad_gate, grad_up, out_acts
    )
    grad_acts = combine_got(of_set(own_back, 1), back, got_input)
    return out_acts[None], grad_acts[None], grad_gate[None], grad_up[None], grad_down[None]


def solution(mesh):
    tokens = P("pipe", "expert", None)
    columns = P("pipe", None, "expert")
    return jax.shard_map(
        on_device,
        mesh=mesh,
        in_specs=(tokens, tokens, tokens, tokens, columns, columns, tokens),
        out_specs=(tokens, tokens, columns, columns, tokens),
        check_vma=False,
    )
```

```python
import jax
import jax.numpy as jnp
from jax import lax
from jax.experimental import pallas as pl
from jax.experimental.pallas import tpu as pltpu
from jax.sharding import PartitionSpec as P

TOPK = 2
MB = 2
TOK_MB = 64
F32 = jnp.float32
BF16 = jnp.bfloat16
NN = ((1,), (0,))
NT = ((1,), (1,))
TN = ((0,), (0,))
VMEM_BYTES = 30 * 1024 * 1024


def dot(a, b, dims):
    return lax.dot_general(a, b, (dims, ((), ())), preferred_element_type=F32)


def tile_of(width):
    return next((n for n in (512, 256) if width % n == 0), width)


def kernel_call(body, grid, in_specs, out_specs, out_shape, scratch=(), scalars=0, cost=1):
    return pl.pallas_call(
        body,
        grid_spec=pltpu.PrefetchScalarGridSpec(
            num_scalar_prefetch=scalars,
            grid=grid,
            in_specs=in_specs,
            out_specs=out_specs,
            scratch_shapes=scratch,
        ),
        out_shape=out_shape,
        compiler_params=pltpu.CompilerParams(
            vmem_limit_bytes=VMEM_BYTES, dimension_semantics=("arbitrary",)
        ),
        cost_estimate=pl.CostEstimate(flops=1, bytes_accessed=cost, transcendentals=0),
    )


def place(placing, rows, gain=None):
    slots = dot(placing, rows, NN)
    return (slots if gain is None else slots * gain).astype(BF16)


HOP_COST = 50_000_000


def wide_tile(width):
    return width // 2 if width % 256 == 0 else width


def place_far(placing, parts, gain=None):
    slots = placing.shape[0]
    width = parts[0].shape[1]
    tile = wide_tile(width)
    fixed = [placing] if gain is None else [placing, gain]

    def body(placing_ref, *refs):
        part_refs, out_ref = refs[len(fixed) - 1 : -1], refs[-1]
        for cut in chunks(tile):
            rows = [ref[:, cut] for ref in part_refs]
            rows = rows[0] if len(rows) == 1 else jnp.concatenate(rows, axis=0)
            total = dot(placing_ref[...], rows, NN)
            if gain is not None:
                total = total * refs[0][...]
            out_ref[:, cut] = total.astype(BF16)

    return kernel_call(
        body,
        (width // tile,),
        [pl.BlockSpec(a.shape, lambda n: (0, 0)) for a in fixed]
        + [pl.BlockSpec((a.shape[0], tile), lambda n: (0, n)) for a in parts],
        pl.BlockSpec((slots, tile), lambda n: (0, n)),
        jax.ShapeDtypeStruct((slots, width), BF16),
        cost=HOP_COST,
    )(*fixed, *parts)


def combine_got(matrix, rows, got):
    tokens, slots = matrix.shape
    width = rows.shape[1]
    tile = wide_tile(width)

    def body(matrix_ref, rows_ref, got_ref, out_ref):
        for cut in chunks(tile):
            total = dot(matrix_ref[...], rows_ref[:, cut], NN)
            out_ref[:, cut] = (total + got_ref[:, cut].astype(F32)).astype(BF16)

    return kernel_call(
        body,
        (width // tile,),
        [
            pl.BlockSpec((tokens, slots), lambda n: (0, 0)),
            pl.BlockSpec((slots, tile), lambda n: (0, n)),
            pl.BlockSpec((tokens, tile), lambda n: (0, n)),
        ],
        pl.BlockSpec((tokens, tile), lambda n: (0, n)),
        jax.ShapeDtypeStruct((tokens, width), BF16),
        cost=HOP_COST,
    )(matrix, rows, got)


def combine(matrix, rows):
    if matrix.dtype == BF16:
        return dot(matrix, rows, NN)
    return lax.dot_general(
        matrix,
        rows.astype(F32),
        (NN, ((), ())),
        precision=lax.Precision.HIGHEST,
        preferred_element_type=F32,
    )


def chunks(width):
    tile = tile_of(width)
    return [slice(n * tile, (n + 1) * tile) for n in range(width // tile)]


def row_spec(rows, tile):
    if isinstance(rows, tuple):
        array, which = rows
        return pl.BlockSpec(
            (array.shape[0], 1, array.shape[2], tile), lambda n, *w: (0, which, 0, n * (tile < array.shape[3]))
        )
    return pl.BlockSpec((rows.shape[0], tile), lambda n, *w: (0, n * (tile < rows.shape[1])))


def row_array(rows):
    return rows[0] if isinstance(rows, tuple) else rows


def flat(ref):
    value = ref[...]
    return value.reshape(-1, value.shape[-1])


def forward(count, rows, gate_weight, up_weight, down_weight):
    width = gate_weight.shape[0]
    half_units = gate_weight.shape[1] // 2

    def body(a_ref, b_ref, gate_ref, up_ref, down_ref, pre_gate_ref, pre_up_ref, hidden_ref, out_a, out_b, x_ref, acc_ref):
        step = pl.program_id(0)

        @pl.when(step == 0)
        def _():
            x_ref[:count] = flat(a_ref)
            x_ref[count:] = flat(b_ref)

        pre_gate = dot(x_ref[...], gate_ref[...], NN)
        pre_up = dot(x_ref[...], up_ref[...], NN)
        pre_gate_ref[0] = pre_gate
        pre_up_ref[0] = pre_up
        hidden = (pre_gate * jax.nn.sigmoid(pre_gate) * pre_up).astype(BF16)
        hidden_ref[0] = hidden

        @pl.when(step == 0)
        def _():
            for cut in chunks(width):
                acc_ref[:, cut] = dot(hidden, down_ref[:, cut], NN)

        @pl.when(step == 1)
        def _():
            for cut in chunks(width):
                total = (acc_ref[:, cut] + dot(hidden, down_ref[:, cut], NN)).astype(BF16)
                out_a[:, cut] = total[:count]
                out_b[:, cut] = total[count:]

    whole = pl.BlockSpec((count, width), lambda n: (0, 0))
    columns = pl.BlockSpec((width, half_units), lambda n: (0, n))
    units = pl.BlockSpec((1, 2 * count, half_units), lambda n: (n, 0, 0))
    return kernel_call(
        body,
        (2,),
        [row_spec(a, width) for a in rows]
        + [columns, columns, pl.BlockSpec((half_units, width), lambda n: (n, 0))],
        [units, units, units, whole, whole],
        [
            jax.ShapeDtypeStruct((2, 2 * count, half_units), F32),
            jax.ShapeDtypeStruct((2, 2 * count, half_units), F32),
            jax.ShapeDtypeStruct((2, 2 * count, half_units), BF16),
            jax.ShapeDtypeStruct((count, width), BF16),
            jax.ShapeDtypeStruct((count, width), BF16),
        ],
        [pltpu.VMEM((2 * count, width), BF16), pltpu.VMEM((2 * count, width), F32)],
    )(*map(row_array, rows), gate_weight, up_weight, down_weight)


def backward(count, rows_grad, pre_gate, pre_up, gate_weight, up_weight, down_weight):
    width = gate_weight.shape[0]
    half_units = gate_weight.shape[1] // 2

    def body(a_ref, b_ref, pre_gate_ref, pre_up_ref, gate_ref, up_ref, down_ref, units_ref, out_a, out_b, x_ref, acc_ref):
        step = pl.program_id(0)

        @pl.when(step == 0)
        def _():
            x_ref[:count] = flat(a_ref)
            x_ref[count:] = flat(b_ref)

        hidden_grad = dot(x_ref[...], down_ref[...], NT)
        pre_gate = pre_gate_ref[0]
        sigma = jax.nn.sigmoid(pre_gate)
        gate_grad = (
            hidden_grad * pre_up_ref[0] * sigma * (1.0 + pre_gate * (1.0 - sigma))
        ).astype(BF16)
        up_grad = (hidden_grad * (pre_gate * sigma)).astype(BF16)
        units_ref[0, :, :half_units] = gate_grad
        units_ref[0, :, half_units:] = up_grad

        @pl.when(step == 0)
        def _():
            for cut in chunks(width):
                acc_ref[:, cut] = dot(gate_grad, gate_ref[cut], NT) + dot(up_grad, up_ref[cut], NT)

        @pl.when(step == 1)
        def _():
            for cut in chunks(width):
                total = acc_ref[:, cut] + dot(gate_grad, gate_ref[cut], NT)
                total = (total + dot(up_grad, up_ref[cut], NT)).astype(BF16)
                out_a[:, cut] = total[:count]
                out_b[:, cut] = total[count:]

    whole = pl.BlockSpec((count, width), lambda n: (0, 0))
    columns = pl.BlockSpec((width, half_units), lambda n: (0, n))
    units = pl.BlockSpec((1, 2 * count, half_units), lambda n: (n, 0, 0))
    return kernel_call(
        body,
        (2,),
        [row_spec(a, width) for a in rows_grad]
        + [units, units, columns, columns, pl.BlockSpec((half_units, width), lambda n: (n, 0))],
        [pl.BlockSpec((1, 2 * count, 2 * half_units), lambda n: (n, 0, 0)), whole, whole],
        [
            jax.ShapeDtypeStruct((2, 2 * count, 2 * half_units), BF16),
            jax.ShapeDtypeStruct((count, width), BF16),
            jax.ShapeDtypeStruct((count, width), BF16),
        ],
        [pltpu.VMEM((2 * count, width), BF16), pltpu.VMEM((2 * count, width), F32)],
    )(*map(row_array, rows_grad), pre_gate, pre_up, gate_weight, up_weight, down_weight)


def down_grad(count, which, hiddens, rows_grad):
    width = row_array(rows_grad[0]).shape[-1]
    half_units = hiddens[0].shape[2]
    tile = tile_of(width)

    def body(which_ref, *refs):
        unit_refs, row_refs, rest = refs[:2], refs[2:6], refs[6:]
        turned_ref = rest[-1]

        @pl.when(pl.program_id(0) == 0)
        def _():
            for n, unit_ref in enumerate(unit_refs):
                turned_ref[:, 2 * n * count : 2 * (n + 1) * count] = unit_ref[0].T

        rows = jnp.concatenate([flat(ref) for ref in row_refs], axis=0)
        total = dot(turned_ref[...], rows, NN)
        rest[-2][...] = total.astype(BF16)

    out_spec = pl.BlockSpec((half_units, tile), lambda n, w: (0, n))
    return kernel_call(
        body,
        (width // tile,),
        [pl.BlockSpec((1, 2 * count, half_units), lambda n, w: (w[0], 0, 0))] * 2
        + [row_spec(a, tile) for a in rows_grad],
        out_spec,
        jax.ShapeDtypeStruct((half_units, width), BF16),
        [pltpu.VMEM((half_units, 4 * count), BF16)],
        scalars=1,
    )(which, *hiddens, *map(row_array, rows_grad))


def gate_up_grad(count, which, units, rows, mirror_units, mirror_rows):
    width = row_array(rows[0]).shape[-1]
    both = units[0].shape[2]
    half_units = both // 2
    tile = tile_of(width)

    def body(which_ref, *refs):
        unit_refs, mirror_refs, row_refs = refs[:2], refs[2:4], refs[4:12]
        gate_ref, up_ref, turned_ref = refs[12:]

        @pl.when(pl.program_id(0) == 0)
        def _():
            for n, factor in enumerate([ref[0] for ref in unit_refs] + [ref[...] for ref in mirror_refs]):
                turned_ref[:, 2 * n * count : 2 * (n + 1) * count] = factor.T

        rows = jnp.concatenate([flat(ref) for ref in row_refs], axis=0)
        total = dot(turned_ref[...], rows, NN).astype(BF16).T
        gate_ref[...] = total[:, :half_units]
        up_ref[...] = total[:, half_units:]

    out_spec = pl.BlockSpec((tile, half_units), lambda n, w: (n, 0))
    return kernel_call(
        body,
        (width // tile,),
        [pl.BlockSpec((1, 2 * count, both), lambda n, w: (w[0], 0, 0))] * 2
        + [pl.BlockSpec((2 * count, both), lambda n, w: (0, 0))] * 2
        + [row_spec(a, tile) for a in (*rows, *mirror_rows)],
        [out_spec] * 2,
        [jax.ShapeDtypeStruct((width, half_units), BF16)] * 2,
        [pltpu.VMEM((both, 8 * count), BF16)],
        scalars=1,
    )(which, *units, *mirror_units, *map(row_array, (*rows, *mirror_rows)))


def route(meta, half, expert_count, capacity):
    ids, gain = meta[:, :TOPK].astype(jnp.int32), meta[:, TOPK:]
    flat_ids = ids.reshape(MB, TOK_MB * TOPK)
    member = (flat_ids[:, :, None] == jnp.arange(expert_count, dtype=jnp.int32)).astype(jnp.int32)
    running = jnp.cumsum(member, axis=1) - 1
    rank = jnp.sum(member * running, axis=2)
    batch = jnp.arange(MB, dtype=jnp.int32)[:, None]
    near = expert_count // 2
    target = (((flat_ids - half * near) * MB + batch) * capacity + rank).reshape(ids.shape)
    slots = jnp.arange(near * MB * capacity, dtype=jnp.int32)
    matches = (target[:, :, None] == slots).astype(F32)
    turned = (target.T[:, None, :] == slots[:, None]).astype(F32)
    weighting = jnp.sum(matches * gain[:, :, None], axis=1)
    slot_gain = jnp.sum(turned * gain.T[:, None, :], axis=(0, 2))[:, None]
    return jnp.sum(turned, axis=0).astype(BF16), jnp.sum(matches, axis=1).astype(BF16), weighting, slot_gain


def on_device(acts, grad_out, expert_ids, route_weights, w_gate, w_up, w_down):
    weights = (w_gate[0], w_up[0], w_down[0])
    devices = lax.axis_size("expert")
    chips = devices // 2
    near = chips // 2
    capacity = 3 * TOPK * TOK_MB // (2 * chips)
    piece = MB * capacity
    width = acts.shape[2]
    half = (lax.axis_index("expert") >= devices // 2).astype(jnp.int32)
    rank_count = lax.axis_size("pipe")
    kept_half = (lax.axis_index("pipe") >= rank_count // 2).astype(jnp.int32)
    kept = kept_half.reshape(1)

    def hop(rows, distance):
        return lax.ppermute(rows, "expert", [(i, i ^ distance) for i in range(devices)])

    def far(rows):
        return hop(rows, devices // 2)

    def swap(rows):
        return hop(rows, 1)

    def mirror(rows):
        return lax.ppermute(rows, "pipe", [(p, rank_count - 1 - p) for p in range(rank_count)])

    groups = [
        [(part * near + member) * 2 + core for member in range(near)]
        for part in range(2)
        for core in range(2)
    ]

    def near_exchange(rows):
        return lax.all_to_all(
            rows.reshape(near, -1, width),
            "expert",
            split_axis=0,
            concat_axis=0,
            axis_index_groups=groups,
            tiled=True,
        ).reshape(rows.shape)

    def tie(*arrays):
        return lax.optimization_barrier(arrays)

    def expert_sum(mine, other):
        return (mine.astype(F32) + swap(other).astype(F32)).astype(BF16)

    def of_set(matrix, which):
        shaped = matrix.reshape(matrix.shape[0], near, 1, piece)
        pair = [jnp.zeros_like(shaped), shaped] if which else [shaped, jnp.zeros_like(shaped)]
        return jnp.concatenate(pair, axis=2).reshape(matrix.shape[0], 2 * near * piece)

    count = near * piece
    meta = jnp.concatenate([expert_ids[0].astype(F32), route_weights[0]], axis=1)
    far_meta = far(meta)
    own_placing, own_back, own_weighting, own_gain = route(meta, half, chips, capacity)
    both_placing = jnp.concatenate([of_set(own_placing.T, 0), of_set(own_placing.T, 1)], axis=0).T
    both_gain = jnp.stack([jnp.ones_like(own_gain).reshape(near, piece), own_gain.reshape(near, piece)], axis=1)
    own = place(
        both_placing, jnp.concatenate([acts[0], grad_out[0]], axis=0), both_gain.reshape(2 * count, 1)
    )
    own, far_meta, tokens = tie(own, far_meta, acts[0])

    far_acts = far(tokens)
    own = near_exchange(own)
    far_placing, far_back, far_weighting, far_gain = route(far_meta, half, chips, capacity)
    own = own.reshape(near, 2, piece, width)
    own_in = own[:, 0].reshape(count, width)
    far_acts, own, own_in, far_placing, far_gain, grads = tie(
        far_acts, own, own_in, far_placing, far_gain, grad_out[0]
    )
    far_in = place_far(far_placing, [far_acts])
    far_in, own, own_in, grads = tie(far_in, own, own_in, grads)

    far_grads = far(grads)
    far_in = near_exchange(far_in)
    own_b = swap(own)
    mirror_own = mirror(own_in)
    own_pre_gate, own_pre_up, own_hidden, own_out, own_out_b = forward(
        count, ((own, 0), (own_b, 0)), *weights
    )
    own_units, own_input, own_input_b = backward(
        count, ((own, 1), (own_b, 1)), own_pre_gate, own_pre_up, *weights
    )
    far_grads, own_out, own_out_b, own_input, own_input_b = tie(
        far_grads, own_out, own_out_b, own_input, own_input_b
    )
    far_grad = place_far(far_placing, [far_grads], far_gain)
    far_grad, far_in, mirror_own, own_out, own_out_b, own_input, own_input_b = tie(
        far_grad, far_in, mirror_own, own_out, own_out_b, own_input, own_input_b
    )

    far_grad = near_exchange(far_grad)
    far_in_b = swap(far_in)
    mirror_own_b = swap(mirror_own)
    own_out = expert_sum(own_out, own_out_b)
    far_pre_gate, far_pre_up, far_hidden, far_out, far_out_b = forward(
        count, (far_in, far_in_b), *weights
    )
    far_grad, far_out, far_out_b, own_out, mirror_own_b = tie(
        far_grad, far_out, far_out_b, own_out, mirror_own_b
    )

    far_out = expert_sum(far_out, far_out_b)
    far_out, far_grad, own_input, own_input_b = tie(far_out, far_grad, own_input, own_input_b)

    far_out = near_exchange(far_out)
    far_grad_b = swap(far_grad)
    own_input = expert_sum(own_input, own_input_b)
    far_units, far_input, far_input_b = backward(
        count, (far_grad, far_grad_b), far_pre_gate, far_pre_up, *weights
    )
    far_out, far_units, far_input, far_input_b, own_input = tie(
        far_out, far_units, far_input, far_input_b, own_input
    )

    far_input = expert_sum(far_input, far_input_b)
    back_out = combine(far_weighting, far_out).astype(BF16)
    far_input, back_out, own_units, far_units, far_grad_b, mirror_far = tie(
        far_input, back_out, own_units, far_units, far_grad_b, far_in
    )

    got_out = far(back_out)
    back = near_exchange(
        jnp.stack([a.reshape(near, piece, width) for a in (far_input, own_input)], axis=1).reshape(2 * count, width)
    )
    mirror_units = [
        mirror(lax.dynamic_index_in_dim(units, 1 - kept_half, 0, keepdims=False))
        for units in (own_units, far_units)
    ]
    mirror_far = mirror(mirror_far)
    rows_grad = ((own, 1), (own_b, 1), far_grad, far_grad_b)
    send_down = down_grad(count, 1 - kept, (own_hidden, far_hidden), rows_grad)
    keep_down = down_grad(count, kept, (own_hidden, far_hidden), rows_grad)
    got_out, back, mirror_own_units, mirror_far_units, mirror_far, send_down, keep_down, own_out = tie(
        got_out, back, *mirror_units, mirror_far, send_down, keep_down, own_out
    )

    got_input = far(combine(of_set(far_back, 0), back).astype(BF16))
    own_out = near_exchange(own_out)
    got_down = mirror(send_down)
    mirror_far_b = swap(mirror_far)
    grad_gate, grad_up = gate_up_grad(
        count,
        kept,
        (own_units, far_units),
        ((own, 0), (own_b, 0), far_in, far_in_b),
        (mirror_own_units, mirror_far_units),
        (mirror_own, mirror_own_b, mirror_far, mirror_far_b),
    )
    out_acts = (combine(own_weighting, own_out) + got_out.astype(F32)).astype(BF16)
    grad_down = (keep_down.astype(F32) + got_down.astype(F32)).astype(BF16)
    got_input, grad_down, grad_gate, grad_up, out_acts = tie(
        got_input, grad_down, grad_gate, grad_up, out_acts
    )
    grad_acts = combine_got(of_set(own_back, 1), back, got_input)
    return out_acts[None], grad_acts[None], grad_gate[None], grad_up[None], grad_down[None]


def solution(mesh):
    tokens = P("pipe", "expert", None)
    columns = P("pipe", None, "expert")
    return jax.shard_map(
        on_device,
        mesh=mesh,
        in_specs=(tokens, tokens, tokens, tokens, columns, columns, tokens),
        out_specs=(tokens, tokens, columns, columns, tokens),
        check_vma=False,
    )
```

```python
import jax
import jax.numpy as jnp
from jax import lax
from jax.experimental import pallas as pl
from jax.experimental.pallas import tpu as pltpu
from jax.sharding import PartitionSpec as P

TOPK = 2
MB = 2
TOK_MB = 64
F32 = jnp.float32
BF16 = jnp.bfloat16
NN = ((1,), (0,))
NT = ((1,), (1,))
TN = ((0,), (0,))
VMEM_BYTES = 56 * 1024 * 1024


def dot(a, b, dims):
    return lax.dot_general(a, b, (dims, ((), ())), preferred_element_type=F32)


def tile_of(width):
    return next((n for n in (512, 256) if width % n == 0), width)


def kernel_call(body, grid, in_specs, out_specs, out_shape, scratch=(), scalars=0, cost=1):
    return pl.pallas_call(
        body,
        grid_spec=pltpu.PrefetchScalarGridSpec(
            num_scalar_prefetch=scalars,
            grid=grid,
            in_specs=in_specs,
            out_specs=out_specs,
            scratch_shapes=scratch,
        ),
        out_shape=out_shape,
        compiler_params=pltpu.CompilerParams(
            vmem_limit_bytes=VMEM_BYTES, dimension_semantics=("arbitrary",)
        ),
        cost_estimate=pl.CostEstimate(flops=1, bytes_accessed=cost, transcendentals=0),
    )


def place(placing, rows, gain=None):
    slots = dot(placing, rows, NN)
    return (slots if gain is None else slots * gain).astype(BF16)


HOP_COST = 22_000_000


def wide_tile(width):
    return width // 2 if width % 256 == 0 else width


def place_far(placing, parts, gain=None):
    slots = placing.shape[0]
    width = parts[0].shape[1]
    tile = wide_tile(width)
    fixed = [placing] if gain is None else [placing, gain]

    def body(placing_ref, *refs):
        part_refs, out_ref = refs[len(fixed) - 1 : -1], refs[-1]
        for cut in chunks(tile):
            rows = [ref[:, cut] for ref in part_refs]
            rows = rows[0] if len(rows) == 1 else jnp.concatenate(rows, axis=0)
            total = dot(placing_ref[...], rows, NN)
            if gain is not None:
                total = total * refs[0][...]
            out_ref[:, cut] = total.astype(BF16)

    return kernel_call(
        body,
        (width // tile,),
        [pl.BlockSpec(a.shape, lambda n: (0, 0)) for a in fixed]
        + [pl.BlockSpec((a.shape[0], tile), lambda n: (0, n)) for a in parts],
        pl.BlockSpec((slots, tile), lambda n: (0, n)),
        jax.ShapeDtypeStruct((slots, width), BF16),
        cost=HOP_COST,
    )(*fixed, *parts)


def combine_got(matrix, rows, got):
    tokens, slots = matrix.shape
    width = rows.shape[1]
    tile = wide_tile(width)

    def body(matrix_ref, rows_ref, got_ref, out_ref):
        for cut in chunks(tile):
            total = dot(matrix_ref[...], rows_ref[:, cut], NN)
            out_ref[:, cut] = (total + got_ref[:, cut].astype(F32)).astype(BF16)

    return kernel_call(
        body,
        (width // tile,),
        [
            pl.BlockSpec((tokens, slots), lambda n: (0, 0)),
            pl.BlockSpec((slots, tile), lambda n: (0, n)),
            pl.BlockSpec((tokens, tile), lambda n: (0, n)),
        ],
        pl.BlockSpec((tokens, tile), lambda n: (0, n)),
        jax.ShapeDtypeStruct((tokens, width), BF16),
        cost=HOP_COST,
    )(matrix, rows, got)


def combine(matrix, rows):
    if matrix.dtype == BF16:
        return dot(matrix, rows, NN)
    return lax.dot_general(
        matrix,
        rows.astype(F32),
        (NN, ((), ())),
        precision=lax.Precision.HIGHEST,
        preferred_element_type=F32,
    )


def chunks(width):
    tile = tile_of(width)
    return [slice(n * tile, (n + 1) * tile) for n in range(width // tile)]


def row_spec(rows, tile):
    if isinstance(rows, tuple):
        array, which = rows
        return pl.BlockSpec(
            (array.shape[0], 1, array.shape[2], tile), lambda n, *w: (0, which, 0, n * (tile < array.shape[3]))
        )
    return pl.BlockSpec((rows.shape[0], tile), lambda n, *w: (0, n * (tile < rows.shape[1])))


def row_array(rows):
    return rows[0] if isinstance(rows, tuple) else rows


def flat(ref):
    value = ref[...]
    return value.reshape(-1, value.shape[-1])


def weight_specs(width, half_units):
    mine, other = (lambda n: jnp.minimum(n, 1)), (lambda n: jnp.maximum(n - 2, 0))
    specs = []
    for at in (mine, other):
        columns = pl.BlockSpec((width, half_units), lambda n, at=at: (0, at(n)))
        specs += [columns, columns, pl.BlockSpec((half_units, width), lambda n, at=at: (at(n), 0))]
    return specs


def forward(count, rows, weights):
    width = weights[0].shape[0]
    half_units = weights[0].shape[1] // 2

    def body(x_ref, *refs):
        pre_gate_ref, pre_up_ref, hidden_ref, out_ref, acc_ref = refs[6:]
        step = pl.program_id(0)

        def quarter(gate_ref, up_ref, down_ref):
            x = flat(x_ref)
            pre_gate = dot(x, gate_ref[...], NN)
            pre_up = dot(x, up_ref[...], NN)
            pre_gate_ref[0] = pre_gate
            pre_up_ref[0] = pre_up
            hidden = (pre_gate * jax.nn.sigmoid(pre_gate) * pre_up).astype(BF16)
            hidden_ref[0] = hidden
            for cut in chunks(width):
                term = dot(hidden, down_ref[:, cut], NN)
                acc_ref[:, cut] = jnp.where(step == 0, term, acc_ref[:, cut] + term)

        pl.when(step < 2)(lambda: quarter(*refs[:3]))
        pl.when(step >= 2)(lambda: quarter(*refs[3:6]))

        @pl.when(step == 3)
        def _():
            out_ref[...] = acc_ref[...].astype(BF16)

    units = pl.BlockSpec((1, count, half_units), lambda n: (n, 0, 0))
    return kernel_call(
        body,
        (4,),
        [row_spec(rows, width)] + weight_specs(width, half_units),
        [units, units, units, pl.BlockSpec((count, width), lambda n: (0, 0))],
        [
            jax.ShapeDtypeStruct((4, count, half_units), F32),
            jax.ShapeDtypeStruct((4, count, half_units), F32),
            jax.ShapeDtypeStruct((4, count, half_units), BF16),
            jax.ShapeDtypeStruct((count, width), BF16),
        ],
        [pltpu.VMEM((count, width), F32)],
    )(row_array(rows), *weights)


def backward(count, rows_grad, pre_gate, pre_up, weights):
    width = weights[0].shape[0]
    half_units = weights[0].shape[1] // 2

    def body(x_ref, pre_gate_ref, pre_up_ref, *refs):
        units_ref, out_ref, acc_ref = refs[6:]
        step = pl.program_id(0)

        def quarter(gate_ref, up_ref, down_ref):
            hidden_grad = dot(flat(x_ref), down_ref[...], NT)
            pre_gate = pre_gate_ref[0]
            sigma = jax.nn.sigmoid(pre_gate)
            gate_grad = (
                hidden_grad * pre_up_ref[0] * sigma * (1.0 + pre_gate * (1.0 - sigma))
            ).astype(BF16)
            up_grad = (hidden_grad * (pre_gate * sigma)).astype(BF16)
            units_ref[0, :, :half_units] = gate_grad
            units_ref[0, :, half_units:] = up_grad
            for cut in chunks(width):
                term = dot(gate_grad, gate_ref[cut], NT) + dot(up_grad, up_ref[cut], NT)
                acc_ref[:, cut] = jnp.where(step == 0, term, acc_ref[:, cut] + term)

        pl.when(step < 2)(lambda: quarter(*refs[:3]))
        pl.when(step >= 2)(lambda: quarter(*refs[3:6]))

        @pl.when(step == 3)
        def _():
            out_ref[...] = acc_ref[...].astype(BF16)

    units = pl.BlockSpec((1, count, half_units), lambda n: (n, 0, 0))
    return kernel_call(
        body,
        (4,),
        [row_spec(rows_grad, width), units, units] + weight_specs(width, half_units),
        [
            pl.BlockSpec((1, count, 2 * half_units), lambda n: (n, 0, 0)),
            pl.BlockSpec((count, width), lambda n: (0, 0)),
        ],
        [
            jax.ShapeDtypeStruct((4, count, 2 * half_units), BF16),
            jax.ShapeDtypeStruct((count, width), BF16),
        ],
        [pltpu.VMEM((count, width), F32)],
    )(row_array(rows_grad), pre_gate, pre_up, *weights)


def down_grad(count, which, hiddens, rows_grad):
    width = row_array(rows_grad[0]).shape[-1]
    half_units = hiddens[0].shape[2]
    tile = tile_of(width)

    def body(which_ref, *refs):
        unit_refs, row_refs, rest = refs[:4], refs[4:8], refs[8:]
        turned_ref = rest[-1]

        @pl.when(pl.program_id(0) == 0)
        def _():
            for n, unit_ref in enumerate(unit_refs):
                turned_ref[:, n * count : (n + 1) * count] = unit_ref[0].T

        rows = jnp.concatenate([flat(ref) for ref in row_refs], axis=0)
        total = dot(turned_ref[...], rows, NN)
        rest[-2][...] = total.astype(BF16)

    out_spec = pl.BlockSpec((half_units, tile), lambda n, w: (0, n))
    return kernel_call(
        body,
        (width // tile,),
        [pl.BlockSpec((1, count, half_units), lambda n, w: (w[0], 0, 0))] * 4
        + [row_spec(a, tile) for a in rows_grad],
        out_spec,
        jax.ShapeDtypeStruct((half_units, width), BF16),
        [pltpu.VMEM((half_units, 4 * count), BF16)],
        scalars=1,
    )(which, *hiddens, *map(row_array, rows_grad))


def gate_up_grad(count, which, units, rows, mirror_units, mirror_rows):
    width = row_array(rows[0]).shape[-1]
    both = units[0].shape[2]
    half_units = both // 2
    tile = tile_of(width)

    def body(which_ref, *refs):
        unit_refs, mirror_refs, row_refs = refs[:4], refs[4:8], refs[8:16]
        gate_ref, up_ref, turned_ref = refs[16:]

        @pl.when(pl.program_id(0) == 0)
        def _():
            for n, factor in enumerate([ref[0] for ref in unit_refs] + [ref[...] for ref in mirror_refs]):
                turned_ref[:, n * count : (n + 1) * count] = factor.T

        rows = jnp.concatenate([flat(ref) for ref in row_refs], axis=0)
        total = dot(turned_ref[...], rows, NN).astype(BF16).T
        gate_ref[...] = total[:, :half_units]
        up_ref[...] = total[:, half_units:]

    out_spec = pl.BlockSpec((tile, half_units), lambda n, w: (n, 0))
    return kernel_call(
        body,
        (width // tile,),
        [pl.BlockSpec((1, count, both), lambda n, w: (w[0], 0, 0))] * 4
        + [pl.BlockSpec((count, both), lambda n, w: (0, 0))] * 4
        + [row_spec(a, tile) for a in (*rows, *mirror_rows)],
        [out_spec] * 2,
        [jax.ShapeDtypeStruct((width, half_units), BF16)] * 2,
        [pltpu.VMEM((both, 8 * count), BF16)],
        scalars=1,
    )(which, *units, *mirror_units, *map(row_array, (*rows, *mirror_rows)))


def route(meta, half, expert_count, capacity):
    ids, gain = meta[:, :TOPK].astype(jnp.int32), meta[:, TOPK:]
    flat_ids = ids.reshape(MB, TOK_MB * TOPK)
    member = (flat_ids[:, :, None] == jnp.arange(expert_count, dtype=jnp.int32)).astype(jnp.int32)
    running = jnp.cumsum(member, axis=1) - 1
    rank = jnp.sum(member * running, axis=2)
    batch = jnp.arange(MB, dtype=jnp.int32)[:, None]
    near = expert_count // 2
    target = (((flat_ids - half * near) * MB + batch) * capacity + rank).reshape(ids.shape)
    slots = jnp.arange(near * MB * capacity, dtype=jnp.int32)
    matches = (target[:, :, None] == slots).astype(F32)
    turned = (target.T[:, None, :] == slots[:, None]).astype(F32)
    weighting = jnp.sum(matches * gain[:, :, None], axis=1)
    slot_gain = jnp.sum(turned * gain.T[:, None, :], axis=(0, 2))[:, None]
    return jnp.sum(turned, axis=0).astype(BF16), jnp.sum(matches, axis=1).astype(BF16), weighting, slot_gain


def on_device(acts, grad_out, expert_ids, route_weights, w_gate, w_up, w_down):
    weights = (w_gate[0], w_up[0], w_down[0])
    devices = lax.axis_size("expert")
    chips = devices // 2
    near = chips // 2
    capacity = 3 * TOPK * TOK_MB // (2 * chips)
    piece = MB * capacity
    width = acts.shape[2]
    half = (lax.axis_index("expert") >= devices // 2).astype(jnp.int32)
    rank_count = lax.axis_size("pipe")
    kept_half = (lax.axis_index("pipe") >= rank_count // 2).astype(jnp.int32)
    kept = kept_half.reshape(1)

    def hop(rows, distance):
        return lax.ppermute(rows, "expert", [(i, i ^ distance) for i in range(devices)])

    def far(rows):
        return hop(rows, devices // 2)

    def swap(rows):
        return hop(rows, 1)

    def mirror(rows):
        return lax.ppermute(rows, "pipe", [(p, rank_count - 1 - p) for p in range(rank_count)])

    groups = [
        [(part * near + member) * 2 + core for member in range(near)]
        for part in range(2)
        for core in range(2)
    ]

    def near_exchange(rows):
        return lax.all_to_all(
            rows.reshape(near, -1, width),
            "expert",
            split_axis=0,
            concat_axis=0,
            axis_index_groups=groups,
            tiled=True,
        ).reshape(rows.shape)

    def tie(*arrays):
        return lax.optimization_barrier(arrays)

    def for_mirror(units):
        return lax.dynamic_index_in_dim(units, 1 - kept_half, 0, keepdims=False)

    def of_set(matrix, which):
        shaped = matrix.reshape(matrix.shape[0], near, 1, piece)
        pair = [jnp.zeros_like(shaped), shaped] if which else [shaped, jnp.zeros_like(shaped)]
        return jnp.concatenate(pair, axis=2).reshape(matrix.shape[0], 2 * near * piece)

    count = near * piece
    first = acts.shape[1] // 8
    far_acts_0 = far(acts[0, :first])
    meta = jnp.concatenate([expert_ids[0].astype(F32), route_weights[0]], axis=1)
    own_placing, own_back, own_weighting, own_gain = route(meta, half, chips, capacity)
    both_placing = jnp.concatenate([of_set(own_placing.T, 0), of_set(own_placing.T, 1)], axis=0).T
    both_gain = jnp.stack([jnp.ones_like(own_gain).reshape(near, piece), own_gain.reshape(near, piece)], axis=1)
    own = place(
        both_placing, jnp.concatenate([acts[0], grad_out[0]], axis=0), both_gain.reshape(2 * count, 1)
    )
    own, far_acts_0, acts_1, meta = tie(own, far_acts_0, acts[0, first:], meta)

    far_acts_1 = far(acts_1)
    own = near_exchange(own).reshape(near, 2, piece, width)
    own_in = own[:, 0].reshape(count, width)
    far_meta = far(meta)
    other = [swap(weight) for weight in weights]
    far_placing, far_back, far_weighting, far_gain = route(far_meta, half, chips, capacity)
    far_in = place_far(far_placing, [far_acts_0, far_acts_1])
    far_in, own, own_in, far_placing, far_gain, grads, *weights = tie(
        far_in, own, own_in, far_placing, far_gain, grad_out[0], *weights, *other
    )

    far_grads = far(grads)
    far_in = near_exchange(far_in)
    own_b = swap(own)
    mirror_own = mirror(own_in)
    own_pre_gate, own_pre_up, own_hidden, own_out = forward(count, (own, 0), weights)
    own_units, own_input = backward(count, (own, 1), own_pre_gate, own_pre_up, weights)
    far_grads, own_out, own_input = tie(far_grads, own_out, own_input)
    far_grad = place_far(far_placing, [far_grads], far_gain)
    far_grad, far_in, own_b, mirror_own, own_out, own_input, own_hidden, own_units = tie(
        far_grad, far_in, own_b, mirror_own, own_out, own_input, own_hidden, own_units
    )

    far_grad = near_exchange(far_grad)
    far_in_b = swap(far_in)
    mirror_own_b = swap(mirror_own)
    own_hidden_b = swap(own_hidden[2:])
    own_units_b = swap(own_units[2:])
    far_pre_gate, far_pre_up, far_hidden, far_out = forward(count, far_in, weights)
    far_grad, far_out, far_in_b, mirror_own_b, own_hidden_b, own_units_b, far_hidden = tie(
        far_grad, far_out, far_in_b, mirror_own_b, own_hidden_b, own_units_b, far_hidden
    )

    far_out = near_exchange(far_out)
    far_grad_b = swap(far_grad)
    far_hidden_b = swap(far_hidden[2:])
    mirror_units = [mirror(for_mirror(units)) for units in (own_units, own_units_b)]
    far_units, far_input = backward(count, far_grad, far_pre_gate, far_pre_up, weights)
    far_out, far_units, far_input, far_grad_b, far_hidden_b, mirror_far, *mirror_units = tie(
        far_out, far_units, far_input, far_grad_b, far_hidden_b, far_in, *mirror_units
    )

    got_out = far(combine(far_weighting, far_out).astype(BF16))
    back = near_exchange(
        jnp.stack([a.reshape(near, piece, width) for a in (far_input, own_input)], axis=1).reshape(2 * count, width)
    )
    mirror_far = mirror(mirror_far)
    mirror_units.append(mirror(for_mirror(far_units)))
    far_units_b = swap(far_units[2:])
    hiddens = (own_hidden, own_hidden_b, far_hidden, far_hidden_b)
    rows_grad = ((own, 1), (own_b.reshape(own.shape), 1), far_grad, far_grad_b)
    send_down = down_grad(count, 1 - kept, hiddens, rows_grad)
    keep_down = down_grad(count, kept, hiddens, rows_grad)
    got_out, back, mirror_far, far_units_b, send_down, keep_down, own_out, *mirror_units = tie(
        got_out, back, mirror_far, far_units_b, send_down, keep_down, own_out, *mirror_units
    )

    got_input = far(combine(of_set(far_back, 0), back).astype(BF16))
    own_out = near_exchange(own_out)
    mirror_units.append(mirror(for_mirror(far_units_b)))
    got_down = mirror(send_down)
    mirror_far_b = swap(mirror_far)
    grad_gate, grad_up = gate_up_grad(
        count,
        kept,
        (own_units, own_units_b, far_units, far_units_b),
        ((own, 0), (own_b.reshape(own.shape), 0), far_in, far_in_b),
        mirror_units,
        (mirror_own, mirror_own_b, mirror_far, mirror_far_b),
    )
    out_acts = (combine(own_weighting, own_out) + got_out.astype(F32)).astype(BF16)
    grad_down = (keep_down.astype(F32) + got_down.astype(F32)).astype(BF16)
    got_input, grad_down, grad_gate, grad_up, out_acts = tie(
        got_input, grad_down, grad_gate, grad_up, out_acts
    )
    grad_acts = combine_got(of_set(own_back, 1), back, got_input)
    return out_acts[None], grad_acts[None], grad_gate[None], grad_up[None], grad_down[None]


def solution(mesh):
    tokens = P("pipe", "expert", None)
    columns = P("pipe", None, "expert")
    return jax.shard_map(
        on_device,
        mesh=mesh,
        in_specs=(tokens, tokens, tokens, tokens, columns, columns, tokens),
        out_specs=(tokens, tokens, columns, columns, tokens),
        check_vma=False,
    )
```

```python
import jax
import jax.numpy as jnp
from jax import lax
from jax.experimental import pallas as pl
from jax.experimental.pallas import tpu as pltpu
from jax.sharding import PartitionSpec as P

TOPK = 2
MB = 2
TOK_MB = 64
F32 = jnp.float32
BF16 = jnp.bfloat16
NN = ((1,), (0,))
NT = ((1,), (1,))
TN = ((0,), (0,))
VMEM_BYTES = 56 * 1024 * 1024


def dot(a, b, dims):
    return lax.dot_general(a, b, (dims, ((), ())), preferred_element_type=F32)


def tile_of(width):
    return next((n for n in (512, 256) if width % n == 0), width)


def kernel_call(body, grid, in_specs, out_specs, out_shape, scratch=(), scalars=0, cost=1):
    return pl.pallas_call(
        body,
        grid_spec=pltpu.PrefetchScalarGridSpec(
            num_scalar_prefetch=scalars,
            grid=grid,
            in_specs=in_specs,
            out_specs=out_specs,
            scratch_shapes=scratch,
        ),
        out_shape=out_shape,
        compiler_params=pltpu.CompilerParams(
            vmem_limit_bytes=VMEM_BYTES, dimension_semantics=("arbitrary",)
        ),
        cost_estimate=pl.CostEstimate(flops=1, bytes_accessed=cost, transcendentals=0),
    )


def place(placing, rows, gain=None):
    slots = dot(placing, rows, NN)
    return (slots if gain is None else slots * gain).astype(BF16)


HOP_COST = 22_000_000


def wide_tile(width):
    return width // 2 if width % 256 == 0 else width


def place_far(placing, parts, gain=None):
    slots = placing.shape[0]
    width = parts[0].shape[1]
    tile = wide_tile(width)
    fixed = [placing] if gain is None else [placing, gain]

    def body(placing_ref, *refs):
        part_refs, out_ref = refs[len(fixed) - 1 : -1], refs[-1]
        for cut in chunks(tile):
            rows = [ref[:, cut] for ref in part_refs]
            rows = rows[0] if len(rows) == 1 else jnp.concatenate(rows, axis=0)
            total = dot(placing_ref[...], rows, NN)
            if gain is not None:
                total = total * refs[0][...]
            out_ref[:, cut] = total.astype(BF16)

    return kernel_call(
        body,
        (width // tile,),
        [pl.BlockSpec(a.shape, lambda n: (0, 0)) for a in fixed]
        + [pl.BlockSpec((a.shape[0], tile), lambda n: (0, n)) for a in parts],
        pl.BlockSpec((slots, tile), lambda n: (0, n)),
        jax.ShapeDtypeStruct((slots, width), BF16),
        cost=HOP_COST,
    )(*fixed, *parts)


def combine_got(matrix, rows, got):
    tokens, slots = matrix.shape
    width = rows.shape[1]
    tile = wide_tile(width)

    def body(matrix_ref, rows_ref, got_ref, out_ref):
        for cut in chunks(tile):
            total = dot(matrix_ref[...], rows_ref[:, cut], NN)
            out_ref[:, cut] = (total + got_ref[:, cut].astype(F32)).astype(BF16)

    return kernel_call(
        body,
        (width // tile,),
        [
            pl.BlockSpec((tokens, slots), lambda n: (0, 0)),
            pl.BlockSpec((slots, tile), lambda n: (0, n)),
            pl.BlockSpec((tokens, tile), lambda n: (0, n)),
        ],
        pl.BlockSpec((tokens, tile), lambda n: (0, n)),
        jax.ShapeDtypeStruct((tokens, width), BF16),
        cost=HOP_COST,
    )(matrix, rows, got)


def combine(matrix, rows):
    if matrix.dtype == BF16:
        return dot(matrix, rows, NN)
    return lax.dot_general(
        matrix,
        rows.astype(F32),
        (NN, ((), ())),
        precision=lax.Precision.HIGHEST,
        preferred_element_type=F32,
    )


def chunks(width):
    tile = tile_of(width)
    return [slice(n * tile, (n + 1) * tile) for n in range(width // tile)]


def row_spec(rows, tile):
    if isinstance(rows, tuple):
        array, which = rows
        return pl.BlockSpec(
            (array.shape[0], 1, array.shape[2], tile), lambda n, *w: (0, which, 0, n * (tile < array.shape[3]))
        )
    return pl.BlockSpec((rows.shape[0], tile), lambda n, *w: (0, n * (tile < rows.shape[1])))


def row_array(rows):
    return rows[0] if isinstance(rows, tuple) else rows


def flat(ref):
    value = ref[...]
    return value.reshape(-1, value.shape[-1])


def weight_specs(width, half_units):
    mine, other = (lambda n: jnp.minimum(n, 1)), (lambda n: jnp.maximum(n - 2, 0))
    specs = []
    for at in (mine, other):
        columns = pl.BlockSpec((width, half_units), lambda n, at=at: (0, at(n)))
        specs += [columns, columns, pl.BlockSpec((half_units, width), lambda n, at=at: (at(n), 0))]
    return specs


def forward(count, rows, weights):
    width = weights[0].shape[0]
    half_units = weights[0].shape[1] // 2

    def body(x_ref, *refs):
        pre_gate_ref, pre_up_ref, hidden_ref, out_ref, acc_ref = refs[6:]
        step = pl.program_id(0)

        def quarter(gate_ref, up_ref, down_ref):
            x = flat(x_ref)
            pre_gate = dot(x, gate_ref[...], NN)
            pre_up = dot(x, up_ref[...], NN)
            pre_gate_ref[0] = pre_gate
            pre_up_ref[0] = pre_up
            hidden = (pre_gate * jax.nn.sigmoid(pre_gate) * pre_up).astype(BF16)
            hidden_ref[0] = hidden
            for cut in chunks(width):
                term = dot(hidden, down_ref[:, cut], NN)
                acc_ref[:, cut] = jnp.where(step == 0, term, acc_ref[:, cut] + term)

        pl.when(step < 2)(lambda: quarter(*refs[:3]))
        pl.when(step >= 2)(lambda: quarter(*refs[3:6]))

        @pl.when(step == 3)
        def _():
            out_ref[...] = acc_ref[...].astype(BF16)

    units = pl.BlockSpec((1, count, half_units), lambda n: (n, 0, 0))
    return kernel_call(
        body,
        (4,),
        [row_spec(rows, width)] + weight_specs(width, half_units),
        [units, units, units, pl.BlockSpec((count, width), lambda n: (0, 0))],
        [
            jax.ShapeDtypeStruct((4, count, half_units), F32),
            jax.ShapeDtypeStruct((4, count, half_units), F32),
            jax.ShapeDtypeStruct((4, count, half_units), BF16),
            jax.ShapeDtypeStruct((count, width), BF16),
        ],
        [pltpu.VMEM((count, width), F32)],
    )(row_array(rows), *weights)


def backward(count, rows_grad, pre_gate, pre_up, weights, beside=None, near=1):
    width = weights[0].shape[0]
    half_units = weights[0].shape[1] // 2

    piece = count // near

    def body(x_ref, pre_gate_ref, pre_up_ref, *refs):
        units_ref, out_ref, acc_ref = refs[-3:]
        step = pl.program_id(0)

        def quarter(gate_ref, up_ref, down_ref):
            hidden_grad = dot(flat(x_ref), down_ref[...], NT)
            pre_gate = pre_gate_ref[0]
            sigma = jax.nn.sigmoid(pre_gate)
            gate_grad = (
                hidden_grad * pre_up_ref[0] * sigma * (1.0 + pre_gate * (1.0 - sigma))
            ).astype(BF16)
            up_grad = (hidden_grad * (pre_gate * sigma)).astype(BF16)
            units_ref[0, :, :half_units] = gate_grad
            units_ref[0, :, half_units:] = up_grad
            for cut in chunks(width):
                term = dot(gate_grad, gate_ref[cut], NT) + dot(up_grad, up_ref[cut], NT)
                acc_ref[:, cut] = jnp.where(step == 0, term, acc_ref[:, cut] + term)

        pl.when(step < 2)(lambda: quarter(*refs[:3]))
        pl.when(step >= 2)(lambda: quarter(*refs[3:6]))

        @pl.when(step == 3)
        def _():
            if beside is None:
                out_ref[...] = acc_ref[...].astype(BF16)
            else:
                for n in range(near):
                    here = slice(n * piece, (n + 1) * piece)
                    out_ref[n, 0] = acc_ref[here].astype(BF16)
                    out_ref[n, 1] = refs[6][here]

    units = pl.BlockSpec((1, count, half_units), lambda n: (n, 0, 0))
    whole = pl.BlockSpec((count, width), lambda n: (0, 0))
    out_spec, out_shape = whole, (count, width)
    if beside is not None:
        out_shape = (near, 2, piece, width)
        out_spec = pl.BlockSpec(out_shape, lambda n: (0, 0, 0, 0))
    return kernel_call(
        body,
        (4,),
        [row_spec(rows_grad, width), units, units]
        + weight_specs(width, half_units)
        + ([] if beside is None else [whole]),
        [
            pl.BlockSpec((1, count, 2 * half_units), lambda n: (n, 0, 0)),
            out_spec,
        ],
        [
            jax.ShapeDtypeStruct((4, count, 2 * half_units), BF16),
            jax.ShapeDtypeStruct(out_shape, BF16),
        ],
        [pltpu.VMEM((count, width), F32)],
    )(row_array(rows_grad), pre_gate, pre_up, *weights, *([] if beside is None else [beside]))


def down_grad(count, which, hiddens, rows_grad):
    width = row_array(rows_grad[0]).shape[-1]
    half_units = hiddens[0].shape[2]
    tile = tile_of(width)

    def body(which_ref, *refs):
        unit_refs, row_refs, rest = refs[:4], refs[4:8], refs[8:]
        turned_ref = rest[-1]

        @pl.when(pl.program_id(0) == 0)
        def _():
            for n, unit_ref in enumerate(unit_refs):
                turned_ref[:, n * count : (n + 1) * count] = unit_ref[0].T

        rows = jnp.concatenate([flat(ref) for ref in row_refs], axis=0)
        total = dot(turned_ref[...], rows, NN)
        rest[-2][...] = total.astype(BF16)

    out_spec = pl.BlockSpec((half_units, tile), lambda n, w: (0, n))
    return kernel_call(
        body,
        (width // tile,),
        [pl.BlockSpec((1, count, half_units), lambda n, w: (w[0], 0, 0))] * 4
        + [row_spec(a, tile) for a in rows_grad],
        out_spec,
        jax.ShapeDtypeStruct((half_units, width), BF16),
        [pltpu.VMEM((half_units, 4 * count), BF16)],
        scalars=1,
    )(which, *hiddens, *map(row_array, rows_grad))


def gate_up_grad(count, which, units, rows, mirror_units, mirror_rows):
    width = row_array(rows[0]).shape[-1]
    both = units[0].shape[2]
    half_units = both // 2
    tile = tile_of(width)

    def body(which_ref, *refs):
        unit_refs, mirror_refs, row_refs = refs[:4], refs[4:8], refs[8:16]
        gate_ref, up_ref, turned_ref = refs[16:]

        @pl.when(pl.program_id(0) == 0)
        def _():
            for n, factor in enumerate([ref[0] for ref in unit_refs] + [ref[...] for ref in mirror_refs]):
                turned_ref[:, n * count : (n + 1) * count] = factor.T

        rows = jnp.concatenate([flat(ref) for ref in row_refs], axis=0)
        total = dot(turned_ref[...], rows, NN).astype(BF16).T
        gate_ref[...] = total[:, :half_units]
        up_ref[...] = total[:, half_units:]

    out_spec = pl.BlockSpec((tile, half_units), lambda n, w: (n, 0))
    return kernel_call(
        body,
        (width // tile,),
        [pl.BlockSpec((1, count, both), lambda n, w: (w[0], 0, 0))] * 4
        + [pl.BlockSpec((count, both), lambda n, w: (0, 0))] * 4
        + [row_spec(a, tile) for a in (*rows, *mirror_rows)],
        [out_spec] * 2,
        [jax.ShapeDtypeStruct((width, half_units), BF16)] * 2,
        [pltpu.VMEM((both, 8 * count), BF16)],
        scalars=1,
    )(which, *units, *mirror_units, *map(row_array, (*rows, *mirror_rows)))


def route(meta, half, expert_count, capacity):
    ids, gain = meta[:, :TOPK].astype(jnp.int32), meta[:, TOPK:]
    flat_ids = ids.reshape(MB, TOK_MB * TOPK)
    member = (flat_ids[:, :, None] == jnp.arange(expert_count, dtype=jnp.int32)).astype(jnp.int32)
    running = jnp.cumsum(member, axis=1) - 1
    rank = jnp.sum(member * running, axis=2)
    batch = jnp.arange(MB, dtype=jnp.int32)[:, None]
    near = expert_count // 2
    target = (((flat_ids - half * near) * MB + batch) * capacity + rank).reshape(ids.shape)
    slots = jnp.arange(near * MB * capacity, dtype=jnp.int32)
    matches = (target[:, :, None] == slots).astype(F32)
    turned = (target.T[:, None, :] == slots[:, None]).astype(F32)
    weighting = jnp.sum(matches * gain[:, :, None], axis=1)
    slot_gain = jnp.sum(turned * gain.T[:, None, :], axis=(0, 2))[:, None]
    return jnp.sum(turned, axis=0).astype(BF16), jnp.sum(matches, axis=1).astype(BF16), weighting, slot_gain


def on_device(acts, grad_out, expert_ids, route_weights, w_gate, w_up, w_down):
    weights = (w_gate[0], w_up[0], w_down[0])
    devices = lax.axis_size("expert")
    chips = devices // 2
    near = chips // 2
    capacity = 3 * TOPK * TOK_MB // (2 * chips)
    piece = MB * capacity
    width = acts.shape[2]
    half = (lax.axis_index("expert") >= devices // 2).astype(jnp.int32)
    rank_count = lax.axis_size("pipe")
    kept_half = (lax.axis_index("pipe") >= rank_count // 2).astype(jnp.int32)
    kept = kept_half.reshape(1)

    def hop(rows, distance):
        return lax.ppermute(rows, "expert", [(i, i ^ distance) for i in range(devices)])

    def far(rows):
        return hop(rows, devices // 2)

    def swap(rows):
        return hop(rows, 1)

    def mirror(rows):
        return lax.ppermute(rows, "pipe", [(p, rank_count - 1 - p) for p in range(rank_count)])

    groups = [
        [(part * near + member) * 2 + core for member in range(near)]
        for part in range(2)
        for core in range(2)
    ]

    def near_exchange(rows):
        return lax.all_to_all(
            rows.reshape(near, -1, width),
            "expert",
            split_axis=0,
            concat_axis=0,
            axis_index_groups=groups,
            tiled=True,
        ).reshape(rows.shape)

    def tie(*arrays):
        return lax.optimization_barrier(arrays)

    def for_mirror(units):
        return lax.dynamic_index_in_dim(units, 1 - kept_half, 0, keepdims=False)

    def of_set(matrix, which):
        shaped = matrix.reshape(matrix.shape[0], near, 1, piece)
        pair = [jnp.zeros_like(shaped), shaped] if which else [shaped, jnp.zeros_like(shaped)]
        return jnp.concatenate(pair, axis=2).reshape(matrix.shape[0], 2 * near * piece)

    count = near * piece
    first = acts.shape[1] // 8
    far_acts_0 = far(acts[0, :first])
    meta = jnp.concatenate([expert_ids[0].astype(F32), route_weights[0]], axis=1)
    own_placing, own_back, own_weighting, own_gain = route(meta, half, chips, capacity)
    both_placing = jnp.concatenate([of_set(own_placing.T, 0), of_set(own_placing.T, 1)], axis=0).T
    both_gain = jnp.stack([jnp.ones_like(own_gain).reshape(near, piece), own_gain.reshape(near, piece)], axis=1)
    own = place(
        both_placing, jnp.concatenate([acts[0], grad_out[0]], axis=0), both_gain.reshape(2 * count, 1)
    )
    own, far_acts_0, acts_1, meta = tie(own, far_acts_0, acts[0, first:], meta)

    far_acts_1 = far(acts_1)
    own = near_exchange(own).reshape(near, 2, piece, width)
    own_in = own[:, 0].reshape(count, width)
    far_meta = far(meta)
    other = [swap(weight) for weight in weights]
    far_placing, far_back, far_weighting, far_gain = route(far_meta, half, chips, capacity)
    far_in = place_far(far_placing, [far_acts_0, far_acts_1])
    far_in, own, own_in, far_placing, far_gain, grads, *weights = tie(
        far_in, own, own_in, far_placing, far_gain, grad_out[0], *weights, *other
    )

    far_grads = far(grads)
    far_in = near_exchange(far_in)
    own_b = swap(own)
    mirror_own = mirror(own_in)
    own_pre_gate, own_pre_up, own_hidden, own_out = forward(count, (own, 0), weights)
    own_units, own_input = backward(count, (own, 1), own_pre_gate, own_pre_up, weights)
    far_grads, own_out, own_input = tie(far_grads, own_out, own_input)
    far_grad = place_far(far_placing, [far_grads], far_gain)
    far_grad, far_in, own_b, mirror_own, own_out, own_input, own_hidden, own_units = tie(
        far_grad, far_in, own_b, mirror_own, own_out, own_input, own_hidden, own_units
    )

    far_grad = near_exchange(far_grad)
    far_in_b = swap(far_in)
    mirror_own_b = swap(mirror_own)
    own_hidden_b = swap(own_hidden[2:])
    own_units_b = swap(own_units[2:])
    far_pre_gate, far_pre_up, far_hidden, far_out = forward(count, far_in, weights)
    far_grad, far_out, far_in_b, mirror_own_b, own_hidden_b, own_units_b, far_hidden = tie(
        far_grad, far_out, far_in_b, mirror_own_b, own_hidden_b, own_units_b, far_hidden
    )

    far_out = near_exchange(far_out)
    far_grad_b = swap(far_grad)
    far_hidden_b = swap(far_hidden[2:])
    far_units, inputs = backward(
        count, far_grad, far_pre_gate, far_pre_up, weights, own_input, near
    )
    far_out, far_units, inputs, far_grad_b, far_hidden_b, mirror_far, own_units, own_units_b = tie(
        far_out, far_units, inputs, far_grad_b, far_hidden_b, far_in, own_units, own_units_b
    )

    got_out = far(combine(far_weighting, far_out).astype(BF16))
    back = near_exchange(inputs.reshape(2 * count, width))
    mirror_far = mirror(mirror_far)
    far_units_b = swap(far_units[2:])
    all_units = (own_units, own_units_b, far_units, far_units_b)
    mirror_units = [
        mirror(jnp.stack([for_mirror(units) for units in all_units[:2]])),
        *[mirror(for_mirror(units)) for units in all_units[2:]],
    ]
    hiddens = (own_hidden, own_hidden_b, far_hidden, far_hidden_b)
    rows_grad = ((own, 1), (own_b.reshape(own.shape), 1), far_grad, far_grad_b)
    send_down = down_grad(count, 1 - kept, hiddens, rows_grad)
    keep_down = down_grad(count, kept, hiddens, rows_grad)
    got_out, back, mirror_far, send_down, keep_down, own_out, *mirror_units = tie(
        got_out, back, mirror_far, send_down, keep_down, own_out, *mirror_units
    )

    got_input = far(combine(of_set(far_back, 0), back).astype(BF16))
    own_out = near_exchange(own_out)
    got_down = mirror(send_down)
    mirror_far_b = swap(mirror_far)
    grad_gate, grad_up = gate_up_grad(
        count,
        kept,
        all_units,
        ((own, 0), (own_b.reshape(own.shape), 0), far_in, far_in_b),
        [mirror_units[0][0], mirror_units[0][1], *mirror_units[1:]],
        (mirror_own, mirror_own_b, mirror_far, mirror_far_b),
    )
    out_acts = (combine(own_weighting, own_out) + got_out.astype(F32)).astype(BF16)
    grad_down = (keep_down.astype(F32) + got_down.astype(F32)).astype(BF16)
    got_input, grad_down, grad_gate, grad_up, out_acts = tie(
        got_input, grad_down, grad_gate, grad_up, out_acts
    )
    grad_acts = combine_got(of_set(own_back, 1), back, got_input)
    return out_acts[None], grad_acts[None], grad_gate[None], grad_up[None], grad_down[None]


def solution(mesh):
    tokens = P("pipe", "expert", None)
    columns = P("pipe", None, "expert")
    return jax.shard_map(
        on_device,
        mesh=mesh,
        in_specs=(tokens, tokens, tokens, tokens, columns, columns, tokens),
        out_specs=(tokens, tokens, columns, columns, tokens),
        check_vma=False,
    )
```

```python
import jax
import jax.numpy as jnp
from jax import lax
from jax.experimental import pallas as pl
from jax.experimental.pallas import tpu as pltpu
from jax.sharding import PartitionSpec as P

TOPK = 2
MB = 2
TOK_MB = 64
F32 = jnp.float32
BF16 = jnp.bfloat16
NN = ((1,), (0,))
NT = ((1,), (1,))
TN = ((0,), (0,))
VMEM_BYTES = 56 * 1024 * 1024


def dot(a, b, dims):
    return lax.dot_general(a, b, (dims, ((), ())), preferred_element_type=F32)


def tile_of(width):
    return next((n for n in (512, 256) if width % n == 0), width)


def kernel_call(body, grid, in_specs, out_specs, out_shape, scratch=(), scalars=0, cost=1):
    return pl.pallas_call(
        body,
        grid_spec=pltpu.PrefetchScalarGridSpec(
            num_scalar_prefetch=scalars,
            grid=grid,
            in_specs=in_specs,
            out_specs=out_specs,
            scratch_shapes=scratch,
        ),
        out_shape=out_shape,
        compiler_params=pltpu.CompilerParams(
            vmem_limit_bytes=VMEM_BYTES, dimension_semantics=("arbitrary",)
        ),
        cost_estimate=pl.CostEstimate(flops=1, bytes_accessed=cost, transcendentals=0),
    )


def place(placing, rows, gain=None):
    slots = dot(placing, rows, NN)
    return (slots if gain is None else slots * gain).astype(BF16)


HOP_COST = 22_000_000


def wide_tile(width):
    return width // 2 if width % 256 == 0 else width


def place_far(placing, parts, gain=None, beside=None, near=1):
    slots = placing.shape[0]
    width = parts[0].shape[1]
    piece = slots // near
    tile = wide_tile(width)
    fixed = [placing] + ([] if gain is None else [gain]) + ([] if beside is None else list(beside[:2]))
    rows = list(parts) + ([] if beside is None else [beside[2]])

    def body(*refs):
        fixed_refs, row_refs, out_ref = refs[: len(fixed)], refs[len(fixed) : -1], refs[-1]
        for cut in chunks(tile):
            tokens = [ref[:, cut] for ref in row_refs[: len(parts)]]
            tokens = tokens[0] if len(tokens) == 1 else jnp.concatenate(tokens, axis=0)
            total = dot(fixed_refs[0][...], tokens, NN)
            if gain is not None:
                total = total * fixed_refs[1][...]
            total = total.astype(BF16)
            if beside is None:
                out_ref[:, cut] = total
            else:
                second = dot(fixed_refs[-2][...], row_refs[-1][:, cut], NN) * fixed_refs[-1][...]
                second = second.astype(BF16)
                for n in range(near):
                    here = slice(n * piece, (n + 1) * piece)
                    out_ref[n, 0, :, cut] = total[here]
                    out_ref[n, 1, :, cut] = second[here]

    out_spec, out_shape = pl.BlockSpec((slots, tile), lambda n: (0, n)), (slots, width)
    if beside is not None:
        out_shape = (near, 2, piece, width)
        out_spec = pl.BlockSpec((near, 2, piece, tile), lambda n: (0, 0, 0, n))
    return kernel_call(
        body,
        (width // tile,),
        [pl.BlockSpec(a.shape, lambda n: (0, 0)) for a in fixed]
        + [pl.BlockSpec((a.shape[0], tile), lambda n: (0, n)) for a in rows],
        out_spec,
        jax.ShapeDtypeStruct(out_shape, BF16),
        cost=HOP_COST,
    )(*fixed, *rows)


def combine_got(matrix, rows, got):
    tokens, slots = matrix.shape
    width = rows.shape[1]
    tile = wide_tile(width)

    def body(matrix_ref, rows_ref, got_ref, out_ref):
        for cut in chunks(tile):
            total = dot(matrix_ref[...], rows_ref[:, cut], NN)
            out_ref[:, cut] = (total + got_ref[:, cut].astype(F32)).astype(BF16)

    return kernel_call(
        body,
        (width // tile,),
        [
            pl.BlockSpec((tokens, slots), lambda n: (0, 0)),
            pl.BlockSpec((slots, tile), lambda n: (0, n)),
            pl.BlockSpec((tokens, tile), lambda n: (0, n)),
        ],
        pl.BlockSpec((tokens, tile), lambda n: (0, n)),
        jax.ShapeDtypeStruct((tokens, width), BF16),
        cost=HOP_COST,
    )(matrix, rows, got)


def combine(matrix, rows):
    if matrix.dtype == BF16:
        return dot(matrix, rows, NN)
    return lax.dot_general(
        matrix,
        rows.astype(F32),
        (NN, ((), ())),
        precision=lax.Precision.HIGHEST,
        preferred_element_type=F32,
    )


def chunks(width):
    tile = tile_of(width)
    return [slice(n * tile, (n + 1) * tile) for n in range(width // tile)]


def row_spec(rows, tile):
    if isinstance(rows, tuple):
        array, which = rows
        return pl.BlockSpec(
            (array.shape[0], 1, array.shape[2], tile), lambda n, *w: (0, which, 0, n * (tile < array.shape[3]))
        )
    return pl.BlockSpec((rows.shape[0], tile), lambda n, *w: (0, n * (tile < rows.shape[1])))


def row_array(rows):
    return rows[0] if isinstance(rows, tuple) else rows


def flat(ref):
    value = ref[...]
    return value.reshape(-1, value.shape[-1])


def weight_specs(width, half_units):
    mine, other = (lambda n: jnp.minimum(n, 1)), (lambda n: jnp.maximum(n - 2, 0))
    specs = []
    for at in (mine, other):
        columns = pl.BlockSpec((width, half_units), lambda n, at=at: (0, at(n)))
        specs += [columns, columns, pl.BlockSpec((half_units, width), lambda n, at=at: (at(n), 0))]
    return specs


def forward(count, rows, weights):
    width = weights[0].shape[0]
    half_units = weights[0].shape[1] // 2

    def body(x_ref, *refs):
        pre_gate_ref, pre_up_ref, hidden_ref, out_ref, acc_ref = refs[6:]
        step = pl.program_id(0)

        def quarter(gate_ref, up_ref, down_ref):
            x = flat(x_ref)
            pre_gate = dot(x, gate_ref[...], NN)
            pre_up = dot(x, up_ref[...], NN)
            pre_gate_ref[0] = pre_gate
            pre_up_ref[0] = pre_up
            hidden = (pre_gate * jax.nn.sigmoid(pre_gate) * pre_up).astype(BF16)
            hidden_ref[0] = hidden
            for cut in chunks(width):
                term = dot(hidden, down_ref[:, cut], NN)
                acc_ref[:, cut] = jnp.where(step == 0, term, acc_ref[:, cut] + term)

        pl.when(step < 2)(lambda: quarter(*refs[:3]))
        pl.when(step >= 2)(lambda: quarter(*refs[3:6]))

        @pl.when(step == 3)
        def _():
            out_ref[...] = acc_ref[...].astype(BF16)

    units = pl.BlockSpec((1, count, half_units), lambda n: (n, 0, 0))
    return kernel_call(
        body,
        (4,),
        [row_spec(rows, width)] + weight_specs(width, half_units),
        [units, units, units, pl.BlockSpec((count, width), lambda n: (0, 0))],
        [
            jax.ShapeDtypeStruct((4, count, half_units), F32),
            jax.ShapeDtypeStruct((4, count, half_units), F32),
            jax.ShapeDtypeStruct((4, count, half_units), BF16),
            jax.ShapeDtypeStruct((count, width), BF16),
        ],
        [pltpu.VMEM((count, width), F32)],
    )(row_array(rows), *weights)


def backward(count, rows_grad, pre_gate, pre_up, weights, beside=None, near=1):
    width = weights[0].shape[0]
    half_units = weights[0].shape[1] // 2

    piece = count // near

    def body(x_ref, pre_gate_ref, pre_up_ref, *refs):
        units_ref, out_ref, acc_ref = refs[-3:]
        step = pl.program_id(0)

        def quarter(gate_ref, up_ref, down_ref):
            hidden_grad = dot(flat(x_ref), down_ref[...], NT)
            pre_gate = pre_gate_ref[0]
            sigma = jax.nn.sigmoid(pre_gate)
            gate_grad = (
                hidden_grad * pre_up_ref[0] * sigma * (1.0 + pre_gate * (1.0 - sigma))
            ).astype(BF16)
            up_grad = (hidden_grad * (pre_gate * sigma)).astype(BF16)
            units_ref[0, :, :half_units] = gate_grad
            units_ref[0, :, half_units:] = up_grad
            for cut in chunks(width):
                term = dot(gate_grad, gate_ref[cut], NT) + dot(up_grad, up_ref[cut], NT)
                acc_ref[:, cut] = jnp.where(step == 0, term, acc_ref[:, cut] + term)

        pl.when(step < 2)(lambda: quarter(*refs[:3]))
        pl.when(step >= 2)(lambda: quarter(*refs[3:6]))

        @pl.when(step == 3)
        def _():
            if beside is None:
                out_ref[...] = acc_ref[...].astype(BF16)
            else:
                for n in range(near):
                    here = slice(n * piece, (n + 1) * piece)
                    out_ref[n, 0] = acc_ref[here].astype(BF16)
                    out_ref[n, 1] = refs[6][here]

    units = pl.BlockSpec((1, count, half_units), lambda n: (n, 0, 0))
    whole = pl.BlockSpec((count, width), lambda n: (0, 0))
    out_spec, out_shape = whole, (count, width)
    if beside is not None:
        out_shape = (near, 2, piece, width)
        out_spec = pl.BlockSpec(out_shape, lambda n: (0, 0, 0, 0))
    return kernel_call(
        body,
        (4,),
        [row_spec(rows_grad, width), units, units]
        + weight_specs(width, half_units)
        + ([] if beside is None else [whole]),
        [
            pl.BlockSpec((1, count, 2 * half_units), lambda n: (n, 0, 0)),
            out_spec,
        ],
        [
            jax.ShapeDtypeStruct((4, count, 2 * half_units), BF16),
            jax.ShapeDtypeStruct(out_shape, BF16),
        ],
        [pltpu.VMEM((count, width), F32)],
    )(row_array(rows_grad), pre_gate, pre_up, *weights, *([] if beside is None else [beside]))


def down_grad(count, which, hiddens, rows_grad):
    width = row_array(rows_grad[0]).shape[-1]
    half_units = hiddens[0].shape[2]
    tile = tile_of(width)

    def body(which_ref, *refs):
        unit_refs, row_refs, rest = refs[:4], refs[4:8], refs[8:]
        turned_ref = rest[-1]

        @pl.when(pl.program_id(0) == 0)
        def _():
            for n, unit_ref in enumerate(unit_refs):
                turned_ref[:, n * count : (n + 1) * count] = unit_ref[0].T

        rows = jnp.concatenate([flat(ref) for ref in row_refs], axis=0)
        total = dot(turned_ref[...], rows, NN)
        rest[-2][...] = total.astype(BF16)

    out_spec = pl.BlockSpec((half_units, tile), lambda n, w: (0, n))
    return kernel_call(
        body,
        (width // tile,),
        [pl.BlockSpec((1, count, half_units), lambda n, w: (w[0], 0, 0))] * 4
        + [row_spec(a, tile) for a in rows_grad],
        out_spec,
        jax.ShapeDtypeStruct((half_units, width), BF16),
        [pltpu.VMEM((half_units, 4 * count), BF16)],
        scalars=1,
    )(which, *hiddens, *map(row_array, rows_grad))


def gate_up_grad(count, which, units, rows, mirror_units, mirror_rows):
    width = row_array(rows[0]).shape[-1]
    both = units[0].shape[2]
    half_units = both // 2
    tile = tile_of(width)

    def body(which_ref, *refs):
        unit_refs, mirror_refs, row_refs = refs[:4], refs[4:8], refs[8:16]
        gate_ref, up_ref, turned_ref = refs[16:]

        @pl.when(pl.program_id(0) == 0)
        def _():
            for n, factor in enumerate([ref[0] for ref in unit_refs] + [ref[...] for ref in mirror_refs]):
                turned_ref[:, n * count : (n + 1) * count] = factor.T

        rows = jnp.concatenate([flat(ref) for ref in row_refs], axis=0)
        total = dot(turned_ref[...], rows, NN).astype(BF16).T
        gate_ref[...] = total[:, :half_units]
        up_ref[...] = total[:, half_units:]

    out_spec = pl.BlockSpec((tile, half_units), lambda n, w: (n, 0))
    return kernel_call(
        body,
        (width // tile,),
        [pl.BlockSpec((1, count, both), lambda n, w: (w[0], 0, 0))] * 4
        + [pl.BlockSpec((count, both), lambda n, w: (0, 0))] * 4
        + [row_spec(a, tile) for a in (*rows, *mirror_rows)],
        [out_spec] * 2,
        [jax.ShapeDtypeStruct((width, half_units), BF16)] * 2,
        [pltpu.VMEM((both, 8 * count), BF16)],
        scalars=1,
    )(which, *units, *mirror_units, *map(row_array, (*rows, *mirror_rows)))


def route(meta, half, expert_count, capacity):
    ids, gain = meta[:, :TOPK].astype(jnp.int32), meta[:, TOPK:]
    flat_ids = ids.reshape(MB, TOK_MB * TOPK)
    member = (flat_ids[:, :, None] == jnp.arange(expert_count, dtype=jnp.int32)).astype(jnp.int32)
    running = jnp.cumsum(member, axis=1) - 1
    rank = jnp.sum(member * running, axis=2)
    batch = jnp.arange(MB, dtype=jnp.int32)[:, None]
    near = expert_count // 2
    target = (((flat_ids - half * near) * MB + batch) * capacity + rank).reshape(ids.shape)
    slots = jnp.arange(near * MB * capacity, dtype=jnp.int32)
    matches = (target[:, :, None] == slots).astype(F32)
    turned = (target.T[:, None, :] == slots[:, None]).astype(F32)
    weighting = jnp.sum(matches * gain[:, :, None], axis=1)
    slot_gain = jnp.sum(turned * gain.T[:, None, :], axis=(0, 2))[:, None]
    return jnp.sum(turned, axis=0).astype(BF16), jnp.sum(matches, axis=1).astype(BF16), weighting, slot_gain


def on_device(acts, grad_out, expert_ids, route_weights, w_gate, w_up, w_down):
    weights = (w_gate[0], w_up[0], w_down[0])
    devices = lax.axis_size("expert")
    chips = devices // 2
    near = chips // 2
    capacity = 3 * TOPK * TOK_MB // (2 * chips)
    piece = MB * capacity
    width = acts.shape[2]
    half = (lax.axis_index("expert") >= devices // 2).astype(jnp.int32)
    rank_count = lax.axis_size("pipe")
    kept_half = (lax.axis_index("pipe") >= rank_count // 2).astype(jnp.int32)
    kept = kept_half.reshape(1)

    def hop(rows, distance):
        return lax.ppermute(rows, "expert", [(i, i ^ distance) for i in range(devices)])

    def far(rows):
        return hop(rows, devices // 2)

    def swap(rows):
        return hop(rows, 1)

    def mirror(rows):
        return lax.ppermute(rows, "pipe", [(p, rank_count - 1 - p) for p in range(rank_count)])

    groups = [
        [(part * near + member) * 2 + core for member in range(near)]
        for part in range(2)
        for core in range(2)
    ]

    def near_exchange(rows):
        return lax.all_to_all(
            rows.reshape(near, -1, width),
            "expert",
            split_axis=0,
            concat_axis=0,
            axis_index_groups=groups,
            tiled=True,
        ).reshape(rows.shape)

    def tie(*arrays):
        return lax.optimization_barrier(arrays)

    def for_mirror(units):
        return lax.dynamic_index_in_dim(units, 1 - kept_half, 0, keepdims=False)

    def of_set(matrix, which):
        shaped = matrix.reshape(matrix.shape[0], near, 1, piece)
        pair = [jnp.zeros_like(shaped), shaped] if which else [shaped, jnp.zeros_like(shaped)]
        return jnp.concatenate(pair, axis=2).reshape(matrix.shape[0], 2 * near * piece)

    count = near * piece
    first = acts.shape[1] // 8
    far_acts_0 = far(acts[0, :first])
    meta = jnp.concatenate([expert_ids[0].astype(F32), route_weights[0]], axis=1)
    own_placing, own_back, own_weighting, own_gain = route(meta, half, chips, capacity)
    own_in = place(own_placing, acts[0])
    own_in, far_acts_0, acts_1, meta = tie(own_in, far_acts_0, acts[0, first:], meta)

    far_acts_1 = far(acts_1)
    own_in = near_exchange(own_in)
    far_meta = far(meta)
    other = [swap(weight) for weight in weights]
    far_placing, far_back, far_weighting, far_gain = route(far_meta, half, chips, capacity)
    mixed = place_far(
        far_placing, [far_acts_0, far_acts_1], None, (own_placing, own_gain, grad_out[0]), near
    )
    mixed, own_in, far_placing, far_gain, grads, *weights = tie(
        mixed, own_in, far_placing, far_gain, grad_out[0], *weights, *other
    )

    far_grads = far(grads)
    mixed = near_exchange(mixed.reshape(2 * count, width)).reshape(mixed.shape)
    own_in_b = swap(own_in)
    mirror_own = mirror(own_in)
    own_pre_gate, own_pre_up, own_hidden, own_out = forward(count, own_in, weights)
    far_pre_gate, far_pre_up, far_hidden, far_out = forward(count, (mixed, 0), weights)
    far_grads, own_out, far_out = tie(far_grads, own_out, far_out)
    far_grad = place_far(far_placing, [far_grads], far_gain)
    far_grad, mixed, own_in_b, mirror_own, own_out, far_out, own_hidden, far_hidden = tie(
        far_grad, mixed, own_in_b, mirror_own, own_out, far_out, own_hidden, far_hidden
    )

    far_grad = near_exchange(far_grad)
    mixed_b = swap(mixed)
    mirror_own_b = swap(mirror_own)
    own_hidden_b = swap(own_hidden[2:])
    far_hidden_b = swap(far_hidden[2:])
    far_in = mixed[:, 0].reshape(count, width)
    own_units, own_input = backward(count, (mixed, 1), own_pre_gate, own_pre_up, weights)
    far_grad, far_out, mixed_b, mirror_own_b, own_hidden_b, far_hidden_b, far_in, own_units, own_input = tie(
        far_grad, far_out, mixed_b, mirror_own_b, own_hidden_b, far_hidden_b, far_in, own_units, own_input
    )

    far_out = near_exchange(far_out)
    own_units_b = swap(own_units[2:])
    far_grad_b = swap(far_grad)
    far_units, inputs = backward(
        count, far_grad, far_pre_gate, far_pre_up, weights, own_input, near
    )
    far_out, far_units, inputs, far_grad_b, mirror_far, own_units, own_units_b = tie(
        far_out, far_units, inputs, far_grad_b, far_in, own_units, own_units_b
    )

    got_out = far(combine(far_weighting, far_out).astype(BF16))
    back = near_exchange(inputs.reshape(2 * count, width))
    mirror_far = mirror(mirror_far)
    far_units_b = swap(far_units[2:])
    all_units = (own_units, own_units_b, far_units, far_units_b)
    mirror_units = [
        mirror(jnp.stack([for_mirror(units) for units in all_units[:2]])),
        *[mirror(for_mirror(units)) for units in all_units[2:]],
    ]
    hiddens = (own_hidden, own_hidden_b, far_hidden, far_hidden_b)
    rows_grad = ((mixed, 1), (mixed_b, 1), far_grad, far_grad_b)
    send_down = down_grad(count, 1 - kept, hiddens, rows_grad)
    keep_down = down_grad(count, kept, hiddens, rows_grad)
    got_out, back, mirror_far, send_down, keep_down, own_out, *mirror_units = tie(
        got_out, back, mirror_far, send_down, keep_down, own_out, *mirror_units
    )

    got_input = far(combine(of_set(far_back, 0), back).astype(BF16))
    own_out = near_exchange(own_out)
    got_down = mirror(send_down)
    mirror_far_b = swap(mirror_far)
    grad_gate, grad_up = gate_up_grad(
        count,
        kept,
        all_units,
        (own_in, own_in_b, (mixed, 0), (mixed_b, 0)),
        [mirror_units[0][0], mirror_units[0][1], *mirror_units[1:]],
        (mirror_own, mirror_own_b, mirror_far, mirror_far_b),
    )
    out_acts = (combine(own_weighting, own_out) + got_out.astype(F32)).astype(BF16)
    grad_down = (keep_down.astype(F32) + got_down.astype(F32)).astype(BF16)
    got_input, grad_down, grad_gate, grad_up, out_acts = tie(
        got_input, grad_down, grad_gate, grad_up, out_acts
    )
    grad_acts = combine_got(of_set(own_back, 1), back, got_input)
    return out_acts[None], grad_acts[None], grad_gate[None], grad_up[None], grad_down[None]


def solution(mesh):
    tokens = P("pipe", "expert", None)
    columns = P("pipe", None, "expert")
    return jax.shard_map(
        on_device,
        mesh=mesh,
        in_specs=(tokens, tokens, tokens, tokens, columns, columns, tokens),
        out_specs=(tokens, tokens, columns, columns, tokens),
        check_vma=False,
    )
```

```python
import jax
import jax.numpy as jnp
from jax import lax
from jax.experimental import pallas as pl
from jax.experimental.pallas import tpu as pltpu
from jax.sharding import PartitionSpec as P

TOPK = 2
MB = 2
TOK_MB = 64
F32 = jnp.float32
BF16 = jnp.bfloat16
NN = ((1,), (0,))
NT = ((1,), (1,))
TN = ((0,), (0,))
VMEM_BYTES = 56 * 1024 * 1024


def dot(a, b, dims):
    return lax.dot_general(a, b, (dims, ((), ())), preferred_element_type=F32)


def tile_of(width):
    return next((n for n in (512, 256) if width % n == 0), width)


def kernel_call(body, grid, in_specs, out_specs, out_shape, scratch=(), scalars=0, cost=1):
    return pl.pallas_call(
        body,
        grid_spec=pltpu.PrefetchScalarGridSpec(
            num_scalar_prefetch=scalars,
            grid=grid,
            in_specs=in_specs,
            out_specs=out_specs,
            scratch_shapes=scratch,
        ),
        out_shape=out_shape,
        compiler_params=pltpu.CompilerParams(
            vmem_limit_bytes=VMEM_BYTES, dimension_semantics=("arbitrary",)
        ),
        cost_estimate=pl.CostEstimate(flops=1, bytes_accessed=cost, transcendentals=0),
    )


def place(placing, rows, gain=None):
    slots = dot(placing, rows, NN)
    return (slots if gain is None else slots * gain).astype(BF16)


HOP_COST = 22_000_000


def wide_tile(width):
    return width // 2 if width % 256 == 0 else width


def place_far(placing, parts, gain=None):
    slots = placing.shape[0]
    width = parts[0].shape[1]
    tile = wide_tile(width)
    fixed = [placing] if gain is None else [placing, gain]

    def body(placing_ref, *refs):
        part_refs, out_ref = refs[len(fixed) - 1 : -1], refs[-1]
        for cut in chunks(tile):
            rows = [ref[:, cut] for ref in part_refs]
            rows = rows[0] if len(rows) == 1 else jnp.concatenate(rows, axis=0)
            total = dot(placing_ref[...], rows, NN)
            if gain is not None:
                total = total * refs[0][...]
            out_ref[:, cut] = total.astype(BF16)

    return kernel_call(
        body,
        (width // tile,),
        [pl.BlockSpec(a.shape, lambda n: (0, 0)) for a in fixed]
        + [pl.BlockSpec((a.shape[0], tile), lambda n: (0, n)) for a in parts],
        pl.BlockSpec((slots, tile), lambda n: (0, n)),
        jax.ShapeDtypeStruct((slots, width), BF16),
        cost=HOP_COST,
    )(*fixed, *parts)


def combine(matrix, rows):
    if matrix.dtype == BF16:
        return dot(matrix, rows, NN)
    return lax.dot_general(
        matrix,
        rows.astype(F32),
        (NN, ((), ())),
        precision=lax.Precision.HIGHEST,
        preferred_element_type=F32,
    )


def chunks(width):
    tile = tile_of(width)
    return [slice(n * tile, (n + 1) * tile) for n in range(width // tile)]


def row_spec(rows, tile):
    if isinstance(rows, tuple):
        array, which = rows
        return pl.BlockSpec(
            (array.shape[0], 1, array.shape[2], tile), lambda n, *w: (0, which, 0, n * (tile < array.shape[3]))
        )
    return pl.BlockSpec((rows.shape[0], tile), lambda n, *w: (0, n * (tile < rows.shape[1])))


def row_array(rows):
    return rows[0] if isinstance(rows, tuple) else rows


def flat(ref):
    value = ref[...]
    return value.reshape(-1, value.shape[-1])


def weight_specs(width, half_units):
    mine, other = (lambda n: jnp.minimum(n, 1)), (lambda n: jnp.maximum(n - 2, 0))
    specs = []
    for at in (mine, other):
        columns = pl.BlockSpec((width, half_units), lambda n, at=at: (0, at(n)))
        specs += [columns, columns, pl.BlockSpec((half_units, width), lambda n, at=at: (at(n), 0))]
    return specs


def forward(count, rows, weights):
    width = weights[0].shape[0]
    half_units = weights[0].shape[1] // 2

    def body(x_ref, *refs):
        pre_gate_ref, pre_up_ref, hidden_ref, out_ref, acc_ref = refs[6:]
        step = pl.program_id(0)

        def quarter(gate_ref, up_ref, down_ref):
            x = flat(x_ref)
            pre_gate = dot(x, gate_ref[...], NN)
            pre_up = dot(x, up_ref[...], NN)
            pre_gate_ref[0] = pre_gate
            pre_up_ref[0] = pre_up
            hidden = (pre_gate * jax.nn.sigmoid(pre_gate) * pre_up).astype(BF16)
            hidden_ref[0] = hidden
            for cut in chunks(width):
                term = dot(hidden, down_ref[:, cut], NN)
                acc_ref[:, cut] = jnp.where(step == 0, term, acc_ref[:, cut] + term)

        pl.when(step < 2)(lambda: quarter(*refs[:3]))
        pl.when(step >= 2)(lambda: quarter(*refs[3:6]))

        @pl.when(step == 3)
        def _():
            out_ref[...] = acc_ref[...].astype(BF16)

    units = pl.BlockSpec((1, count, half_units), lambda n: (n, 0, 0))
    return kernel_call(
        body,
        (4,),
        [row_spec(rows, width)] + weight_specs(width, half_units),
        [units, units, units, pl.BlockSpec((count, width), lambda n: (0, 0))],
        [
            jax.ShapeDtypeStruct((4, count, half_units), F32),
            jax.ShapeDtypeStruct((4, count, half_units), F32),
            jax.ShapeDtypeStruct((4, count, half_units), BF16),
            jax.ShapeDtypeStruct((count, width), BF16),
        ],
        [pltpu.VMEM((count, width), F32)],
    )(row_array(rows), *weights)


def backward(count, rows_grad, pre_gate, pre_up, weights, beside=None, near=1):
    width = weights[0].shape[0]
    half_units = weights[0].shape[1] // 2

    piece = count // near

    def body(x_ref, pre_gate_ref, pre_up_ref, *refs):
        units_ref, out_ref, acc_ref = refs[-3:]
        step = pl.program_id(0)

        def quarter(gate_ref, up_ref, down_ref):
            hidden_grad = dot(flat(x_ref), down_ref[...], NT)
            pre_gate = pre_gate_ref[0]
            sigma = jax.nn.sigmoid(pre_gate)
            gate_grad = (
                hidden_grad * pre_up_ref[0] * sigma * (1.0 + pre_gate * (1.0 - sigma))
            ).astype(BF16)
            up_grad = (hidden_grad * (pre_gate * sigma)).astype(BF16)
            units_ref[0, :, :half_units] = gate_grad
            units_ref[0, :, half_units:] = up_grad
            for cut in chunks(width):
                term = dot(gate_grad, gate_ref[cut], NT) + dot(up_grad, up_ref[cut], NT)
                acc_ref[:, cut] = jnp.where(step == 0, term, acc_ref[:, cut] + term)

        pl.when(step < 2)(lambda: quarter(*refs[:3]))
        pl.when(step >= 2)(lambda: quarter(*refs[3:6]))

        @pl.when(step == 3)
        def _():
            if beside is None:
                out_ref[...] = acc_ref[...].astype(BF16)
            else:
                for n in range(near):
                    here = slice(n * piece, (n + 1) * piece)
                    out_ref[n, 0] = acc_ref[here].astype(BF16)
                    out_ref[n, 1] = refs[6][here]

    units = pl.BlockSpec((1, count, half_units), lambda n: (n, 0, 0))
    whole = pl.BlockSpec((count, width), lambda n: (0, 0))
    out_spec, out_shape = whole, (count, width)
    if beside is not None:
        out_shape = (near, 2, piece, width)
        out_spec = pl.BlockSpec(out_shape, lambda n: (0, 0, 0, 0))
    return kernel_call(
        body,
        (4,),
        [row_spec(rows_grad, width), units, units]
        + weight_specs(width, half_units)
        + ([] if beside is None else [whole]),
        [
            pl.BlockSpec((1, count, 2 * half_units), lambda n: (n, 0, 0)),
            out_spec,
        ],
        [
            jax.ShapeDtypeStruct((4, count, 2 * half_units), BF16),
            jax.ShapeDtypeStruct(out_shape, BF16),
        ],
        [pltpu.VMEM((count, width), F32)],
    )(row_array(rows_grad), pre_gate, pre_up, *weights, *([] if beside is None else [beside]))


def down_grad(count, which, hiddens, rows_grad):
    width = row_array(rows_grad[0]).shape[-1]
    half_units = hiddens[0].shape[2]
    tile = tile_of(width)

    def body(which_ref, *refs):
        unit_refs, row_refs, rest = refs[:4], refs[4:8], refs[8:]
        turned_ref = rest[-1]

        @pl.when(pl.program_id(0) == 0)
        def _():
            for n, unit_ref in enumerate(unit_refs):
                turned_ref[:, n * count : (n + 1) * count] = unit_ref[0].T

        rows = jnp.concatenate([flat(ref) for ref in row_refs], axis=0)
        total = dot(turned_ref[...], rows, NN)
        rest[-2][...] = total.astype(BF16)

    out_spec = pl.BlockSpec((half_units, tile), lambda n, w: (0, n))
    return kernel_call(
        body,
        (width // tile,),
        [pl.BlockSpec((1, count, half_units), lambda n, w: (w[0], 0, 0))] * 4
        + [row_spec(a, tile) for a in rows_grad],
        out_spec,
        jax.ShapeDtypeStruct((half_units, width), BF16),
        [pltpu.VMEM((half_units, 4 * count), BF16)],
        scalars=1,
    )(which, *hiddens, *map(row_array, rows_grad))


def gate_up_grad(count, which, units, rows, mirror_units, mirror_rows):
    width = row_array(rows[0]).shape[-1]
    both = units[0].shape[2]
    half_units = both // 2
    tile = tile_of(width)

    def body(which_ref, *refs):
        unit_refs, mirror_refs, row_refs = refs[:4], refs[4:8], refs[8:16]
        gate_ref, up_ref, turned_ref = refs[16:]

        @pl.when(pl.program_id(0) == 0)
        def _():
            for n, factor in enumerate([ref[0] for ref in unit_refs] + [ref[...] for ref in mirror_refs]):
                turned_ref[:, n * count : (n + 1) * count] = factor.T

        rows = jnp.concatenate([flat(ref) for ref in row_refs], axis=0)
        total = dot(turned_ref[...], rows, NN).astype(BF16).T
        gate_ref[...] = total[:, :half_units]
        up_ref[...] = total[:, half_units:]

    out_spec = pl.BlockSpec((tile, half_units), lambda n, w: (n, 0))
    return kernel_call(
        body,
        (width // tile,),
        [pl.BlockSpec((1, count, both), lambda n, w: (w[0], 0, 0))] * 4
        + [pl.BlockSpec((count, both), lambda n, w: (0, 0))] * 4
        + [row_spec(a, tile) for a in (*rows, *mirror_rows)],
        [out_spec] * 2,
        [jax.ShapeDtypeStruct((width, half_units), BF16)] * 2,
        [pltpu.VMEM((both, 8 * count), BF16)],
        scalars=1,
    )(which, *units, *mirror_units, *map(row_array, (*rows, *mirror_rows)))


def route(meta, half, expert_count, capacity):
    ids, gain = meta[:, :TOPK].astype(jnp.int32), meta[:, TOPK:]
    flat_ids = ids.reshape(MB, TOK_MB * TOPK)
    member = (flat_ids[:, :, None] == jnp.arange(expert_count, dtype=jnp.int32)).astype(jnp.int32)
    running = jnp.cumsum(member, axis=1) - 1
    rank = jnp.sum(member * running, axis=2)
    batch = jnp.arange(MB, dtype=jnp.int32)[:, None]
    near = expert_count // 2
    target = (((flat_ids - half * near) * MB + batch) * capacity + rank).reshape(ids.shape)
    slots = jnp.arange(near * MB * capacity, dtype=jnp.int32)
    matches = (target[:, :, None] == slots).astype(F32)
    turned = (target.T[:, None, :] == slots[:, None]).astype(F32)
    weighting = jnp.sum(matches * gain[:, :, None], axis=1)
    slot_gain = jnp.sum(turned * gain.T[:, None, :], axis=(0, 2))[:, None]
    return jnp.sum(turned, axis=0).astype(BF16), jnp.sum(matches, axis=1).astype(BF16), weighting, slot_gain


def on_device(acts, grad_out, expert_ids, route_weights, w_gate, w_up, w_down):
    weights = (w_gate[0], w_up[0], w_down[0])
    devices = lax.axis_size("expert")
    chips = devices // 2
    near = chips // 2
    capacity = 3 * TOPK * TOK_MB // (2 * chips)
    piece = MB * capacity
    width = acts.shape[2]
    half = (lax.axis_index("expert") >= devices // 2).astype(jnp.int32)
    rank_count = lax.axis_size("pipe")
    kept_half = (lax.axis_index("pipe") >= rank_count // 2).astype(jnp.int32)
    kept = kept_half.reshape(1)

    def hop(rows, distance):
        return lax.ppermute(rows, "expert", [(i, i ^ distance) for i in range(devices)])

    def far(rows):
        return hop(rows, devices // 2)

    def swap(rows):
        return hop(rows, 1)

    def mirror(rows):
        return lax.ppermute(rows, "pipe", [(p, rank_count - 1 - p) for p in range(rank_count)])

    groups = [
        [(part * near + member) * 2 + core for member in range(near)]
        for part in range(2)
        for core in range(2)
    ]

    def near_exchange(rows):
        return lax.all_to_all(
            rows.reshape(near, -1, width),
            "expert",
            split_axis=0,
            concat_axis=0,
            axis_index_groups=groups,
            tiled=True,
        ).reshape(rows.shape)

    def tie(*arrays):
        return lax.optimization_barrier(arrays)

    def for_mirror(units):
        return lax.dynamic_index_in_dim(units, 1 - kept_half, 0, keepdims=False)

    def of_set(matrix, which):
        shaped = matrix.reshape(matrix.shape[0], near, 1, piece)
        pair = [jnp.zeros_like(shaped), shaped] if which else [shaped, jnp.zeros_like(shaped)]
        return jnp.concatenate(pair, axis=2).reshape(matrix.shape[0], 2 * near * piece)

    count = near * piece
    first = acts.shape[1] // 8
    far_acts_0 = far(acts[0, :first])
    meta = jnp.concatenate([expert_ids[0].astype(F32), route_weights[0]], axis=1)
    own_placing, own_back, own_weighting, own_gain = route(meta, half, chips, capacity)
    both_placing = jnp.concatenate([of_set(own_placing.T, 0), of_set(own_placing.T, 1)], axis=0).T
    both_gain = jnp.stack([jnp.ones_like(own_gain).reshape(near, piece), own_gain.reshape(near, piece)], axis=1)
    own = place(
        both_placing, jnp.concatenate([acts[0], grad_out[0]], axis=0), both_gain.reshape(2 * count, 1)
    )
    own, far_acts_0, acts_1, meta = tie(own, far_acts_0, acts[0, first:], meta)

    far_acts_1 = far(acts_1)
    own = near_exchange(own).reshape(near, 2, piece, width)
    own_in = own[:, 0].reshape(count, width)
    far_meta = far(meta)
    other = [swap(weight) for weight in weights]
    far_placing, far_back, far_weighting, far_gain = route(far_meta, half, chips, capacity)
    far_in = place_far(far_placing, [far_acts_0, far_acts_1])
    far_in, own, own_in, far_placing, far_gain, grads, *weights = tie(
        far_in, own, own_in, far_placing, far_gain, grad_out[0], *weights, *other
    )

    far_grads = far(grads)
    far_in = near_exchange(far_in)
    own_b = swap(own)
    mirror_own = mirror(own_in)
    own_pre_gate, own_pre_up, own_hidden, own_out = forward(count, (own, 0), weights)
    own_units, own_input = backward(count, (own, 1), own_pre_gate, own_pre_up, weights)
    far_grads, own_out, own_input, far_weighting, own_weighting, far_mix, own_mix = tie(
        far_grads,
        own_out,
        own_input,
        far_weighting,
        own_weighting,
        of_set(far_back, 0),
        of_set(own_back, 1),
    )
    far_grad = place_far(far_placing, [far_grads], far_gain)
    far_grad, far_in, own_b, mirror_own, own_out, own_input, own_hidden, own_units = tie(
        far_grad, far_in, own_b, mirror_own, own_out, own_input, own_hidden, own_units
    )

    far_grad = near_exchange(far_grad)
    far_in_b = swap(far_in)
    mirror_own_b = swap(mirror_own)
    own_hidden_b = swap(own_hidden[2:])
    own_units_b = swap(own_units[2:])
    far_pre_gate, far_pre_up, far_hidden, far_out = forward(count, far_in, weights)
    far_grad, far_out, far_in_b, mirror_own_b, own_hidden_b, own_units_b, far_hidden = tie(
        far_grad, far_out, far_in_b, mirror_own_b, own_hidden_b, own_units_b, far_hidden
    )

    far_out = near_exchange(far_out)
    far_grad_b = swap(far_grad)
    far_hidden_b = swap(far_hidden[2:])
    far_units, inputs = backward(
        count, far_grad, far_pre_gate, far_pre_up, weights, own_input, near
    )
    far_out, far_units, inputs, far_grad_b, far_hidden_b, mirror_far, own_units, own_units_b = tie(
        far_out, far_units, inputs, far_grad_b, far_hidden_b, far_in, own_units, own_units_b
    )

    got_out = far(combine(far_weighting, far_out).astype(BF16))
    back = near_exchange(inputs.reshape(2 * count, width))
    mirror_far = mirror(mirror_far)
    far_units_b = swap(far_units[2:])
    all_units = (own_units, own_units_b, far_units, far_units_b)
    mirror_units = [
        mirror(jnp.stack([for_mirror(units) for units in all_units[:2]])),
        *[mirror(for_mirror(units)) for units in all_units[2:]],
    ]
    hiddens = (own_hidden, own_hidden_b, far_hidden, far_hidden_b)
    rows_grad = ((own, 1), (own_b.reshape(own.shape), 1), far_grad, far_grad_b)
    send_down = down_grad(count, 1 - kept, hiddens, rows_grad)
    keep_down = down_grad(count, kept, hiddens, rows_grad)
    got_out, back, mirror_far, send_down, keep_down, own_out, *mirror_units = tie(
        got_out, back, mirror_far, send_down, keep_down, own_out, *mirror_units
    )

    got_input = far(combine(far_mix, back).astype(BF16))
    own_out = near_exchange(own_out)
    got_down = mirror(send_down)
    mirror_far_b = swap(mirror_far)
    grad_gate, grad_up = gate_up_grad(
        count,
        kept,
        all_units,
        ((own, 0), (own_b.reshape(own.shape), 0), far_in, far_in_b),
        [mirror_units[0][0], mirror_units[0][1], *mirror_units[1:]],
        (mirror_own, mirror_own_b, mirror_far, mirror_far_b),
    )
    out_acts = (combine(own_weighting, own_out) + got_out.astype(F32)).astype(BF16)
    grad_down = (keep_down.astype(F32) + got_down.astype(F32)).astype(BF16)
    own_part = combine(own_mix, back)
    got_input, grad_down, grad_gate, grad_up, out_acts, own_part = tie(
        got_input, grad_down, grad_gate, grad_up, out_acts, own_part
    )
    grad_acts = (own_part + got_input.astype(F32)).astype(BF16)
    return out_acts[None], grad_acts[None], grad_gate[None], grad_up[None], grad_down[None]


def solution(mesh):
    tokens = P("pipe", "expert", None)
    columns = P("pipe", None, "expert")
    return jax.shard_map(
        on_device,
        mesh=mesh,
        in_specs=(tokens, tokens, tokens, tokens, columns, columns, tokens),
        out_specs=(tokens, tokens, columns, columns, tokens),
        check_vma=False,
    )
```

```python
import jax
import jax.numpy as jnp
from jax import lax
from jax.experimental import pallas as pl
from jax.experimental.pallas import tpu as pltpu
from jax.sharding import PartitionSpec as P

TOPK = 2
MB = 2
TOK_MB = 64
F32 = jnp.float32
BF16 = jnp.bfloat16
NN = ((1,), (0,))
NT = ((1,), (1,))
TN = ((0,), (0,))
VMEM_BYTES = 61 * 1024 * 1024


def dot(a, b, dims):
    return lax.dot_general(a, b, (dims, ((), ())), preferred_element_type=F32)


def tile_of(width):
    return next((n for n in (512, 256) if width % n == 0), width)


def kernel_call(body, grid, in_specs, out_specs, out_shape, scratch=(), scalars=0, cost=1):
    return pl.pallas_call(
        body,
        grid_spec=pltpu.PrefetchScalarGridSpec(
            num_scalar_prefetch=scalars,
            grid=grid,
            in_specs=in_specs,
            out_specs=out_specs,
            scratch_shapes=scratch,
        ),
        out_shape=out_shape,
        compiler_params=pltpu.CompilerParams(
            vmem_limit_bytes=VMEM_BYTES, dimension_semantics=("arbitrary",)
        ),
        cost_estimate=pl.CostEstimate(flops=1, bytes_accessed=cost, transcendentals=0),
    )


def place(placing, rows, gain=None):
    slots = dot(placing, rows, NN)
    return (slots if gain is None else slots * gain).astype(BF16)


HOP_COST = 22_000_000


def wide_tile(width):
    return width // 2 if width % 256 == 0 else width


def place_far(placing, parts, gain=None):
    slots = placing.shape[0]
    width = parts[0].shape[1]
    tile = wide_tile(width)
    fixed = [placing] if gain is None else [placing, gain]

    def body(placing_ref, *refs):
        part_refs, out_ref = refs[len(fixed) - 1 : -1], refs[-1]
        for cut in chunks(tile):
            rows = [ref[:, cut] for ref in part_refs]
            rows = rows[0] if len(rows) == 1 else jnp.concatenate(rows, axis=0)
            total = dot(placing_ref[...], rows, NN)
            if gain is not None:
                total = total * refs[0][...]
            out_ref[:, cut] = total.astype(BF16)

    return kernel_call(
        body,
        (width // tile,),
        [pl.BlockSpec(a.shape, lambda n: (0, 0)) for a in fixed]
        + [pl.BlockSpec((a.shape[0], tile), lambda n: (0, n)) for a in parts],
        pl.BlockSpec((slots, tile), lambda n: (0, n)),
        jax.ShapeDtypeStruct((slots, width), BF16),
        cost=HOP_COST,
    )(*fixed, *parts)


def combine(matrix, rows):
    if matrix.dtype == BF16:
        return dot(matrix, rows, NN)
    return lax.dot_general(
        matrix,
        rows.astype(F32),
        (NN, ((), ())),
        precision=lax.Precision.HIGH,
        preferred_element_type=F32,
    )


def chunks(width):
    tile = tile_of(width)
    return [slice(n * tile, (n + 1) * tile) for n in range(width // tile)]


def row_spec(rows, tile):
    if isinstance(rows, tuple):
        array, which = rows
        return pl.BlockSpec(
            (array.shape[0], 1, array.shape[2], tile), lambda n, *w: (0, which, 0, n * (tile < array.shape[3]))
        )
    return pl.BlockSpec((rows.shape[0], tile), lambda n, *w: (0, n * (tile < rows.shape[1])))


def row_array(rows):
    return rows[0] if isinstance(rows, tuple) else rows


def flat(ref):
    value = ref[...]
    return value.reshape(-1, value.shape[-1])


def weight_specs(width, half_units):
    mine, other = (lambda n: jnp.minimum(n, 1)), (lambda n: jnp.maximum(n - 2, 0))
    specs = []
    for at in (mine, other):
        columns = pl.BlockSpec((width, half_units), lambda n, at=at: (0, at(n)))
        specs += [columns, columns, pl.BlockSpec((half_units, width), lambda n, at=at: (at(n), 0))]
    return specs


def forward(count, rows, weights):
    width = weights[0].shape[0]
    half_units = weights[0].shape[1] // 2

    def body(x_ref, *refs):
        pre_gate_ref, pre_up_ref, hidden_ref, out_ref, acc_ref = refs[6:]
        step = pl.program_id(0)

        def quarter(gate_ref, up_ref, down_ref):
            x = flat(x_ref)
            pre_gate = dot(x, gate_ref[...], NN)
            pre_up = dot(x, up_ref[...], NN)
            pre_gate_ref[0] = pre_gate
            pre_up_ref[0] = pre_up
            hidden = (pre_gate * jax.nn.sigmoid(pre_gate) * pre_up).astype(BF16)
            hidden_ref[0] = hidden
            for cut in chunks(width):
                term = dot(hidden, down_ref[:, cut], NN)
                acc_ref[:, cut] = jnp.where(step == 0, term, acc_ref[:, cut] + term)

        pl.when(step < 2)(lambda: quarter(*refs[:3]))
        pl.when(step >= 2)(lambda: quarter(*refs[3:6]))

        @pl.when(step == 3)
        def _():
            out_ref[...] = acc_ref[...].astype(BF16)

    units = pl.BlockSpec((1, count, half_units), lambda n: (n, 0, 0))
    return kernel_call(
        body,
        (4,),
        [row_spec(rows, width)] + weight_specs(width, half_units),
        [units, units, units, pl.BlockSpec((count, width), lambda n: (0, 0))],
        [
            jax.ShapeDtypeStruct((4, count, half_units), F32),
            jax.ShapeDtypeStruct((4, count, half_units), F32),
            jax.ShapeDtypeStruct((4, count, half_units), BF16),
            jax.ShapeDtypeStruct((count, width), BF16),
        ],
        [pltpu.VMEM((count, width), F32)],
    )(row_array(rows), *weights)


def backward(count, rows_grad, pre_gate, pre_up, weights, beside=None, near=1):
    width = weights[0].shape[0]
    half_units = weights[0].shape[1] // 2

    piece = count // near

    def body(x_ref, pre_gate_ref, pre_up_ref, *refs):
        units_ref, out_ref, acc_ref = refs[-3:]
        step = pl.program_id(0)

        def quarter(gate_ref, up_ref, down_ref):
            hidden_grad = dot(flat(x_ref), down_ref[...], NT)
            pre_gate = pre_gate_ref[0]
            sigma = jax.nn.sigmoid(pre_gate)
            gate_grad = (
                hidden_grad * pre_up_ref[0] * sigma * (1.0 + pre_gate * (1.0 - sigma))
            ).astype(BF16)
            up_grad = (hidden_grad * (pre_gate * sigma)).astype(BF16)
            units_ref[0, :, :half_units] = gate_grad
            units_ref[0, :, half_units:] = up_grad
            for cut in chunks(width):
                term = dot(gate_grad, gate_ref[cut], NT) + dot(up_grad, up_ref[cut], NT)
                acc_ref[:, cut] = jnp.where(step == 0, term, acc_ref[:, cut] + term)

        pl.when(step < 2)(lambda: quarter(*refs[:3]))
        pl.when(step >= 2)(lambda: quarter(*refs[3:6]))

        @pl.when(step == 3)
        def _():
            if beside is None:
                out_ref[...] = acc_ref[...].astype(BF16)
            else:
                for n in range(near):
                    here = slice(n * piece, (n + 1) * piece)
                    out_ref[n, 0] = acc_ref[here].astype(BF16)
                    out_ref[n, 1] = refs[6][here]

    units = pl.BlockSpec((1, count, half_units), lambda n: (n, 0, 0))
    whole = pl.BlockSpec((count, width), lambda n: (0, 0))
    out_spec, out_shape = whole, (count, width)
    if beside is not None:
        out_shape = (near, 2, piece, width)
        out_spec = pl.BlockSpec(out_shape, lambda n: (0, 0, 0, 0))
    return kernel_call(
        body,
        (4,),
        [row_spec(rows_grad, width), units, units]
        + weight_specs(width, half_units)
        + ([] if beside is None else [whole]),
        [
            pl.BlockSpec((1, count, 2 * half_units), lambda n: (n, 0, 0)),
            out_spec,
        ],
        [
            jax.ShapeDtypeStruct((4, count, 2 * half_units), BF16),
            jax.ShapeDtypeStruct(out_shape, BF16),
        ],
        [pltpu.VMEM((count, width), F32)],
    )(row_array(rows_grad), pre_gate, pre_up, *weights, *([] if beside is None else [beside]))


def down_grad(count, which, hiddens, rows_grad):
    width = row_array(rows_grad[0]).shape[-1]
    half_units = hiddens[0].shape[2]
    tile = tile_of(width)

    def body(which_ref, *refs):
        unit_refs, row_refs, rest = refs[:4], refs[4:8], refs[8:]
        turned_ref = rest[-1]

        @pl.when(pl.program_id(0) == 0)
        def _():
            for n, unit_ref in enumerate(unit_refs):
                turned_ref[:, n * count : (n + 1) * count] = unit_ref[0].T

        rows = jnp.concatenate([flat(ref) for ref in row_refs], axis=0)
        total = dot(turned_ref[...], rows, NN)
        rest[-2][...] = total.astype(BF16)

    out_spec = pl.BlockSpec((half_units, tile), lambda n, w: (0, n))
    return kernel_call(
        body,
        (width // tile,),
        [pl.BlockSpec((1, count, half_units), lambda n, w: (w[0], 0, 0))] * 4
        + [row_spec(a, tile) for a in rows_grad],
        out_spec,
        jax.ShapeDtypeStruct((half_units, width), BF16),
        [pltpu.VMEM((half_units, 4 * count), BF16)],
        scalars=1,
    )(which, *hiddens, *map(row_array, rows_grad))


def gate_up_grad(count, which, units, rows, mirror_units, mirror_rows):
    width = row_array(rows[0]).shape[-1]
    both = units[0].shape[2]
    half_units = both // 2
    tile = tile_of(width)

    def body(which_ref, *refs):
        unit_refs, mirror_refs, row_refs = refs[:4], refs[4:8], refs[8:16]
        gate_ref, up_ref, turned_ref = refs[16:]

        @pl.when(pl.program_id(0) == 0)
        def _():
            for n, factor in enumerate([ref[0] for ref in unit_refs] + [ref[...] for ref in mirror_refs]):
                turned_ref[:, n * count : (n + 1) * count] = factor.T

        rows = jnp.concatenate([flat(ref) for ref in row_refs], axis=0)
        total = dot(turned_ref[...], rows, NN).astype(BF16).T
        gate_ref[...] = total[:, :half_units]
        up_ref[...] = total[:, half_units:]

    out_spec = pl.BlockSpec((tile, half_units), lambda n, w: (n, 0))
    return kernel_call(
        body,
        (width // tile,),
        [pl.BlockSpec((1, count, both), lambda n, w: (w[0], 0, 0))] * 4
        + [pl.BlockSpec((count, both), lambda n, w: (0, 0))] * 4
        + [row_spec(a, tile) for a in (*rows, *mirror_rows)],
        [out_spec] * 2,
        [jax.ShapeDtypeStruct((width, half_units), BF16)] * 2,
        [pltpu.VMEM((both, 8 * count), BF16)],
        scalars=1,
    )(which, *units, *mirror_units, *map(row_array, (*rows, *mirror_rows)))


def route(meta, half, expert_count, capacity):
    ids, gain = meta[:, :TOPK].astype(jnp.int32), meta[:, TOPK:]
    flat_ids = ids.reshape(MB, TOK_MB * TOPK)
    member = (flat_ids[:, :, None] == jnp.arange(expert_count, dtype=jnp.int32)).astype(jnp.int32)
    running = jnp.cumsum(member, axis=1) - 1
    rank = jnp.sum(member * running, axis=2)
    batch = jnp.arange(MB, dtype=jnp.int32)[:, None]
    near = expert_count // 2
    target = (((flat_ids - half * near) * MB + batch) * capacity + rank).reshape(ids.shape)
    slots = jnp.arange(near * MB * capacity, dtype=jnp.int32)
    matches = (target[:, :, None] == slots).astype(F32)
    turned = (target.T[:, None, :] == slots[:, None]).astype(F32)
    weighting = jnp.sum(matches * gain[:, :, None], axis=1)
    slot_gain = jnp.sum(turned * gain.T[:, None, :], axis=(0, 2))[:, None]
    return jnp.sum(turned, axis=0).astype(BF16), jnp.sum(matches, axis=1).astype(BF16), weighting, slot_gain


def on_device(acts, grad_out, expert_ids, route_weights, w_gate, w_up, w_down):
    weights = (w_gate[0], w_up[0], w_down[0])
    devices = lax.axis_size("expert")
    chips = devices // 2
    near = chips // 2
    capacity = 3 * TOPK * TOK_MB // (2 * chips)
    piece = MB * capacity
    width = acts.shape[2]
    half = (lax.axis_index("expert") >= devices // 2).astype(jnp.int32)
    rank_count = lax.axis_size("pipe")
    kept_half = (lax.axis_index("pipe") >= rank_count // 2).astype(jnp.int32)
    kept = kept_half.reshape(1)

    def hop(rows, distance):
        return lax.ppermute(rows, "expert", [(i, i ^ distance) for i in range(devices)])

    def far(rows):
        return hop(rows, devices // 2)

    def swap(rows):
        return hop(rows, 1)

    def mirror(rows):
        return lax.ppermute(rows, "pipe", [(p, rank_count - 1 - p) for p in range(rank_count)])

    groups = [
        [(part * near + member) * 2 + core for member in range(near)]
        for part in range(2)
        for core in range(2)
    ]

    def near_exchange(rows):
        return lax.all_to_all(
            rows.reshape(near, -1, width),
            "expert",
            split_axis=0,
            concat_axis=0,
            axis_index_groups=groups,
            tiled=True,
        ).reshape(rows.shape)

    def tie(*arrays):
        return lax.optimization_barrier(arrays)

    def for_mirror(units):
        return lax.dynamic_index_in_dim(units, 1 - kept_half, 0, keepdims=False)

    def of_set(matrix, which):
        shaped = matrix.reshape(matrix.shape[0], near, 1, piece)
        pair = [jnp.zeros_like(shaped), shaped] if which else [shaped, jnp.zeros_like(shaped)]
        return jnp.concatenate(pair, axis=2).reshape(matrix.shape[0], 2 * near * piece)

    count = near * piece
    first = acts.shape[1] // 8
    far_acts_0 = far(acts[0, :first])
    meta = jnp.concatenate([expert_ids[0].astype(F32), route_weights[0]], axis=1)
    own_placing, own_back, own_weighting, own_gain = route(meta, half, chips, capacity)
    both_placing = jnp.concatenate([of_set(own_placing.T, 0), of_set(own_placing.T, 1)], axis=0).T
    both_gain = jnp.stack([jnp.ones_like(own_gain).reshape(near, piece), own_gain.reshape(near, piece)], axis=1)
    own = place(
        both_placing, jnp.concatenate([acts[0], grad_out[0]], axis=0), both_gain.reshape(2 * count, 1)
    )
    own, far_acts_0, acts_1, meta = tie(own, far_acts_0, acts[0, first:], meta)

    far_acts_1 = far(acts_1)
    own = near_exchange(own).reshape(near, 2, piece, width)
    own_in = own[:, 0].reshape(count, width)
    far_meta = far(meta)
    other = [swap(weight) for weight in weights]
    far_placing, far_back, far_weighting, far_gain = route(far_meta, half, chips, capacity)
    far_in = place_far(far_placing, [far_acts_0, far_acts_1])
    far_in, own, own_in, far_placing, far_gain, grads, *weights = tie(
        far_in, own, own_in, far_placing, far_gain, grad_out[0], *weights, *other
    )

    far_grads = far(grads)
    far_in = near_exchange(far_in)
    own_b = swap(own)
    mirror_own = mirror(own_in)
    own_pre_gate, own_pre_up, own_hidden, own_out = forward(count, (own, 0), weights)
    own_units, own_input = backward(count, (own, 1), own_pre_gate, own_pre_up, weights)
    far_grads, own_out, own_input, far_weighting, own_weighting, far_mix, own_mix = tie(
        far_grads,
        own_out,
        own_input,
        far_weighting,
        own_weighting,
        of_set(far_back, 0),
        of_set(own_back, 1),
    )
    far_grad = place_far(far_placing, [far_grads], far_gain)
    far_grad, far_in, own_b, mirror_own, own_out, own_input, own_hidden, own_units = tie(
        far_grad, far_in, own_b, mirror_own, own_out, own_input, own_hidden, own_units
    )

    far_grad = near_exchange(far_grad)
    far_in_b = swap(far_in)
    mirror_own_b = swap(mirror_own)
    own_hidden_b = swap(own_hidden[2:])
    own_units_b = swap(own_units[2:])
    far_pre_gate, far_pre_up, far_hidden, far_out = forward(count, far_in, weights)
    far_grad, far_out, far_in_b, mirror_own_b, own_hidden_b, own_units_b, far_hidden = tie(
        far_grad, far_out, far_in_b, mirror_own_b, own_hidden_b, own_units_b, far_hidden
    )

    far_out = near_exchange(far_out)
    far_grad_b = swap(far_grad)
    far_hidden_b = swap(far_hidden[2:])
    far_units, inputs = backward(
        count, far_grad, far_pre_gate, far_pre_up, weights, own_input, near
    )
    far_out, far_units, inputs, far_grad_b, far_hidden_b, mirror_far, own_units, own_units_b = tie(
        far_out, far_units, inputs, far_grad_b, far_hidden_b, far_in, own_units, own_units_b
    )

    got_out = far(combine(far_weighting, far_out).astype(BF16))
    back = near_exchange(inputs.reshape(2 * count, width))
    mirror_far = mirror(mirror_far)
    far_units_b = swap(far_units[2:])
    all_units = (own_units, own_units_b, far_units, far_units_b)
    mirror_units = [
        mirror(jnp.stack([for_mirror(units) for units in all_units[:2]])),
        *[mirror(for_mirror(units)) for units in all_units[2:]],
    ]
    hiddens = (own_hidden, own_hidden_b, far_hidden, far_hidden_b)
    rows_grad = ((own, 1), (own_b.reshape(own.shape), 1), far_grad, far_grad_b)
    send_down = down_grad(count, 1 - kept, hiddens, rows_grad)
    keep_down = down_grad(count, kept, hiddens, rows_grad)
    got_out, back, mirror_far, send_down, keep_down, own_out, *mirror_units = tie(
        got_out, back, mirror_far, send_down, keep_down, own_out, *mirror_units
    )

    got_input = far(combine(far_mix, back).astype(BF16))
    own_out = near_exchange(own_out)
    got_down = mirror(send_down)
    mirror_far_b = swap(mirror_far)
    grad_gate, grad_up = gate_up_grad(
        count,
        kept,
        all_units,
        ((own, 0), (own_b.reshape(own.shape), 0), far_in, far_in_b),
        [mirror_units[0][0], mirror_units[0][1], *mirror_units[1:]],
        (mirror_own, mirror_own_b, mirror_far, mirror_far_b),
    )
    out_acts = (combine(own_weighting, own_out) + got_out.astype(F32)).astype(BF16)
    grad_down = (keep_down.astype(F32) + got_down.astype(F32)).astype(BF16)
    own_part = combine(own_mix, back)
    got_input, grad_down, grad_gate, grad_up, out_acts, own_part = tie(
        got_input, grad_down, grad_gate, grad_up, out_acts, own_part
    )
    grad_acts = (own_part + got_input.astype(F32)).astype(BF16)
    return out_acts[None], grad_acts[None], grad_gate[None], grad_up[None], grad_down[None]


def solution(mesh):
    tokens = P("pipe", "expert", None)
    columns = P("pipe", None, "expert")
    return jax.shard_map(
        on_device,
        mesh=mesh,
        in_specs=(tokens, tokens, tokens, tokens, columns, columns, tokens),
        out_specs=(tokens, tokens, columns, columns, tokens),
        check_vma=False,
    )
```

```python
import jax
import jax.numpy as jnp
from jax import lax
from jax.experimental import pallas as pl
from jax.experimental.pallas import tpu as pltpu
from jax.sharding import PartitionSpec as P

TOPK = 2
MB = 2
TOK_MB = 64
F32 = jnp.float32
BF16 = jnp.bfloat16
NN = ((1,), (0,))
NT = ((1,), (1,))
TN = ((0,), (0,))
VMEM_BYTES = 56 * 1024 * 1024


def dot(a, b, dims):
    return lax.dot_general(a, b, (dims, ((), ())), preferred_element_type=F32)


def tile_of(width):
    return next((n for n in (512, 256) if width % n == 0), width)


def kernel_call(body, grid, in_specs, out_specs, out_shape, scratch=(), scalars=0, cost=1):
    return pl.pallas_call(
        body,
        grid_spec=pltpu.PrefetchScalarGridSpec(
            num_scalar_prefetch=scalars,
            grid=grid,
            in_specs=in_specs,
            out_specs=out_specs,
            scratch_shapes=scratch,
        ),
        out_shape=out_shape,
        compiler_params=pltpu.CompilerParams(
            vmem_limit_bytes=VMEM_BYTES, dimension_semantics=("arbitrary",)
        ),
        cost_estimate=pl.CostEstimate(flops=1, bytes_accessed=cost, transcendentals=0),
    )


def place(placing, rows, gain=None):
    slots = dot(placing, rows, NN)
    return (slots if gain is None else slots * gain).astype(BF16)


HOP_COST = 22_000_000


def wide_tile(width):
    return width // 2 if width % 256 == 0 else width


def place_far(placing, parts, gain=None):
    slots = placing.shape[0]
    width = parts[0].shape[1]
    tile = wide_tile(width)
    fixed = [placing] if gain is None else [placing, gain]

    def body(placing_ref, *refs):
        part_refs, out_ref = refs[len(fixed) - 1 : -1], refs[-1]
        for cut in chunks(tile):
            rows = [ref[:, cut] for ref in part_refs]
            rows = rows[0] if len(rows) == 1 else jnp.concatenate(rows, axis=0)
            total = dot(placing_ref[...], rows, NN)
            if gain is not None:
                total = total * refs[0][...]
            out_ref[:, cut] = total.astype(BF16)

    return kernel_call(
        body,
        (width // tile,),
        [pl.BlockSpec(a.shape, lambda n: (0, 0)) for a in fixed]
        + [pl.BlockSpec((a.shape[0], tile), lambda n: (0, n)) for a in parts],
        pl.BlockSpec((slots, tile), lambda n: (0, n)),
        jax.ShapeDtypeStruct((slots, width), BF16),
        cost=HOP_COST,
    )(*fixed, *parts)


def combine(matrix, rows):
    if matrix.dtype == BF16:
        return dot(matrix, rows, NN)
    return lax.dot_general(
        matrix,
        rows.astype(F32),
        (NN, ((), ())),
        precision=lax.Precision.HIGHEST,
        preferred_element_type=F32,
    )


def chunks(width):
    tile = tile_of(width)
    return [slice(n * tile, (n + 1) * tile) for n in range(width // tile)]


def row_spec(rows, tile):
    if isinstance(rows, tuple):
        array, which = rows
        return pl.BlockSpec(
            (array.shape[0], 1, array.shape[2], tile), lambda n, *w: (0, which, 0, n * (tile < array.shape[3]))
        )
    return pl.BlockSpec((rows.shape[0], tile), lambda n, *w: (0, n * (tile < rows.shape[1])))


def row_array(rows):
    return rows[0] if isinstance(rows, tuple) else rows


def flat(ref):
    value = ref[...]
    return value.reshape(-1, value.shape[-1])


def weight_specs(width, half_units):
    mine, other = (lambda n: jnp.minimum(n, 1)), (lambda n: jnp.maximum(n - 2, 0))
    specs = []
    for at in (mine, other):
        columns = pl.BlockSpec((width, half_units), lambda n, at=at: (0, at(n)))
        specs += [columns, columns, pl.BlockSpec((half_units, width), lambda n, at=at: (at(n), 0))]
    return specs


def forward(count, rows, weights):
    width = weights[0].shape[0]
    half_units = weights[0].shape[1] // 2

    def body(x_ref, *refs):
        pre_gate_ref, pre_up_ref, hidden_ref, out_ref, acc_ref = refs[6:]
        step = pl.program_id(0)

        def finish(cut, total):
            out_ref[:, cut] = total.astype(BF16)

        def quarter(last, gate_ref, up_ref, down_ref):
            x = flat(x_ref)
            pre_gate = dot(x, gate_ref[...], NN)
            pre_up = dot(x, up_ref[...], NN)
            pre_gate_ref[0] = pre_gate
            pre_up_ref[0] = pre_up
            hidden = (pre_gate * jax.nn.sigmoid(pre_gate) * pre_up).astype(BF16)
            hidden_ref[0] = hidden
            for cut in chunks(width):
                term = dot(hidden, down_ref[:, cut], NN)
                if last:
                    finish(cut, acc_ref[:, cut] + term)
                else:
                    acc_ref[:, cut] = jnp.where(step == 0, term, acc_ref[:, cut] + term)

        pl.when(step < 2)(lambda: quarter(False, *refs[:3]))
        pl.when(step == 2)(lambda: quarter(False, *refs[3:6]))
        pl.when(step == 3)(lambda: quarter(True, *refs[3:6]))

    units = pl.BlockSpec((1, count, half_units), lambda n: (n, 0, 0))
    return kernel_call(
        body,
        (4,),
        [row_spec(rows, width)] + weight_specs(width, half_units),
        [units, units, units, pl.BlockSpec((count, width), lambda n: (0, 0))],
        [
            jax.ShapeDtypeStruct((4, count, half_units), F32),
            jax.ShapeDtypeStruct((4, count, half_units), F32),
            jax.ShapeDtypeStruct((4, count, half_units), BF16),
            jax.ShapeDtypeStruct((count, width), BF16),
        ],
        [pltpu.VMEM((count, width), F32)],
    )(row_array(rows), *weights)


def backward(count, rows_grad, pre_gate, pre_up, weights, beside=None, near=1):
    width = weights[0].shape[0]
    half_units = weights[0].shape[1] // 2

    piece = count // near

    def body(x_ref, pre_gate_ref, pre_up_ref, *refs):
        units_ref, out_ref, acc_ref = refs[-3:]
        step = pl.program_id(0)

        def finish(cut, total):
            total = total.astype(BF16)
            if beside is None:
                out_ref[:, cut] = total
            else:
                for n in range(near):
                    out_ref[n, 0, :, cut] = total[n * piece : (n + 1) * piece]

        def quarter(last, gate_ref, up_ref, down_ref):
            hidden_grad = dot(flat(x_ref), down_ref[...], NT)
            pre_gate = pre_gate_ref[0]
            sigma = jax.nn.sigmoid(pre_gate)
            gate_grad = (
                hidden_grad * pre_up_ref[0] * sigma * (1.0 + pre_gate * (1.0 - sigma))
            ).astype(BF16)
            up_grad = (hidden_grad * (pre_gate * sigma)).astype(BF16)
            units_ref[0, :, :half_units] = gate_grad
            units_ref[0, :, half_units:] = up_grad
            for cut in chunks(width):
                term = dot(gate_grad, gate_ref[cut], NT) + dot(up_grad, up_ref[cut], NT)
                if last:
                    finish(cut, acc_ref[:, cut] + term)
                else:
                    acc_ref[:, cut] = jnp.where(step == 0, term, acc_ref[:, cut] + term)

        pl.when(step < 2)(lambda: quarter(False, *refs[:3]))
        pl.when(step == 2)(lambda: quarter(False, *refs[3:6]))
        pl.when(step == 3)(lambda: quarter(True, *refs[3:6]))

        if beside is not None:

            @pl.when(step == 3)
            def _():
                for n in range(near):
                    out_ref[n, 1] = refs[6][n * piece : (n + 1) * piece]

    units = pl.BlockSpec((1, count, half_units), lambda n: (n, 0, 0))
    whole = pl.BlockSpec((count, width), lambda n: (0, 0))
    out_spec, out_shape = whole, (count, width)
    if beside is not None:
        out_shape = (near, 2, piece, width)
        out_spec = pl.BlockSpec(out_shape, lambda n: (0, 0, 0, 0))
    return kernel_call(
        body,
        (4,),
        [row_spec(rows_grad, width), units, units]
        + weight_specs(width, half_units)
        + ([] if beside is None else [whole]),
        [
            pl.BlockSpec((1, count, 2 * half_units), lambda n: (n, 0, 0)),
            out_spec,
        ],
        [
            jax.ShapeDtypeStruct((4, count, 2 * half_units), BF16),
            jax.ShapeDtypeStruct(out_shape, BF16),
        ],
        [pltpu.VMEM((count, width), F32)],
    )(row_array(rows_grad), pre_gate, pre_up, *weights, *([] if beside is None else [beside]))


def down_grad(count, which, hiddens, rows_grad):
    width = row_array(rows_grad[0]).shape[-1]
    half_units = hiddens[0].shape[2]
    tile = tile_of(width)

    def body(which_ref, *refs):
        unit_refs, row_refs, rest = refs[:4], refs[4:8], refs[8:]
        turned_ref = rest[-1]

        @pl.when(pl.program_id(0) == 0)
        def _():
            for n, unit_ref in enumerate(unit_refs):
                turned_ref[:, n * count : (n + 1) * count] = unit_ref[0].T

        rows = jnp.concatenate([flat(ref) for ref in row_refs], axis=0)
        total = dot(turned_ref[...], rows, NN)
        rest[-2][...] = total.astype(BF16)

    out_spec = pl.BlockSpec((half_units, tile), lambda n, w: (0, n))
    return kernel_call(
        body,
        (width // tile,),
        [pl.BlockSpec((1, count, half_units), lambda n, w: (w[0], 0, 0))] * 4
        + [row_spec(a, tile) for a in rows_grad],
        out_spec,
        jax.ShapeDtypeStruct((half_units, width), BF16),
        [pltpu.VMEM((half_units, 4 * count), BF16)],
        scalars=1,
    )(which, *hiddens, *map(row_array, rows_grad))


def gate_up_grad(count, which, units, rows, mirror_units, mirror_rows):
    width = row_array(rows[0]).shape[-1]
    both = units[0].shape[2]
    half_units = both // 2
    tile = tile_of(width)

    def body(which_ref, *refs):
        unit_refs, mirror_refs, row_refs = refs[:4], refs[4:8], refs[8:16]
        gate_ref, up_ref, turned_ref = refs[16:]

        @pl.when(pl.program_id(0) == 0)
        def _():
            for n, factor in enumerate([ref[0] for ref in unit_refs] + [ref[...] for ref in mirror_refs]):
                turned_ref[:, n * count : (n + 1) * count] = factor.T

        rows = jnp.concatenate([flat(ref) for ref in row_refs], axis=0)
        total = dot(turned_ref[...], rows, NN).astype(BF16).T
        gate_ref[...] = total[:, :half_units]
        up_ref[...] = total[:, half_units:]

    out_spec = pl.BlockSpec((tile, half_units), lambda n, w: (n, 0))
    return kernel_call(
        body,
        (width // tile,),
        [pl.BlockSpec((1, count, both), lambda n, w: (w[0], 0, 0))] * 4
        + [pl.BlockSpec((count, both), lambda n, w: (0, 0))] * 4
        + [row_spec(a, tile) for a in (*rows, *mirror_rows)],
        [out_spec] * 2,
        [jax.ShapeDtypeStruct((width, half_units), BF16)] * 2,
        [pltpu.VMEM((both, 8 * count), BF16)],
        scalars=1,
    )(which, *units, *mirror_units, *map(row_array, (*rows, *mirror_rows)))


def route(meta, half, expert_count, capacity):
    ids, gain = meta[:, :TOPK].astype(jnp.int32), meta[:, TOPK:]
    flat_ids = ids.reshape(MB, TOK_MB * TOPK)
    member = (flat_ids[:, :, None] == jnp.arange(expert_count, dtype=jnp.int32)).astype(jnp.int32)
    running = jnp.cumsum(member, axis=1) - 1
    rank = jnp.sum(member * running, axis=2)
    batch = jnp.arange(MB, dtype=jnp.int32)[:, None]
    near = expert_count // 2
    target = (((flat_ids - half * near) * MB + batch) * capacity + rank).reshape(ids.shape)
    slots = jnp.arange(near * MB * capacity, dtype=jnp.int32)
    matches = (target[:, :, None] == slots).astype(F32)
    turned = (target.T[:, None, :] == slots[:, None]).astype(F32)
    weighting = jnp.sum(matches * gain[:, :, None], axis=1)
    slot_gain = jnp.sum(turned * gain.T[:, None, :], axis=(0, 2))[:, None]
    return jnp.sum(turned, axis=0).astype(BF16), jnp.sum(matches, axis=1).astype(BF16), weighting, slot_gain


def on_device(acts, grad_out, expert_ids, route_weights, w_gate, w_up, w_down):
    weights = (w_gate[0], w_up[0], w_down[0])
    devices = lax.axis_size("expert")
    chips = devices // 2
    near = chips // 2
    capacity = 3 * TOPK * TOK_MB // (2 * chips)
    piece = MB * capacity
    width = acts.shape[2]
    half = (lax.axis_index("expert") >= devices // 2).astype(jnp.int32)
    rank_count = lax.axis_size("pipe")
    kept_half = (lax.axis_index("pipe") >= rank_count // 2).astype(jnp.int32)
    kept = kept_half.reshape(1)

    def hop(rows, distance):
        return lax.ppermute(rows, "expert", [(i, i ^ distance) for i in range(devices)])

    def far(rows):
        return hop(rows, devices // 2)

    def swap(rows):
        return hop(rows, 1)

    def mirror(rows):
        return lax.ppermute(rows, "pipe", [(p, rank_count - 1 - p) for p in range(rank_count)])

    groups = [
        [(part * near + member) * 2 + core for member in range(near)]
        for part in range(2)
        for core in range(2)
    ]

    def near_exchange(rows):
        return lax.all_to_all(
            rows.reshape(near, -1, width),
            "expert",
            split_axis=0,
            concat_axis=0,
            axis_index_groups=groups,
            tiled=True,
        ).reshape(rows.shape)

    def tie(*arrays):
        return lax.optimization_barrier(arrays)

    def for_mirror(units):
        return lax.dynamic_index_in_dim(units, 1 - kept_half, 0, keepdims=False)

    def of_set(matrix, which):
        shaped = matrix.reshape(matrix.shape[0], near, 1, piece)
        pair = [jnp.zeros_like(shaped), shaped] if which else [shaped, jnp.zeros_like(shaped)]
        return jnp.concatenate(pair, axis=2).reshape(matrix.shape[0], 2 * near * piece)

    count = near * piece
    first = acts.shape[1] // 8
    far_acts_0 = far(acts[0, :first])
    meta = jnp.concatenate([expert_ids[0].astype(F32), route_weights[0]], axis=1)
    own_placing, own_back, own_weighting, own_gain = route(meta, half, chips, capacity)
    both_placing = jnp.concatenate([of_set(own_placing.T, 0), of_set(own_placing.T, 1)], axis=0).T
    both_gain = jnp.stack([jnp.ones_like(own_gain).reshape(near, piece), own_gain.reshape(near, piece)], axis=1)
    own = place(
        both_placing, jnp.concatenate([acts[0], grad_out[0]], axis=0), both_gain.reshape(2 * count, 1)
    )
    own, far_acts_0, acts_1, meta = tie(own, far_acts_0, acts[0, first:], meta)

    far_acts_1 = far(acts_1)
    own = near_exchange(own).reshape(near, 2, piece, width)
    own_in = own[:, 0].reshape(count, width)
    far_meta = far(meta)
    other = [swap(weight) for weight in weights]
    far_placing, far_back, far_weighting, far_gain = route(far_meta, half, chips, capacity)
    far_in = place_far(far_placing, [far_acts_0, far_acts_1])
    far_in, own, own_in, far_placing, far_gain, grads, *weights = tie(
        far_in, own, own_in, far_placing, far_gain, grad_out[0], *weights, *other
    )

    far_grads = far(grads)
    far_in = near_exchange(far_in)
    own_b = swap(own)
    mirror_own = mirror(own_in)
    own_pre_gate, own_pre_up, own_hidden, own_out = forward(count, (own, 0), weights)
    own_units, own_input = backward(count, (own, 1), own_pre_gate, own_pre_up, weights)
    far_grads, own_out, own_input, far_weighting, own_weighting, far_mix, own_mix = tie(
        far_grads,
        own_out,
        own_input,
        far_weighting,
        own_weighting,
        of_set(far_back, 0),
        of_set(own_back, 1),
    )
    far_grad = place_far(far_placing, [far_grads], far_gain)
    far_grad, far_in, own_b, mirror_own, own_out, own_input, own_hidden, own_units = tie(
        far_grad, far_in, own_b, mirror_own, own_out, own_input, own_hidden, own_units
    )

    far_grad = near_exchange(far_grad)
    far_in_b = swap(far_in)
    mirror_own_b = swap(mirror_own)
    own_hidden_b = swap(own_hidden[2:])
    own_units_b = swap(own_units[2:])
    far_pre_gate, far_pre_up, far_hidden, far_out = forward(count, far_in, weights)
    far_grad, far_out, far_in_b, mirror_own_b, own_hidden_b, own_units_b, far_hidden = tie(
        far_grad, far_out, far_in_b, mirror_own_b, own_hidden_b, own_units_b, far_hidden
    )

    far_out = near_exchange(far_out)
    far_grad_b = swap(far_grad)
    far_hidden_b = swap(far_hidden[2:])
    far_units, inputs = backward(
        count, far_grad, far_pre_gate, far_pre_up, weights, own_input, near
    )
    far_out, far_units, inputs, far_grad_b, far_hidden_b, mirror_far, own_units, own_units_b = tie(
        far_out, far_units, inputs, far_grad_b, far_hidden_b, far_in, own_units, own_units_b
    )

    got_out = far(combine(far_weighting, far_out).astype(BF16))
    back = near_exchange(inputs.reshape(2 * count, width))
    mirror_far = mirror(mirror_far)
    far_units_b = swap(far_units[2:])
    all_units = (own_units, own_units_b, far_units, far_units_b)
    mirror_units = [
        mirror(jnp.stack([for_mirror(units) for units in all_units[:2]])),
        *[mirror(for_mirror(units)) for units in all_units[2:]],
    ]
    hiddens = (own_hidden, own_hidden_b, far_hidden, far_hidden_b)
    rows_grad = ((own, 1), (own_b.reshape(own.shape), 1), far_grad, far_grad_b)
    send_down = down_grad(count, 1 - kept, hiddens, rows_grad)
    keep_down = down_grad(count, kept, hiddens, rows_grad)
    got_out, back, mirror_far, send_down, keep_down, own_out, *mirror_units = tie(
        got_out, back, mirror_far, send_down, keep_down, own_out, *mirror_units
    )

    got_input = far(combine(far_mix, back).astype(BF16))
    own_out = near_exchange(own_out)
    got_down = mirror(send_down)
    mirror_far_b = swap(mirror_far)
    grad_gate, grad_up = gate_up_grad(
        count,
        kept,
        all_units,
        ((own, 0), (own_b.reshape(own.shape), 0), far_in, far_in_b),
        [mirror_units[0][0], mirror_units[0][1], *mirror_units[1:]],
        (mirror_own, mirror_own_b, mirror_far, mirror_far_b),
    )
    out_acts = (combine(own_weighting, own_out) + got_out.astype(F32)).astype(BF16)
    grad_down = (keep_down.astype(F32) + got_down.astype(F32)).astype(BF16)
    own_part = combine(own_mix, back)
    got_input, grad_down, grad_gate, grad_up, out_acts, own_part = tie(
        got_input, grad_down, grad_gate, grad_up, out_acts, own_part
    )
    grad_acts = (own_part + got_input.astype(F32)).astype(BF16)
    return out_acts[None], grad_acts[None], grad_gate[None], grad_up[None], grad_down[None]


def solution(mesh):
    tokens = P("pipe", "expert", None)
    columns = P("pipe", None, "expert")
    return jax.shard_map(
        on_device,
        mesh=mesh,
        in_specs=(tokens, tokens, tokens, tokens, columns, columns, tokens),
        out_specs=(tokens, tokens, columns, columns, tokens),
        check_vma=False,
    )
```
